128 devices in a mesh: seq: 2 (over y_lo), ctx: 32 (over y_hi, z, x), wsh: 2 (over core).
Axes of the slice: x: 4, y: 4 (y_hi: 2, y_lo: 2; y = y_hi * 2 + y_lo), z: 4, core: 2. Of those that a mesh axis runs over, the one named last changes fastest.
Arguments:
- tokens: bfloat16 [4, 4096, 768], P(('seq', 'wsh'), 'ctx'), may hold values from -6 to 6
- lengths: int32 [4], P(('seq', 'wsh')), may hold values from 512 to 4096, as said below
- w_query: bfloat16 [768, 768], P('wsh'), may hold values from -0.21875 to 0.21875
- b_query: bfloat16 [768], P('wsh'), may hold values from -3 to 3
- w_key: bfloat16 [768, 768], P('wsh'), may hold values from -0.21875 to 0.21875
- w_value: bfloat16 [768, 768], P('wsh'), may hold values from -0.21875 to 0.21875
- b_value: bfloat16 [768], P('wsh'), may hold values from -3 to 3
- w_out: bfloat16 [768, 768], P('wsh'), may hold values from -6 to 6
- b_out: bfloat16 [768], P('wsh'), may hold values from -3 to 3
- gain_one: bfloat16 [768], P('wsh'), may hold values from 0.5 to 1.5
- shift_one: bfloat16 [768], P('wsh'), may hold values from -3 to 3
- w_up: bfloat16 [768, 3072], P('wsh'), may hold values from -0.21875 to 0.21875
- b_up: bfloat16 [3072], P('wsh'), may hold values from -3 to 3
- w_down: bfloat16 [3072, 768], P('wsh'), may hold values from -0.109375 to 0.109375
- b_down: bfloat16 [768], P('wsh'), may hold values from -3 to 3
- gain_two: bfloat16 [768], P('wsh'), may hold values from 0.5 to 1.5
- shift_two: bfloat16 [768], P('wsh'), may hold values from -3 to 3
- cotangent: bfloat16 [4, 4096, 768], P(('seq', 'wsh'), 'ctx'), may hold values from -6 to 6
Outputs:
- output: bfloat16 [4, 4096, 768], P(('seq', 'wsh'), 'ctx')
- grad_tokens: float32 [4, 4096, 768], P(('seq', 'wsh'), 'ctx')
- grad_w_query: float32 [768, 768], P('wsh')
- grad_b_query: float32 [768], P('wsh')
- grad_w_key: float32 [768, 768], P('wsh')
- grad_w_value: float32 [768, 768], P('wsh')
- grad_b_value: float32 [768], P('wsh')
- grad_w_out: float32 [768, 768], P('wsh')
- grad_b_out: float32 [768], P('wsh')
- grad_gain_one: float32 [768], P('wsh')
- grad_shift_one: float32 [768], P('wsh')
- grad_w_up: float32 [768, 3072], P('wsh')
- grad_b_up: float32 [3072], P('wsh')
- grad_w_down: float32 [3072, 768], P('wsh')
- grad_b_down: float32 [768], P('wsh')
- grad_gain_two: float32 [768], P('wsh')
- grad_shift_two: float32 [768], P('wsh')
The draws below stay inside these ranges and needn't reach their ends.
Inputs may be any that keep to these rules, and one draw needn't show every extreme that they name: Sequence s has lengths[s] valid tokens at its start, the rest is padding; in every draw some sequence is full, with 4096 valid tokens.
All inputs are finite; a program needn't handle non-finite values.
Results may differ from the reference program's by a relative error of at most 0.024.
Values may be sent and summed in bfloat16 or wider, within the bound.
A program may use at most 192 MiB of HBM per device.

```python
import jax
import jax.numpy as jnp
from jax import lax

D = 768
H = 12
HD = 64
FF = 3072
SEQLEN = 4096
SEQS = 4


def draw_lengths(key, part):
    first_key = jax.random.fold_in(key, 11)
    second_key = jax.random.fold_in(key, 23)
    drawn = jax.random.randint(first_key, (SEQS,), SEQLEN // 8, SEQLEN + 1)
    chosen = jax.random.randint(second_key, (), 0, SEQS)
    return jnp.where(jnp.arange(SEQS) == chosen, SEQLEN, drawn).astype(jnp.int32)


def shard_levels(stream_key, dims, pieces, low, largest):
    def one(axis_at, shards_of):
        steps = jax.random.uniform(jax.random.fold_in(jax.random.fold_in(stream_key, 6), axis_at), (shards_of,), jnp.float32, low / len(pieces), largest / len(pieces))
        return jnp.repeat(jnp.exp(steps), dims[axis_at] // shards_of).reshape((-1,) + (1,) * (len(dims) - axis_at - 1))

    level = one(*pieces[0])
    for cut in pieces[1:]:
        level = level * one(*cut)
    return level


def gaussian(stream_key, dims, scale, reach, shards=(), dtype=jnp.bfloat16):
    factor_of = shard_levels(stream_key, dims, shards, -0.22, 0.18) if shards else 1.0
    values = jax.random.normal(stream_key, dims, jnp.float32) * scale * factor_of
    return jnp.minimum(jnp.maximum(values, -reach), reach).astype(dtype)


def setup_inputs(seed: int = 0) -> dict:
    key_list = jax.random.split(jax.random.key(seed), 19)
    return {
        "tokens": gaussian(key_list[0], (SEQS, SEQLEN, D), 1.0, 6.0, ((0, 4), (1, 32))),
        "lengths": draw_lengths(jax.random.fold_in(key_list[18], 71), 0),
        "w_query": gaussian(key_list[2], (D, D), D ** -0.5, 0.21875, ((0, 2),)),
        "b_query": gaussian(key_list[3], (D,), 0.5, 3.0, ((0, 2),)),
        "w_key": gaussian(key_list[4], (D, D), D ** -0.5, 0.21875, ((0, 2),)),
        "w_value": gaussian(key_list[5], (D, D), D ** -0.5, 0.21875, ((0, 2),)),
        "b_value": gaussian(key_list[6], (D,), 0.5, 3.0, ((0, 2),)),
        "w_out": gaussian(key_list[7], (D, D), ((SEQLEN / D) ** 0.5 / 4), 6.0, ((0, 2),)),
        "b_out": gaussian(key_list[8], (D,), 0.5, 3.0, ((0, 2),)),
        "gain_one": jnp.clip(1.0 + 0.1 * jax.random.normal(key_list[9], (D,), jnp.float32), 0.5, 1.5).astype(jnp.bfloat16),
        "shift_one": gaussian(key_list[10], (D,), 0.5, 3.0, ((0, 2),)),
        "w_up": gaussian(key_list[11], (D, FF), D ** -0.5, 0.21875, ((0, 2),)),
        "b_up": gaussian(key_list[12], (FF,), 0.5, 3.0, ((0, 2),)),
        "w_down": gaussian(key_list[13], (FF, D), FF ** -0.5, 0.109375, ((0, 2),)),
        "b_down": gaussian(key_list[14], (D,), 0.5, 3.0, ((0, 2),)),
        "gain_two": jnp.clip(1.0 + 0.1 * jax.random.normal(key_list[15], (D,), jnp.float32), 0.5, 1.5).astype(jnp.bfloat16),
        "shift_two": gaussian(key_list[16], (D,), 0.5, 3.0, ((0, 2),)),
        "cotangent": gaussian(key_list[17], (SEQS, SEQLEN, D), 1.0, 6.0, ((0, 4), (1, 32))),
    }


@jax.custom_vjp
def low(v):
    return lax.optimization_barrier(v.astype(jnp.bfloat16)).astype(jnp.float32)

@jax.custom_vjp
def low_back(v):
    return v

def low_keep(v):
    return (low(v), None)

def low_pass(kept, grad):
    return (grad,)

def back_keep(v):
    return (v, None)

def back_low(kept, grad):
    return (low(grad),)
low.defvjp(low_keep, low_pass)
low_back.defvjp(back_keep, back_low)

def matmul(left, right):
    return jnp.dot(left, right, precision=lax.Precision.HIGHEST)

def layer_norm(resid, gain, shift):
    centre = resid - lax.optimization_barrier(jnp.mean(resid, axis=-1, keepdims=True))
    spread = lax.optimization_barrier(jnp.mean(centre * centre, axis=-1, keepdims=True))
    return centre * lax.rsqrt(spread + 1e-12) * gain + shift

def attend(query, keys, values, length):
    seqlen = query.shape[0]
    block = 512 if seqlen % 512 == 0 else seqlen
    valid = (jnp.arange(seqlen) < length)[None, None, :]

    def one_block(query_block):
        scores = jnp.einsum('qhd,khd->hqk', query_block, keys, precision=lax.Precision.HIGHEST) * 0.125
        scores = low_back(scores)
        masked = jnp.where(valid, scores, -1e+30)
        top = lax.optimization_barrier(jnp.max(masked, axis=-1, keepdims=True))
        expo = jnp.where(valid, jnp.exp(masked - top), 0.0)
        weights = expo / lax.optimization_barrier(jnp.sum(expo, axis=-1, keepdims=True))
        return jnp.einsum('hqk,khd->qhd', low(weights), values, precision=lax.Precision.HIGHEST)
    blocks = query.reshape(seqlen // block, block, H, HD)
    joined = lax.map(jax.checkpoint(one_block), blocks)
    return joined.reshape(seqlen, H * HD)

def forward(inputs, params, lengths):
    w_query, b_query, w_key, w_value, b_value, w_out, b_out, gain_one, shift_one, w_up, b_up, w_down, b_down, gain_two, shift_two = params
    flat = inputs.reshape(SEQS * SEQLEN, D)
    query = low_back(low(matmul(flat, w_query) + b_query)).reshape(SEQS, SEQLEN, H, HD)
    keys = low_back(low(matmul(flat, w_key))).reshape(SEQS, SEQLEN, H, HD)
    values = low_back(low(matmul(flat, w_value) + b_value)).reshape(SEQS, SEQLEN, H, HD)

    def per_sequence(items):
        return attend(items[0], items[1], items[2], items[3])
    attn = lax.map(per_sequence, (query, keys, values, lengths))
    mixed = low_back(low(attn.reshape(SEQS * SEQLEN, D)))
    branch = low_back(matmul(mixed, w_out)) + b_out
    first = layer_norm(flat + branch, gain_one, shift_one)
    pre = low_back(matmul(low(first), w_up) + b_up)
    act = low(jax.nn.gelu(pre, approximate=False))
    down = low_back(matmul(act, w_down)) + b_down
    result = layer_norm(first + down, gain_two, shift_two)
    return result.reshape(SEQS, SEQLEN, D)

def reference(tokens, lengths, w_query, b_query, w_key, w_value, b_value, w_out, b_out, gain_one, shift_one, w_up, b_up, w_down, b_down, gain_two, shift_two, cotangent):
    params = (w_query, b_query, w_key, w_value, b_value, w_out, b_out, gain_one, shift_one, w_up, b_up, w_down, b_down, gain_two, shift_two)
    params = tuple((item.astype(jnp.float32) for item in params))
    inputs = tokens.astype(jnp.float32)

    def wrapped(inputs, params):
        return forward(inputs, params, lengths)
    result, pullback = jax.vjp(wrapped, inputs, params)
    grad_inputs, grads = pullback(cotangent.astype(jnp.float32))
    return (result.astype(jnp.bfloat16), grad_inputs, grads[0], grads[1], grads[2], grads[3], grads[4], grads[5], grads[6], grads[7], grads[8], grads[9], grads[10], grads[11], grads[12], grads[13], grads[14])
```

```python
import functools
import math

import jax
import jax.numpy as jnp
from jax import lax
from jax.experimental import pallas as pl
from jax.experimental.pallas import tpu as pltpu
from jax.sharding import Mesh
from jax.sharding import PartitionSpec as P

H = 12
HD = 64
D = 768
CTX = ("ctx_0", "ctx_1", "ctx_2")
f32 = jnp.float32
bf16 = jnp.bfloat16
MESH = pl.DeviceIdType.MESH
ANY = pl.ANY
MIB = 1024 * 1024


def place(axis):
    if axis == "x":
        return lax.axis_index("ctx_2")
    if axis == "z":
        return lax.axis_index("ctx_1")
    return lax.axis_index("ctx_0") * 2 + lax.axis_index("seq")


def away(axis, step):
    at = lax.rem(place(axis) + step + 4, 4)
    if axis == "x":
        return {"ctx_2": at}
    if axis == "z":
        return {"ctx_1": at}
    return {"ctx_0": at // 2, "seq": lax.rem(at, 2)}


def sibling():
    return {"wsh": 1 - lax.axis_index("wsh")}


def far():
    return {"ctx_0": 1 - lax.axis_index("ctx_0")}


def meet(devices):
    barrier = pltpu.get_barrier_semaphore()
    for d in devices:
        pl.semaphore_signal(barrier, inc=1, device_id=d, device_id_type=MESH)
    pl.semaphore_wait(barrier, len(devices))


class Sends:
    def __init__(self, send, recv):
        self.send, self.recv, self.used, self.all = send, recv, 0, []

    def start(self, src, dst, device):
        k = self.used
        self.used += 1
        copy = pltpu.make_async_remote_copy(
            src_ref=src,
            dst_ref=dst,
            send_sem=self.send.at[k],
            recv_sem=self.recv.at[k],
            device_id=device,
            device_id_type=MESH,
        )
        copy.start()
        self.all.append(copy)
        return copy

    def finish(self):
        for copy in self.all:
            copy.wait_send()


def gather_kernel(rows, n_pair, *refs):
    n = len(rows)
    ins, pair_ins = refs[:n], refs[n : n + n_pair]
    outs, pair_outs = refs[n + n_pair : 2 * n + n_pair], refs[2 * n + n_pair : 2 * (n + n_pair)]
    send, recv, local = refs[2 * (n + n_pair) :]
    sends = Sends(send, recv)
    y, z, x = (lax.axis_index(a) for a in CTX)
    core = lax.axis_index("wsh")
    devices = [away("x", 1), away("x", -1), away("z", 1), away("z", -1), far()]
    if n_pair:
        devices.append(sibling())
    meet(devices)
    locals_ = []

    def keep(src, dst):
        copy = pltpu.make_async_copy(src, dst, local.at[len(locals_)])
        copy.start()
        locals_.append(copy)
        return copy

    own = [keep(i, o.at[y, z, x]) for i, o in zip(ins, outs)]
    crossing = [sends.start(i, o.at[y, z, x], far()) for i, o in zip(ins, outs)]

    def first(layer, mine):
        flights = []
        for i, o, r in zip(ins, outs, rows):
            h = r // 2
            for axis, lo in (("x", 0), ("z", h)):
                src = i.at[pl.ds(lo, h)] if mine else o.at[layer, z, x, pl.ds(lo, h)]
                dst = o.at[layer, z, x, pl.ds(lo, h)]
                flights.append(
                    [sends.start(src, dst, away(axis, 1)), sends.start(src, dst, away(axis, -1))]
                )
        return flights

    def first_on(layer, flights):
        later, at = [], 0
        for o, r in zip(outs, rows):
            q = r // 4
            for axis, lo in (("x", 0), ("z", 2 * q)):
                right, left = flights[at]
                at += 1
                pos = place(axis)
                before, after = lax.rem(pos + 3, 4), lax.rem(pos + 1, 4)
                right.wait_recv()
                if axis == "x":
                    a = o.at[layer, z, before, pl.ds(lo, q)]
                    b = o.at[layer, z, after, pl.ds(lo + q, q)]
                else:
                    a = o.at[layer, before, x, pl.ds(lo, q)]
                    b = o.at[layer, after, x, pl.ds(lo + q, q)]
                up = sends.start(a, a, away(axis, 1))
                left.wait_recv()
                later.append([up, sends.start(b, b, away(axis, -1))])
        return later

    def second(layer, flights):
        later, at = [], 0
        for o, r in zip(outs, rows):
            h = r // 2
            for axis, lo in (("z", 0), ("x", h)):
                for copy in flights[at]:
                    copy.wait_recv()
                at += 1
                if axis == "z":
                    a = o.at[layer, z, :, pl.ds(lo, h)]
                else:
                    a = o.at[layer, :, x, pl.ds(lo, h)]
                later.append([sends.start(a, a, away(axis, 1)), sends.start(a, a, away(axis, -1))])
        return later

    def second_on(layer, flights):
        later, at = [], 0
        for o, r in zip(outs, rows):
            h = r // 2
            for axis, lo in (("z", 0), ("x", h)):
                right, left = flights[at]
                at += 1
                pos = place(axis)
                before, after = lax.rem(pos + 3, 4), lax.rem(pos + 1, 4)
                right.wait_recv()
                if axis == "z":
                    a = o.at[layer, before, pl.ds(0, 2), pl.ds(lo, h)]
                    b = o.at[layer, after, pl.ds(2, 2), pl.ds(lo, h)]
                else:
                    a = o.at[layer, pl.ds(0, 2), before, pl.ds(lo, h)]
                    b = o.at[layer, pl.ds(2, 2), after, pl.ds(lo, h)]
                up = sends.start(a, a, away(axis, 1))
                left.wait_recv()
                later.append([up, sends.start(b, b, away(axis, -1))])
        return later

    mine = first(y, True)
    pairs = []
    for i, o in zip(pair_ins, pair_outs):
        pairs.append(sends.start(i, o.at[core], sibling()))
        keep(i, o.at[core])
    other = 1 - y
    mine = first_on(y, mine)
    for copy in crossing:
        copy.wait_recv()
    theirs = first(other, False)
    for copy in own:
        copy.wait()
    mine = second(y, mine)
    theirs = first_on(other, theirs)
    mine = second_on(y, mine)
    theirs = second(other, theirs)
    theirs = second_on(other, theirs)
    for flights in (mine, theirs):
        for pair in flights:
            for copy in pair:
                copy.wait_recv()
    for copy in pairs:
        copy.wait_recv()
    for copy in locals_[len(own) :]:
        copy.wait()
    sends.finish()


def gather(arrays, pairs, cid):
    n, m = len(arrays), len(pairs)
    outs = pl.pallas_call(
        functools.partial(gather_kernel, tuple(a.shape[0] for a in arrays), m),
        out_shape=[jax.ShapeDtypeStruct((2, 4, 4, *a.shape), a.dtype) for a in arrays]
        + [jax.ShapeDtypeStruct((2, *a.shape), a.dtype) for a in pairs],
        in_specs=[pl.BlockSpec(memory_space=ANY)] * (n + m),
        out_specs=[pl.BlockSpec(memory_space=ANY)] * (n + m),
        scratch_shapes=[
            pltpu.SemaphoreType.DMA((33 * n + m,)),
            pltpu.SemaphoreType.DMA((33 * n + m,)),
            pltpu.SemaphoreType.DMA((n + m,)),
        ],
        compiler_params=pltpu.CompilerParams(collective_id=cid, has_side_effects=True),
    )(*arrays, *pairs)
    return outs[:n], outs[n:]


ORDERS = (("x", "y", "z"), ("y", "z", "x"), ("z", "x", "y"))
AXES = ("x", "y", "z")
SPLIT = ((192, 192), (48, 48), (32, 16))
CHUNK = ((384, 768), (96, 768), (48, 384))


def reduce_kernel(
    g0, g1, g2, small, out, small_out,
    acc, pair, t0, t1, t2, u0, u1, u2, cur, slots, send, recv, local,
):
    core = lax.axis_index("wsh")
    twin = 1 - core
    sends = Sends(send, recv)
    tt, uu = (t0, t1, t2), (u0, u1, u2)
    pos = {a: place(a) for a in AXES}
    meet([sibling()] + [away(a, k) for a in AXES for k in (1, 2, 3)])

    def share(s, m, half):
        if s == 0:
            return g0.at[m, pl.ds(pl.multiple_of(half * 384, 384), 384)]
        if s == 1:
            return g1.at[pl.ds(pl.multiple_of(half * 384, 384), 384), pl.ds(m * 768, 768)]
        return g2.at[pl.ds(pl.multiple_of(half * 1536 + m * 384, 384), 384)]

    small_pair = sends.start(small.at[twin], slots.at[3, 0], sibling())
    flights, kept = [], []
    for m in range(4):
        for s in range(3):
            flights.append((s, m, sends.start(share(s, m, twin), pair.at[s, m], sibling())))
            copy = pltpu.make_async_copy(share(s, m, core), acc.at[s, m], local.at[s * 4 + m])
            copy.start()
            kept.append(copy)
    mine = pltpu.make_async_copy(small.at[core], cur, local.at[12])
    mine.start()
    mine.wait()
    small_pair.wait_recv()
    cur[...] = cur[...] + slots[3, 0]

    def add(dst, dst_at, src, src_at, shape):
        rows, cols = shape

        @pl.loop(0, rows // 16)
        def _(k):
            a = dst_at(pl.multiple_of(k * 16, 16))
            b = src_at(pl.multiple_of(k * 16, 16))
            dst[a] = (dst[a].astype(f32) + src[b].astype(f32)).astype(bf16)

    for (s, m, flight), copy in zip(flights, kept):
        copy.wait()
        flight.wait_recv()
        add(
            acc, lambda r, s=s, m=m: (s, m, pl.ds(r, 16)),
            pair, lambda r, s=s, m=m: (s, m, pl.ds(r, 16)), (384, 768),
        )

    def region(ph, s, c, r, n):
        a, b, _ = (pos[k] for k in ORDERS[s])
        if ph == 0:
            return (s, c, pl.ds(r, n))
        if ph == 1:
            return (s, a, pl.ds(pl.multiple_of(96 * c + r, 16), n))
        return (
            s, a, pl.ds(pl.multiple_of(96 * b + 48 * (c // 2) + r, 16), n),
            pl.ds(pl.multiple_of(lax.rem(c, 2) * 384, 384), 384),
        )

    small_axis = {}
    for ph in range(3):
        axis = AXES[ph]
        slots[ph, pos[axis]] = cur[...]
        small_axis = [
            sends.start(cur, slots.at[ph, pos[axis]], away(axis, k)) for k in (1, 2, 3)
        ]
        rows, cols = CHUNK[ph]
        near, rest = SPLIT[ph]
        steps = []
        for s in range(3):
            axis_s = ORDERS[s][ph]
            p = pos[axis_s]
            c = lax.rem(p + 2, 4)
            steps.append((
                sends.start(
                    acc.at[region(ph, s, c, 0, near)], tt[ph].at[s, 0, pl.ds(0, near)], away(axis_s, 1)
                ),
                sends.start(
                    acc.at[region(ph, s, c, near, rest)], tt[ph].at[s, 1, pl.ds(0, rest)], away(axis_s, -1)
                ),
            ))
        nexts = []
        for s in range(3):
            axis_s = ORDERS[s][ph]
            p = pos[axis_s]
            up, down = lax.rem(p + 1, 4), lax.rem(p + 3, 4)
            steps[s][0].wait_recv()
            add(
                acc, lambda r, s=s, up=up: region(ph, s, up, r, 16),
                tt[ph], lambda r, s=s: (s, 0, pl.ds(r, 16)), (near, cols),
            )
            a = sends.start(acc.at[region(ph, s, up, 0, rows)], uu[ph].at[s, 0], away(axis_s, 1))
            steps[s][1].wait_recv()
            add(
                acc, lambda r, s=s, down=down: region(ph, s, down, near + r, 16),
                tt[ph], lambda r, s=s: (s, 1, pl.ds(r, 16)), (rest, cols),
            )
            b = sends.start(acc.at[region(ph, s, down, 0, rows)], uu[ph].at[s, 1], away(axis_s, -1))
            nexts.append((a, b))
        for s in range(3):
            p = pos[ORDERS[s][ph]]
            for k in range(2):
                nexts[s][k].wait_recv()
                add(
                    acc, lambda r, s=s, p=p: region(ph, s, p, r, 16),
                    uu[ph], lambda r, s=s, k=k: (s, k, pl.ds(r, 16)), (rows, cols),
                )
        for copy in small_axis:
            copy.wait()
        sends.all = [c for c in sends.all if all(c is not d for d in small_axis)]
        cur[...] = (slots[ph, 0] + slots[ph, 1]) + (slots[ph, 2] + slots[ph, 3])

    small_out[...] = cur[...]

    for ph in (2, 1, 0):
        rows, cols = CHUNK[ph]
        near, rest = SPLIT[ph]
        steps = []
        for s in range(3):
            axis_s = ORDERS[s][ph]
            p = pos[axis_s]
            here = region(ph, s, p, 0, rows)
            if ph == 2:
                kept_copy = pltpu.make_async_copy(acc.at[here], out.at[here], local.at[s])
                kept_copy.start()
                src = acc.at[here]
            else:
                kept_copy = None
                src = out.at[here]
            steps.append((
                sends.start(src, out.at[here], away(axis_s, 1)),
                sends.start(src, out.at[here], away(axis_s, -1)),
                kept_copy,
            ))
        nexts = []
        for s in range(3):
            axis_s = ORDERS[s][ph]
            p = pos[axis_s]
            up, down = lax.rem(p + 1, 4), lax.rem(p + 3, 4)
            steps[s][0].wait_recv()
            part = out.at[region(ph, s, down, 0, near)]
            a = sends.start(part, part, away(axis_s, 1))
            steps[s][1].wait_recv()
            part = out.at[region(ph, s, up, near, rest)]
            b = sends.start(part, part, away(axis_s, -1))
            nexts.append((a, b))
        for s in range(3):
            if steps[s][2] is not None:
                steps[s][2].wait()
            for copy in nexts[s]:
                copy.wait_recv()
    sends.finish()


def reduce_params(g0, g1, g2, small, cid):
    scratch = [pltpu.VMEM((3, 4, 384, 768), bf16), pltpu.VMEM((3, 4, 384, 768), bf16)]
    scratch += [pltpu.VMEM((3, 2, SPLIT[k][0], CHUNK[k][1]), bf16) for k in range(3)]
    scratch += [pltpu.VMEM((3, 2, *CHUNK[k]), bf16) for k in range(3)]
    scratch += [pltpu.VMEM((40, 128), f32), pltpu.VMEM((4, 4, 40, 128), f32)]
    count = 1 + 12 + 9 + 3 * 24
    scratch += [
        pltpu.SemaphoreType.DMA((count,)),
        pltpu.SemaphoreType.DMA((count,)),
        pltpu.SemaphoreType.DMA((13,)),
    ]
    return pl.pallas_call(
        reduce_kernel,
        out_shape=[
            jax.ShapeDtypeStruct((3, 4, 384, 768), bf16),
            jax.ShapeDtypeStruct((40, 128), f32),
        ],
        in_specs=[pl.BlockSpec(memory_space=ANY)] * 4,
        out_specs=[pl.BlockSpec(memory_space=ANY), pl.BlockSpec(memory_space=pltpu.VMEM)],
        scratch_shapes=scratch,
        compiler_params=pltpu.CompilerParams(
            collective_id=cid, has_side_effects=True, vmem_limit_bytes=40 * MIB
        ),
    )(g0, g1, g2, small)


def nt(a, b):
    return lax.dot_general(a, b, (((1,), (1,)), ((), ())), preferred_element_type=f32)


def nn(a, b):
    return jnp.dot(a, b, preferred_element_type=f32)


def stacked(block):
    lane = lax.broadcasted_iota(jnp.int32, block.shape, 1) // HD
    zero = jnp.zeros_like(block)
    return jnp.concatenate([jnp.where(lane == i, block, zero) for i in range(4)], axis=0)


def unstacked(tall):
    n = tall.shape[0] // 4
    lane = lax.broadcasted_iota(jnp.int32, (n, tall.shape[1]), 1) // HD
    total = jnp.where(lane == 0, tall[:n], 0.0)
    for i in range(1, 4):
        total = total + jnp.where(lane == i, tall[i * n : (i + 1) * n], 0.0)
    return total


def as_rows(column):
    wide = jnp.broadcast_to(column, (column.shape[0], 128))
    return jnp.concatenate(
        [wide[i * 128 : (i + 1) * 128].T[:1] for i in range(4)] + [jnp.zeros((4, 128), f32)], axis=0
    )


TILE = 1024


def forward_kernel(q_ref, k_ref, v_ref, bias_ref, attn_ref, lse_ref, rows_ref, score):
    q = stacked(q_ref[...] * jnp.asarray(0.125, bf16))
    top = None
    for t in range(4096 // TILE):
        at = pl.ds(t * TILE, TILE)
        s = nt(q, k_ref[at, :]) + bias_ref[:, at]
        score[:, at] = s
        m = jnp.max(s, axis=-1, keepdims=True)
        top = m if top is None else jnp.maximum(top, m)
    total, out = 0.0, 0.0
    for t in range(4096 // TILE):
        at = pl.ds(t * TILE, TILE)
        p = jnp.exp(score[:, at] - top)
        total = total + jnp.sum(p, axis=-1, keepdims=True)
        out = out + nn(p.astype(bf16), v_ref[at, :])
    attn_ref[...] = unstacked(out * (1.0 / total))
    lse = top + jnp.log(total)
    lse_ref[0] = jnp.broadcast_to(lse, (512, 128))
    rows_ref[0] = as_rows(lse)


def attend(q, k, v, bias):
    wide = pl.BlockSpec((4096, 256), lambda g: (0, g))
    own = pl.BlockSpec((128, 256), lambda g: (0, g))
    return pl.pallas_call(
        forward_kernel,
        grid=(3,),
        out_shape=[
            jax.ShapeDtypeStruct((128, D), f32),
            jax.ShapeDtypeStruct((3, 512, 128), f32),
            jax.ShapeDtypeStruct((3, 8, 128), f32),
        ],
        in_specs=[own, wide, wide, pl.BlockSpec((1, 4096), lambda g: (0, 0))],
        out_specs=[
            own,
            pl.BlockSpec((1, 512, 128), lambda g: (g, 0, 0)),
            pl.BlockSpec((1, 8, 128), lambda g: (g, 0, 0)),
        ],
        scratch_shapes=[pltpu.VMEM((512, 4096), f32)],
        compiler_params=pltpu.CompilerParams(vmem_limit_bytes=56 * MIB),
    )(q, k, v, bias)


def query_kernel(q_ref, k_ref, v_ref, bias_ref, g_ref, attn_ref, lse_ref, dq_ref, rows_ref):
    q = stacked(q_ref[...] * jnp.asarray(0.125, bf16))
    g = stacked(g_ref[...])
    attn = attn_ref[...]
    tall = jnp.concatenate([attn] * 4, axis=0)
    delta = jnp.sum(g.astype(f32) * tall, axis=-1, keepdims=True)
    rows_ref[0] = as_rows(delta)
    lse = lse_ref[0][:, :1]
    dq = 0.0
    for t in range(4096 // TILE):
        at = pl.ds(t * TILE, TILE)
        p = jnp.exp(nt(q, k_ref[at, :]) + bias_ref[:, at] - lse)
        dp = nt(g, v_ref[at, :])
        ds = (p * (dp - delta)).astype(bf16)
        dq = dq + nn(ds, k_ref[at, :])
    dq_ref[...] = (unstacked(dq) * 0.125).astype(bf16)


def query_grads(q, k, v, bias, g, attn, lse):
    wide = pl.BlockSpec((4096, 256), lambda g: (0, g))
    own = pl.BlockSpec((128, 256), lambda g: (0, g))
    return pl.pallas_call(
        query_kernel,
        grid=(3,),
        out_shape=[jax.ShapeDtypeStruct((128, D), bf16), jax.ShapeDtypeStruct((3, 8, 128), f32)],
        in_specs=[
            own, wide, wide, pl.BlockSpec((1, 4096), lambda g: (0, 0)), own, own,
            pl.BlockSpec((1, 512, 128), lambda g: (g, 0, 0)),
        ],
        out_specs=[own, pl.BlockSpec((1, 8, 128), lambda g: (g, 0, 0))],
        compiler_params=pltpu.CompilerParams(vmem_limit_bytes=56 * MIB),
    )(q, k, v, bias, g, attn, lse)


def key_kernel(k_ref, v_ref, bias_ref, q_ref, g_ref, lse_ref, delta_ref, dk_ref, dv_ref):
    k = stacked(k_ref[...] * jnp.asarray(0.125, bf16))
    v = stacked(v_ref[...])
    bias = jnp.concatenate([bias_ref[:, :1]] * 4, axis=0)
    dk, dv = 0.0, 0.0
    for t in range(4096 // TILE):
        at = pl.ds(t * TILE, TILE)
        q, g = q_ref[at, :], g_ref[at, :]
        lse = jnp.concatenate(
            [jnp.broadcast_to(lse_ref[0, i : i + 1, at], (128, TILE)) for i in range(4)], axis=0
        )
        delta = jnp.concatenate(
            [jnp.broadcast_to(delta_ref[0, i : i + 1, at], (128, TILE)) for i in range(4)], axis=0
        )
        p = jnp.exp(nt(k, q) + bias - lse)
        ds = (p * (nt(v, g) - delta)).astype(bf16)
        dv = dv + nn(p.astype(bf16), g)
        dk = dk + nn(ds, q)
    dk_ref[...] = (unstacked(dk) * 0.125).astype(bf16)
    dv_ref[...] = unstacked(dv).astype(bf16)


def key_grads(k, v, bias, q, g, lse, delta):
    wide = pl.BlockSpec((4096, 256), lambda g: (0, g))
    own = pl.BlockSpec((128, 256), lambda g: (0, g))
    stat = pl.BlockSpec((1, 8, 4096), lambda g: (g, 0, 0))
    return pl.pallas_call(
        key_kernel,
        grid=(3,),
        out_shape=[jax.ShapeDtypeStruct((128, D), bf16)] * 2,
        in_specs=[own, own, pl.BlockSpec((128, 128), lambda g: (0, 0)), wide, wide, stat, stat],
        out_specs=[own, own],
        compiler_params=pltpu.CompilerParams(vmem_limit_bytes=56 * MIB),
    )(k, v, bias, q, g, lse, delta)


def layer_norm(resid, gain, shift):
    centre = resid - jnp.mean(resid, axis=-1, keepdims=True)
    spread = jnp.mean(centre * centre, axis=-1, keepdims=True)
    return centre * lax.rsqrt(spread + 1e-12) * gain + shift


def gelu_exact(value):
    return jax.nn.gelu(value, approximate=False)


def local(
    tokens, lengths, w_query, b_query, w_key, w_value, b_value, w_out, b_out, gain_one, shift_one,
    w_up, b_up, w_down, b_down, gain_two, shift_two, cotangent,
):
    inputs = tokens[0]
    vectors = jnp.stack(
        [b_query, b_value, b_out, gain_one, shift_one, b_down, gain_two, shift_two]
    )
    vectors = jnp.concatenate([vectors, b_up.reshape(4, 384), jnp.zeros((4, 384), bf16)], axis=0)
    (xs,), whole = gather(
        [inputs], [w_query, w_key, w_value, w_out, w_up, w_down, vectors], 0
    )
    wq, wk, wv, wo, wup, wdown = (w.reshape(-1, w.shape[-1]) for w in whole[:6])
    vecs = whole[6].astype(f32)
    bq, bv, bo, gone, sone, bdown, gtwo, stwo = (
        vecs[:, i].reshape(768) for i in range(8)
    )
    bup = vecs[:, 8:12].reshape(3072)
    xs = xs.reshape(4096, D)
    seq_len = lengths[0]
    block = (lax.axis_index("ctx_0") * 4 + lax.axis_index("ctx_1")) * 4 + lax.axis_index("ctx_2")
    all_q = (jnp.dot(xs, wq, preferred_element_type=f32) + bq).astype(bf16)
    all_k = jnp.dot(xs, wk, preferred_element_type=f32).astype(bf16)
    all_v = (jnp.dot(xs, wv, preferred_element_type=f32) + bv).astype(bf16)
    q = lax.dynamic_slice_in_dim(all_q, block * 128, 128)
    k = lax.dynamic_slice_in_dim(all_k, block * 128, 128)
    v = lax.dynamic_slice_in_dim(all_v, block * 128, 128)
    bias = jnp.where(jnp.arange(4096) < seq_len, 0.0, -1e30).astype(f32)[None]
    own_bias = jnp.where(jnp.arange(128) + block * 128 < seq_len, 0.0, -1e30).astype(f32)
    own_bias = jnp.broadcast_to(own_bias[:, None], (128, 128))
    attn, lse, lse_rows = attend(q, all_k, all_v, bias)
    mixed = attn.astype(bf16)
    resid_one = inputs.astype(f32) + jnp.dot(mixed, wo, preferred_element_type=f32) + bo
    first, pull_one = jax.vjp(layer_norm, resid_one, gone, sone)
    first_low = first.astype(bf16)
    pre = jnp.dot(first_low, wup, preferred_element_type=f32) + bup
    act, pull_gelu = jax.vjp(gelu_exact, pre)
    act_low = act.astype(bf16)
    resid_two = first + jnp.dot(act_low, wdown, preferred_element_type=f32) + bdown
    result, pull_two = jax.vjp(layer_norm, resid_two, gtwo, stwo)
    grad_resid_two, grad_gtwo, grad_stwo = pull_two(cotangent[0].astype(f32))
    grad_down_low = grad_resid_two.astype(bf16)
    grad_bdown = jnp.sum(grad_resid_two, axis=0)
    grad_wdown = jnp.einsum("tf,td->fd", act_low, grad_down_low, preferred_element_type=f32)
    grad_act = jnp.einsum("td,fd->tf", grad_down_low, wdown, preferred_element_type=f32)
    grad_pre_low = pull_gelu(grad_act)[0].astype(bf16)
    grad_bup = jnp.sum(grad_pre_low.astype(f32), axis=0)
    grad_wup = jnp.einsum("td,tf->df", first_low, grad_pre_low, preferred_element_type=f32)
    grad_first = grad_resid_two + jnp.einsum(
        "tf,df->td", grad_pre_low, wup, preferred_element_type=f32
    )
    grad_resid_one, grad_gone, grad_sone = pull_one(grad_first)
    grad_branch = grad_resid_one.astype(bf16)
    grad_bout = jnp.sum(grad_resid_one, axis=0)
    grad_mixed = jnp.einsum("te,de->td", grad_branch, wo, preferred_element_type=f32).astype(bf16)
    grad_query_low, delta_rows = query_grads(q, all_k, all_v, bias, grad_mixed, attn, lse)
    pad = jnp.zeros((4, 128), f32)
    stats = jnp.concatenate(
        [lse_rows[:, :4].reshape(12, 128), pad, delta_rows[:, :4].reshape(12, 128), pad], axis=0
    )
    (all_g, all_stats), _ = gather([grad_mixed, stats], [], 1)
    all_g = all_g.reshape(4096, D)
    all_stats = all_stats.reshape(32, 32, 128).transpose(1, 0, 2).reshape(32, 4096)
    all_lse = jnp.pad(all_stats[:12].reshape(3, 4, 4096), ((0, 0), (0, 4), (0, 0)))
    all_delta = jnp.pad(all_stats[16:28].reshape(3, 4, 4096), ((0, 0), (0, 4), (0, 0)))
    grad_keys_low, grad_values_low = key_grads(k, v, own_bias, all_q, all_g, all_lse, all_delta)
    lefts = jnp.stack([inputs, inputs, inputs, mixed])
    rights = jnp.stack([grad_query_low, grad_keys_low, grad_values_low, grad_branch])
    grad_four = jnp.einsum("ktd,kte->kde", lefts, rights, preferred_element_type=f32).astype(bf16)
    grad_bq = jnp.sum(grad_query_low.astype(f32), axis=0)
    grad_bv = jnp.sum(grad_values_low.astype(f32), axis=0)
    grad_inputs = grad_resid_one + jnp.einsum(
        "te,de->td", grad_query_low, wq, preferred_element_type=f32
    )
    grad_inputs = grad_inputs + jnp.einsum(
        "te,de->td", grad_keys_low, wk, preferred_element_type=f32
    )
    grad_inputs = grad_inputs + jnp.einsum(
        "te,de->td", grad_values_low, wv, preferred_element_type=f32
    )
    small = jnp.stack(
        [grad_bq, grad_bv, grad_bout, grad_gone, grad_sone, grad_bdown, grad_gtwo, grad_stwo]
    )
    small = small.reshape(8, 2, 384).transpose(1, 0, 2).reshape(2, 3072)
    small = jnp.concatenate(
        [small, grad_bup.reshape(2, 1536), jnp.zeros((2, 512), f32)], axis=1
    ).reshape(2, 40, 128)
    big, small = reduce_params(
        grad_four, grad_wup.astype(bf16), grad_wdown.astype(bf16), small, 2
    )
    small = small.reshape(5120)
    tot_bq, tot_bv, tot_bo, tot_gone, tot_sone, tot_bdown, tot_gtwo, tot_stwo = (
        small[i * 384 : (i + 1) * 384] for i in range(8)
    )
    tot_bup = small[3072:4608]
    big = big.astype(f32)
    return (
        result.astype(bf16)[None],
        grad_inputs[None],
        big[0, 0],
        tot_bq,
        big[0, 1],
        big[0, 2],
        tot_bv,
        big[0, 3],
        tot_bo,
        tot_gone,
        tot_sone,
        big[1].transpose(1, 0, 2).reshape(384, 3072),
        tot_bup,
        big[2].reshape(1536, 768),
        tot_bdown,
        tot_gtwo,
        tot_stwo,
    )


def solution(mesh):
    split = Mesh(
        mesh.devices.reshape(mesh.shape["seq"], 2, 4, 4, mesh.shape["wsh"]),
        ("seq", "ctx_0", "ctx_1", "ctx_2", "wsh"),
    )
    rows = P(("seq", "wsh"), CTX, None)
    mat, vec = P("wsh", None), P("wsh")
    params = (mat, vec, mat, mat, vec, mat, vec, vec, vec, mat, vec, mat, vec, vec, vec)
    return jax.shard_map(
        local,
        mesh=split,
        in_specs=(rows, P(("seq", "wsh")), *params, rows),
        out_specs=(rows, rows, *params),
        check_vma=False,
    )
```

```python
import functools
import math

import jax
import jax.numpy as jnp
from jax import lax
from jax.experimental import pallas as pl
from jax.experimental.pallas import tpu as pltpu
from jax.sharding import Mesh
from jax.sharding import PartitionSpec as P

H = 12
HD = 64
D = 768
CTX = ("ctx_0", "ctx_1", "ctx_2")
f32 = jnp.float32
bf16 = jnp.bfloat16
MESH = pl.DeviceIdType.MESH
ANY = pl.ANY
MIB = 1024 * 1024


def place(axis):
    if axis == "x":
        return lax.axis_index("ctx_2")
    if axis == "z":
        return lax.axis_index("ctx_1")
    return lax.axis_index("ctx_0") * 2 + lax.axis_index("seq")


def away(axis, step):
    at = lax.rem(place(axis) + step + 4, 4)
    if axis == "x":
        return {"ctx_2": at}
    if axis == "z":
        return {"ctx_1": at}
    return {"ctx_0": at // 2, "seq": lax.rem(at, 2)}


def sibling():
    return {"wsh": 1 - lax.axis_index("wsh")}


def far():
    return {"ctx_0": 1 - lax.axis_index("ctx_0")}


def meet(devices):
    barrier = pltpu.get_barrier_semaphore()
    for d in devices:
        pl.semaphore_signal(barrier, inc=1, device_id=d, device_id_type=MESH)
    pl.semaphore_wait(barrier, len(devices))


class Sends:
    def __init__(self, send, recv):
        self.send, self.recv, self.used, self.all = send, recv, 0, []

    def start(self, src, dst, device):
        k = self.used
        self.used += 1
        copy = pltpu.make_async_remote_copy(
            src_ref=src,
            dst_ref=dst,
            send_sem=self.send.at[k],
            recv_sem=self.recv.at[k],
            device_id=device,
            device_id_type=MESH,
        )
        copy.start()
        self.all.append(copy)
        return copy

    def finish(self):
        for copy in self.all:
            copy.wait_send()


def gather_kernel(rows, n_pair, *refs):
    n = len(rows)
    ins, pair_ins = refs[:n], refs[n : n + n_pair]
    outs, pair_outs = refs[n + n_pair : 2 * n + n_pair], refs[2 * n + n_pair : 2 * (n + n_pair)]
    send, recv, local = refs[2 * (n + n_pair) :]
    sends = Sends(send, recv)
    y, z, x = (lax.axis_index(a) for a in CTX)
    core = lax.axis_index("wsh")
    devices = [away("x", 1), away("x", -1), away("z", 1), away("z", -1), far()]
    if n_pair:
        devices.append(sibling())
    meet(devices)
    locals_ = []

    def keep(src, dst):
        copy = pltpu.make_async_copy(src, dst, local.at[len(locals_)])
        copy.start()
        locals_.append(copy)
        return copy

    own = [keep(i, o.at[y, z, x]) for i, o in zip(ins, outs)]
    crossing = [sends.start(i, o.at[y, z, x], far()) for i, o in zip(ins, outs)]

    def first(layer, mine):
        flights = []
        for i, o, r in zip(ins, outs, rows):
            h = r // 2
            for axis, lo in (("x", 0), ("z", h)):
                src = i.at[pl.ds(lo, h)] if mine else o.at[layer, z, x, pl.ds(lo, h)]
                dst = o.at[layer, z, x, pl.ds(lo, h)]
                flights.append(
                    [sends.start(src, dst, away(axis, 1)), sends.start(src, dst, away(axis, -1))]
                )
        return flights

    def first_on(layer, flights):
        later, at = [], 0
        for o, r in zip(outs, rows):
            q = r // 4
            for axis, lo in (("x", 0), ("z", 2 * q)):
                right, left = flights[at]
                at += 1
                pos = place(axis)
                before, after = lax.rem(pos + 3, 4), lax.rem(pos + 1, 4)
                right.wait_recv()
                if axis == "x":
                    a = o.at[layer, z, before, pl.ds(lo, q)]
                    b = o.at[layer, z, after, pl.ds(lo + q, q)]
                else:
                    a = o.at[layer, before, x, pl.ds(lo, q)]
                    b = o.at[layer, after, x, pl.ds(lo + q, q)]
                up = sends.start(a, a, away(axis, 1))
                left.wait_recv()
                later.append([up, sends.start(b, b, away(axis, -1))])
        return later

    def second(layer, flights):
        later, at = [], 0
        for o, r in zip(outs, rows):
            h = r // 2
            for axis, lo in (("z", 0), ("x", h)):
                for copy in flights[at]:
                    copy.wait_recv()
                at += 1
                if axis == "z":
                    a = o.at[layer, z, :, pl.ds(lo, h)]
                else:
                    a = o.at[layer, :, x, pl.ds(lo, h)]
                later.append([sends.start(a, a, away(axis, 1)), sends.start(a, a, away(axis, -1))])
        return later

    def second_on(layer, flights):
        later, at = [], 0
        for o, r in zip(outs, rows):
            h = r // 2
            for axis, lo in (("z", 0), ("x", h)):
                right, left = flights[at]
                at += 1
                pos = place(axis)
                before, after = lax.rem(pos + 3, 4), lax.rem(pos + 1, 4)
                right.wait_recv()
                if axis == "z":
                    a = o.at[layer, before, pl.ds(0, 2), pl.ds(lo, h)]
                    b = o.at[layer, after, pl.ds(2, 2), pl.ds(lo, h)]
                else:
                    a = o.at[layer, pl.ds(0, 2), before, pl.ds(lo, h)]
                    b = o.at[layer, pl.ds(2, 2), after, pl.ds(lo, h)]
                up = sends.start(a, a, away(axis, 1))
                left.wait_recv()
                later.append([up, sends.start(b, b, away(axis, -1))])
        return later

    mine = first(y, True)
    pairs = []
    for i, o in zip(pair_ins, pair_outs):
        pairs.append(sends.start(i, o.at[core], sibling()))
        keep(i, o.at[core])
    other = 1 - y
    mine = first_on(y, mine)
    for copy in crossing:
        copy.wait_recv()
    theirs = first(other, False)
    for copy in own:
        copy.wait()
    mine = second(y, mine)
    theirs = first_on(other, theirs)
    mine = second_on(y, mine)
    theirs = second(other, theirs)
    theirs = second_on(other, theirs)
    for flights in (mine, theirs):
        for pair in flights:
            for copy in pair:
                copy.wait_recv()
    for copy in pairs:
        copy.wait_recv()
    for copy in locals_[len(own) :]:
        copy.wait()
    sends.finish()


def gather(arrays, pairs, cid):
    n, m = len(arrays), len(pairs)
    outs = pl.pallas_call(
        functools.partial(gather_kernel, tuple(a.shape[0] for a in arrays), m),
        out_shape=[jax.ShapeDtypeStruct((2, 4, 4, *a.shape), a.dtype) for a in arrays]
        + [jax.ShapeDtypeStruct((2, *a.shape), a.dtype) for a in pairs],
        in_specs=[pl.BlockSpec(memory_space=ANY)] * (n + m),
        out_specs=[pl.BlockSpec(memory_space=ANY)] * (n + m),
        scratch_shapes=[
            pltpu.SemaphoreType.DMA((33 * n + m,)),
            pltpu.SemaphoreType.DMA((33 * n + m,)),
            pltpu.SemaphoreType.DMA((n + m,)),
        ],
        compiler_params=pltpu.CompilerParams(collective_id=cid, has_side_effects=True),
    )(*arrays, *pairs)
    return outs[:n], outs[n:]


class Flow:
    def __init__(self, sends, ins, outs, layer, mine):
        self.sends, self.ins, self.outs, self.layer, self.mine = sends, ins, outs, layer, mine
        self.z, self.x = lax.axis_index("ctx_1"), lax.axis_index("ctx_2")
        self.flights = []

    def wait(self):
        for pair in self.flights:
            for copy in pair:
                copy.wait_recv()

    def near(self, axis):
        pos = place(axis)
        return lax.rem(pos + 3, 4), lax.rem(pos + 1, 4)

    def first(self):
        y, z, x = self.layer, self.z, self.x
        self.flights = []
        for i, o in zip(self.ins, self.outs):
            h = i.shape[0] // 2
            for axis, lo in (("x", 0), ("z", h)):
                src = i.at[pl.ds(lo, h)] if self.mine else o.at[y, z, x, pl.ds(lo, h)]
                dst = o.at[y, z, x, pl.ds(lo, h)]
                self.flights.append(
                    [self.sends.start(src, dst, away(axis, k)) for k in (1, -1)]
                )

    def first_on(self):
        y, z, x, at, later = self.layer, self.z, self.x, 0, []
        for i, o in zip(self.ins, self.outs):
            q = i.shape[0] // 4
            for axis, lo in (("x", 0), ("z", 2 * q)):
                right, left = self.flights[at]
                at += 1
                before, after = self.near(axis)
                if axis == "x":
                    a = o.at[y, z, before, pl.ds(lo, q)]
                    b = o.at[y, z, after, pl.ds(lo + q, q)]
                else:
                    a = o.at[y, before, x, pl.ds(lo, q)]
                    b = o.at[y, after, x, pl.ds(lo + q, q)]
                right.wait_recv()
                up = self.sends.start(a, a, away(axis, 1))
                left.wait_recv()
                later.append([up, self.sends.start(b, b, away(axis, -1))])
        self.flights = later

    def second(self):
        y, z, x, at, later = self.layer, self.z, self.x, 0, []
        for i, o in zip(self.ins, self.outs):
            h = i.shape[0] // 2
            for axis, lo in (("z", 0), ("x", h)):
                for copy in self.flights[at]:
                    copy.wait_recv()
                at += 1
                a = o.at[y, z, :, pl.ds(lo, h)] if axis == "z" else o.at[y, :, x, pl.ds(lo, h)]
                later.append([self.sends.start(a, a, away(axis, k)) for k in (1, -1)])
        self.flights = later

    def second_on(self):
        y, at, later = self.layer, 0, []
        for i, o in zip(self.ins, self.outs):
            h = i.shape[0] // 2
            for axis, lo in (("z", 0), ("x", h)):
                right, left = self.flights[at]
                at += 1
                before, after = self.near(axis)
                if axis == "z":
                    a = o.at[y, before, pl.ds(0, 2), pl.ds(lo, h)]
                    b = o.at[y, after, pl.ds(2, 2), pl.ds(lo, h)]
                else:
                    a = o.at[y, pl.ds(0, 2), before, pl.ds(lo, h)]
                    b = o.at[y, pl.ds(2, 2), after, pl.ds(lo, h)]
                right.wait_recv()
                up = self.sends.start(a, a, away(axis, 1))
                left.wait_recv()
                later.append([up, self.sends.start(b, b, away(axis, -1))])
        self.flights = later


def units(layer, steps):
    z, x = lax.axis_index("ctx_1"), lax.axis_index("ctx_2")
    picked = []
    for k in steps:
        picked.append(("A", layer, lax.rem(z + k + 4, 4)))
        picked.append(("B", layer, lax.rem(x + k + 4, 4)))
    return picked


def unit_at(unit):
    half, layer, i = unit
    if half == "A":
        return (layer, i, slice(None), pl.ds(0, 64))
    return (layer, slice(None), i, pl.ds(64, 64))


def start_kernel(*refs):
    x_in, pair_ins = refs[0], refs[1:8]
    outs, pair_outs = refs[8:11], refs[11:18]
    xs, held, made = refs[18], refs[19:26], refs[26:29]
    send, recv, local, leave = refs[29:]
    sends = Sends(send, recv)
    y, z, x = (lax.axis_index(a) for a in CTX)
    core = lax.axis_index("wsh")
    meet(
        [away("x", 1), away("x", -1), away("z", 1), away("z", -1), far(), sibling()]
    )
    crossing = sends.start(x_in, xs.at[y, z, x], far())
    mine = Flow(sends, [x_in], [xs], y, True)
    theirs = Flow(sends, [x_in], [xs], 1 - y, False)
    mine.first()
    own = pltpu.make_async_copy(x_in, xs.at[y, z, x], local.at[7])
    own.start()
    pairs, kept, left = [], [], []
    for n, (i, o) in enumerate(zip(pair_ins, held)):
        pairs.append(sends.start(i, o.at[core], sibling()))
        copy = pltpu.make_async_copy(i, o.at[core], local.at[n])
        copy.start()
        kept.append(copy)

    def depart(src, dst):
        copy = pltpu.make_async_copy(src, dst, leave.at[len(left)])
        copy.start()
        left.append(copy)

    def whole(n):
        kept[n].wait()
        pairs[n].wait_recv()
        depart(held[n], pair_outs[n])

    def project(unit):
        at = unit_at(unit)
        block = xs[at].reshape(256, D)
        for n, row in ((0, 0), (1, None), (2, 1)):
            value = nn(block, held[n][...].reshape(D, D))
            if row is not None:
                value = value + jnp.concatenate(
                    [held[6][c, row : row + 1] for c in range(2)], axis=1
                ).astype(f32)
            made[n][at] = value.astype(bf16).reshape(4, 64, D)
            depart(made[n].at[at], outs[n].at[at])

    mine.first_on()
    crossing.wait_recv()
    theirs.first()
    own.wait()
    mine.second()
    theirs.first_on()
    for n in (6, 0, 1, 2):
        whole(n)
    for unit in units(y, (0,)):
        project(unit)
    mine.second_on()
    theirs.second()
    for unit in units(y, (1, -1)):
        project(unit)
    mine.wait()
    for unit in units(y, (2,)):
        project(unit)
    for unit in units(1 - y, (0,)):
        project(unit)
    theirs.second_on()
    for n in (3, 4, 5):
        whole(n)
    for unit in units(1 - y, (1, -1)):
        project(unit)
    theirs.wait()
    for unit in units(1 - y, (2,)):
        project(unit)
    for copy in left:
        copy.wait()
    sends.finish()


def start(block, pairs, cid):
    n_send = 1 + 32 + 7
    return pl.pallas_call(
        start_kernel,
        out_shape=[jax.ShapeDtypeStruct((2, 4, 4, 128, D), bf16)] * 3
        + [jax.ShapeDtypeStruct((2, *a.shape), a.dtype) for a in pairs],
        in_specs=[pl.BlockSpec(memory_space=pltpu.HBM)] * 8,
        out_specs=[pl.BlockSpec(memory_space=pltpu.HBM)] * 10,
        scratch_shapes=[pltpu.VMEM((2, 4, 4, 128, D), bf16)]
        + [pltpu.VMEM((2, *a.shape), a.dtype) for a in pairs]
        + [pltpu.VMEM((2, 4, 4, 128, D), bf16)] * 3
        + [
            pltpu.SemaphoreType.DMA((n_send,)),
            pltpu.SemaphoreType.DMA((n_send,)),
            pltpu.SemaphoreType.DMA((8,)),
            pltpu.SemaphoreType.DMA((16 * 3 + 7,)),
        ],
        compiler_params=pltpu.CompilerParams(
            collective_id=cid, has_side_effects=True, vmem_limit_bytes=60 * MIB
        ),
    )(block, *pairs)


ORDERS = (("x", "y", "z"), ("y", "z", "x"), ("z", "x", "y"))
AXES = ("x", "y", "z")
SPLIT = ((192, 192), (48, 48), (32, 16))
CHUNK = ((384, 768), (96, 768), (48, 384))


def reduce_kernel(
    g0, g1, g2, small, out, small_out,
    acc, pair, t0, t1, t2, u0, u1, u2, cur, slots, send, recv, local,
):
    core = lax.axis_index("wsh")
    twin = 1 - core
    sends = Sends(send, recv)
    tt, uu = (t0, t1, t2), (u0, u1, u2)
    pos = {a: place(a) for a in AXES}
    meet([sibling()] + [away(a, k) for a in AXES for k in (1, 2, 3)])

    def share(s, m, half):
        if s == 0:
            return g0.at[m, pl.ds(pl.multiple_of(half * 384, 384), 384)]
        if s == 1:
            return g1.at[pl.ds(pl.multiple_of(half * 384, 384), 384), pl.ds(m * 768, 768)]
        return g2.at[pl.ds(pl.multiple_of(half * 1536 + m * 384, 384), 384)]

    small_pair = sends.start(small.at[twin], slots.at[3, 0], sibling())
    flights, kept = [], []
    for m in range(4):
        for s in range(3):
            flights.append((s, m, sends.start(share(s, m, twin), pair.at[s, m], sibling())))
            copy = pltpu.make_async_copy(share(s, m, core), acc.at[s, m], local.at[s * 4 + m])
            copy.start()
            kept.append(copy)
    mine = pltpu.make_async_copy(small.at[core], cur, local.at[12])
    mine.start()
    mine.wait()
    small_pair.wait_recv()
    cur[...] = cur[...] + slots[3, 0]

    def add(dst, dst_at, src, src_at, shape):
        rows, cols = shape

        @pl.loop(0, rows // 16)
        def _(k):
            a = dst_at(pl.multiple_of(k * 16, 16))
            b = src_at(pl.multiple_of(k * 16, 16))
            dst[a] = (dst[a].astype(f32) + src[b].astype(f32)).astype(bf16)

    for (s, m, flight), copy in zip(flights, kept):
        copy.wait()
        flight.wait_recv()
        add(
            acc, lambda r, s=s, m=m: (s, m, pl.ds(r, 16)),
            pair, lambda r, s=s, m=m: (s, m, pl.ds(r, 16)), (384, 768),
        )

    def region(ph, s, c, r, n):
        a, b, _ = (pos[k] for k in ORDERS[s])
        if ph == 0:
            return (s, c, pl.ds(r, n))
        if ph == 1:
            return (s, a, pl.ds(pl.multiple_of(96 * c + r, 16), n))
        return (
            s, a, pl.ds(pl.multiple_of(96 * b + 48 * (c // 2) + r, 16), n),
            pl.ds(pl.multiple_of(lax.rem(c, 2) * 384, 384), 384),
        )

    small_axis = {}
    for ph in range(3):
        axis = AXES[ph]
        slots[ph, pos[axis]] = cur[...]
        small_axis = [
            sends.start(cur, slots.at[ph, pos[axis]], away(axis, k)) for k in (1, 2, 3)
        ]
        rows, cols = CHUNK[ph]
        near, rest = SPLIT[ph]
        steps = []
        for s in range(3):
            axis_s = ORDERS[s][ph]
            p = pos[axis_s]
            c = lax.rem(p + 2, 4)
            steps.append((
                sends.start(
                    acc.at[region(ph, s, c, 0, near)], tt[ph].at[s, 0, pl.ds(0, near)], away(axis_s, 1)
                ),
                sends.start(
                    acc.at[region(ph, s, c, near, rest)], tt[ph].at[s, 1, pl.ds(0, rest)], away(axis_s, -1)
                ),
            ))
        nexts = []
        for s in range(3):
            axis_s = ORDERS[s][ph]
            p = pos[axis_s]
            up, down = lax.rem(p + 1, 4), lax.rem(p + 3, 4)
            steps[s][0].wait_recv()
            add(
                acc, lambda r, s=s, up=up: region(ph, s, up, r, 16),
                tt[ph], lambda r, s=s: (s, 0, pl.ds(r, 16)), (near, cols),
            )
            a = sends.start(acc.at[region(ph, s, up, 0, rows)], uu[ph].at[s, 0], away(axis_s, 1))
            steps[s][1].wait_recv()
            add(
                acc, lambda r, s=s, down=down: region(ph, s, down, near + r, 16),
                tt[ph], lambda r, s=s: (s, 1, pl.ds(r, 16)), (rest, cols),
            )
            b = sends.start(acc.at[region(ph, s, down, 0, rows)], uu[ph].at[s, 1], away(axis_s, -1))
            nexts.append((a, b))
        for s in range(3):
            p = pos[ORDERS[s][ph]]
            for k in range(2):
                nexts[s][k].wait_recv()
                add(
                    acc, lambda r, s=s, p=p: region(ph, s, p, r, 16),
                    uu[ph], lambda r, s=s, k=k: (s, k, pl.ds(r, 16)), (rows, cols),
                )
        for copy in small_axis:
            copy.wait()
        sends.all = [c for c in sends.all if all(c is not d for d in small_axis)]
        cur[...] = (slots[ph, 0] + slots[ph, 1]) + (slots[ph, 2] + slots[ph, 3])

    small_out[...] = cur[...]

    for ph in (2, 1, 0):
        rows, cols = CHUNK[ph]
        near, rest = SPLIT[ph]
        steps = []
        for s in range(3):
            axis_s = ORDERS[s][ph]
            p = pos[axis_s]
            here = region(ph, s, p, 0, rows)
            if ph == 2:
                kept_copy = pltpu.make_async_copy(acc.at[here], out.at[here], local.at[s])
                kept_copy.start()
                src = acc.at[here]
            else:
                kept_copy = None
                src = out.at[here]
            steps.append((
                sends.start(src, out.at[here], away(axis_s, 1)),
                sends.start(src, out.at[here], away(axis_s, -1)),
                kept_copy,
            ))
        nexts = []
        for s in range(3):
            axis_s = ORDERS[s][ph]
            p = pos[axis_s]
            up, down = lax.rem(p + 1, 4), lax.rem(p + 3, 4)
            steps[s][0].wait_recv()
            part = out.at[region(ph, s, down, 0, near)]
            a = sends.start(part, part, away(axis_s, 1))
            steps[s][1].wait_recv()
            part = out.at[region(ph, s, up, near, rest)]
            b = sends.start(part, part, away(axis_s, -1))
            nexts.append((a, b))
        for s in range(3):
            if steps[s][2] is not None:
                steps[s][2].wait()
            for copy in nexts[s]:
                copy.wait_recv()
    sends.finish()


def reduce_params(g0, g1, g2, small, cid):
    scratch = [pltpu.VMEM((3, 4, 384, 768), bf16), pltpu.VMEM((3, 4, 384, 768), bf16)]
    scratch += [pltpu.VMEM((3, 2, SPLIT[k][0], CHUNK[k][1]), bf16) for k in range(3)]
    scratch += [pltpu.VMEM((3, 2, *CHUNK[k]), bf16) for k in range(3)]
    scratch += [pltpu.VMEM((40, 128), f32), pltpu.VMEM((4, 4, 40, 128), f32)]
    count = 1 + 12 + 9 + 3 * 24
    scratch += [
        pltpu.SemaphoreType.DMA((count,)),
        pltpu.SemaphoreType.DMA((count,)),
        pltpu.SemaphoreType.DMA((13,)),
    ]
    return pl.pallas_call(
        reduce_kernel,
        out_shape=[
            jax.ShapeDtypeStruct((3, 4, 384, 768), bf16),
            jax.ShapeDtypeStruct((40, 128), f32),
        ],
        in_specs=[pl.BlockSpec(memory_space=pltpu.HBM)] * 4,
        out_specs=[pl.BlockSpec(memory_space=pltpu.HBM), pl.BlockSpec(memory_space=pltpu.VMEM)],
        scratch_shapes=scratch,
        compiler_params=pltpu.CompilerParams(
            collective_id=cid, has_side_effects=True, vmem_limit_bytes=40 * MIB
        ),
    )(g0, g1, g2, small)


def finish_kernel(big_ref, q_ref, k_ref, v_ref, o_ref, up_ref, down_ref):
    for n, ref in enumerate((q_ref, k_ref, v_ref, o_ref)):
        ref[...] = big_ref[0, n].astype(f32)
        up_ref[:, n * 768 : (n + 1) * 768] = big_ref[1, n].astype(f32)
        down_ref[n] = big_ref[2, n].astype(f32)


def finish(big):
    mat = pl.BlockSpec((96, 768), lambda r: (r, 0))
    return pl.pallas_call(
        finish_kernel,
        grid=(4,),
        out_shape=[jax.ShapeDtypeStruct((384, 768), f32)] * 4
        + [
            jax.ShapeDtypeStruct((384, 3072), f32),
            jax.ShapeDtypeStruct((4, 384, 768), f32),
        ],
        in_specs=[pl.BlockSpec((3, 4, 96, 768), lambda r: (0, 0, r, 0))],
        out_specs=[mat] * 4
        + [
            pl.BlockSpec((96, 3072), lambda r: (r, 0)),
            pl.BlockSpec((4, 96, 768), lambda r: (0, r, 0)),
        ],
        compiler_params=pltpu.CompilerParams(vmem_limit_bytes=40 * MIB),
    )(big)


def nt(a, b):
    return lax.dot_general(a, b, (((1,), (1,)), ((), ())), preferred_element_type=f32)


def nn(a, b):
    return jnp.dot(a, b, preferred_element_type=f32)


def stacked(block):
    lane = lax.broadcasted_iota(jnp.int32, block.shape, 1) // HD
    zero = jnp.zeros_like(block)
    return jnp.concatenate([jnp.where(lane == i, block, zero) for i in range(4)], axis=0)


def unstacked(tall):
    n = tall.shape[0] // 4
    lane = lax.broadcasted_iota(jnp.int32, (n, tall.shape[1]), 1) // HD
    total = jnp.where(lane == 0, tall[:n], 0.0)
    for i in range(1, 4):
        total = total + jnp.where(lane == i, tall[i * n : (i + 1) * n], 0.0)
    return total


def as_rows(column):
    wide = jnp.broadcast_to(column, (column.shape[0], 128))
    return jnp.concatenate(
        [wide[i * 128 : (i + 1) * 128].T[:1] for i in range(4)] + [jnp.zeros((4, 128), f32)], axis=0
    )


TILE = 1024


def forward_kernel(q_ref, k_ref, v_ref, bias_ref, attn_ref, lse_ref, rows_ref, score):
    q = stacked(q_ref[...] * jnp.asarray(0.125, bf16))
    top = None
    for t in range(4096 // TILE):
        at = pl.ds(t * TILE, TILE)
        s = nt(q, k_ref[at, :]) + bias_ref[:, at]
        score[:, at] = s
        m = jnp.max(s, axis=-1, keepdims=True)
        top = m if top is None else jnp.maximum(top, m)
    total, out = 0.0, 0.0
    for t in range(4096 // TILE):
        at = pl.ds(t * TILE, TILE)
        p = jnp.exp(score[:, at] - top)
        total = total + jnp.sum(p, axis=-1, keepdims=True)
        out = out + nn(p.astype(bf16), v_ref[at, :])
    attn_ref[...] = unstacked(out * (1.0 / total))
    lse = top + jnp.log(total)
    lse_ref[0] = jnp.broadcast_to(lse, (512, 128))
    rows_ref[0] = as_rows(lse)


def attend(q, k, v, bias):
    wide = pl.BlockSpec((4096, 256), lambda g: (0, g))
    own = pl.BlockSpec((128, 256), lambda g: (0, g))
    return pl.pallas_call(
        forward_kernel,
        grid=(3,),
        out_shape=[
            jax.ShapeDtypeStruct((128, D), f32),
            jax.ShapeDtypeStruct((3, 512, 128), f32),
            jax.ShapeDtypeStruct((3, 8, 128), f32),
        ],
        in_specs=[own, wide, wide, pl.BlockSpec((1, 4096), lambda g: (0, 0))],
        out_specs=[
            own,
            pl.BlockSpec((1, 512, 128), lambda g: (g, 0, 0)),
            pl.BlockSpec((1, 8, 128), lambda g: (g, 0, 0)),
        ],
        scratch_shapes=[pltpu.VMEM((512, 4096), f32)],
        compiler_params=pltpu.CompilerParams(vmem_limit_bytes=56 * MIB),
    )(q, k, v, bias)


def query_kernel(q_ref, k_ref, v_ref, bias_ref, g_ref, attn_ref, lse_ref, dq_ref, rows_ref):
    q = stacked(q_ref[...] * jnp.asarray(0.125, bf16))
    g = stacked(g_ref[...])
    attn = attn_ref[...]
    tall = jnp.concatenate([attn] * 4, axis=0)
    delta = jnp.sum(g.astype(f32) * tall, axis=-1, keepdims=True)
    rows_ref[0] = as_rows(delta)
    lse = lse_ref[0][:, :1]
    dq = 0.0
    for t in range(4096 // TILE):
        at = pl.ds(t * TILE, TILE)
        p = jnp.exp(nt(q, k_ref[at, :]) + bias_ref[:, at] - lse)
        dp = nt(g, v_ref[at, :])
        ds = (p * (dp - delta)).astype(bf16)
        dq = dq + nn(ds, k_ref[at, :])
    dq_ref[...] = (unstacked(dq) * 0.125).astype(bf16)


def query_grads(q, k, v, bias, g, attn, lse):
    wide = pl.BlockSpec((4096, 256), lambda g: (0, g))
    own = pl.BlockSpec((128, 256), lambda g: (0, g))
    return pl.pallas_call(
        query_kernel,
        grid=(3,),
        out_shape=[jax.ShapeDtypeStruct((128, D), bf16), jax.ShapeDtypeStruct((3, 8, 128), f32)],
        in_specs=[
            own, wide, wide, pl.BlockSpec((1, 4096), lambda g: (0, 0)), own, own,
            pl.BlockSpec((1, 512, 128), lambda g: (g, 0, 0)),
        ],
        out_specs=[own, pl.BlockSpec((1, 8, 128), lambda g: (g, 0, 0))],
        compiler_params=pltpu.CompilerParams(vmem_limit_bytes=56 * MIB),
    )(q, k, v, bias, g, attn, lse)


def key_kernel(k_ref, v_ref, bias_ref, q_ref, g_ref, lse_ref, delta_ref, dk_ref, dv_ref):
    k = stacked(k_ref[...] * jnp.asarray(0.125, bf16))
    v = stacked(v_ref[...])
    bias = jnp.concatenate([bias_ref[:, :1]] * 4, axis=0)
    dk, dv = 0.0, 0.0
    for t in range(4096 // TILE):
        at = pl.ds(t * TILE, TILE)
        q, g = q_ref[at, :], g_ref[at, :]
        lse = jnp.concatenate(
            [jnp.broadcast_to(lse_ref[0, i : i + 1, at], (128, TILE)) for i in range(4)], axis=0
        )
        delta = jnp.concatenate(
            [jnp.broadcast_to(delta_ref[0, i : i + 1, at], (128, TILE)) for i in range(4)], axis=0
        )
        p = jnp.exp(nt(k, q) + bias - lse)
        ds = (p * (nt(v, g) - delta)).astype(bf16)
        dv = dv + nn(p.astype(bf16), g)
        dk = dk + nn(ds, q)
    dk_ref[...] = (unstacked(dk) * 0.125).astype(bf16)
    dv_ref[...] = unstacked(dv).astype(bf16)


def key_grads(k, v, bias, q, g, lse, delta):
    wide = pl.BlockSpec((4096, 256), lambda g: (0, g))
    own = pl.BlockSpec((128, 256), lambda g: (0, g))
    stat = pl.BlockSpec((1, 8, 4096), lambda g: (g, 0, 0))
    return pl.pallas_call(
        key_kernel,
        grid=(3,),
        out_shape=[jax.ShapeDtypeStruct((128, D), bf16)] * 2,
        in_specs=[own, own, pl.BlockSpec((128, 128), lambda g: (0, 0)), wide, wide, stat, stat],
        out_specs=[own, own],
        compiler_params=pltpu.CompilerParams(vmem_limit_bytes=56 * MIB),
    )(k, v, bias, q, g, lse, delta)


def layer_norm(resid, gain, shift):
    centre = resid - jnp.mean(resid, axis=-1, keepdims=True)
    spread = jnp.mean(centre * centre, axis=-1, keepdims=True)
    return centre * lax.rsqrt(spread + 1e-12) * gain + shift


def gelu_exact(value):
    return jax.nn.gelu(value, approximate=False)


def local(
    tokens, lengths, w_query, b_query, w_key, w_value, b_value, w_out, b_out, gain_one, shift_one,
    w_up, b_up, w_down, b_down, gain_two, shift_two, cotangent,
):
    inputs = tokens[0]
    vectors = jnp.stack(
        [b_query, b_value, b_out, gain_one, shift_one, b_down, gain_two, shift_two]
    )
    vectors = jnp.concatenate([vectors, b_up.reshape(4, 384), jnp.zeros((4, 384), bf16)], axis=0)
    all_q, all_k, all_v, *whole = start(
        inputs, [w_query, w_key, w_value, w_out, w_up, w_down, vectors], 0
    )
    all_q, all_k, all_v = (a.reshape(4096, D) for a in (all_q, all_k, all_v))
    wq, wk, wv, wo, wup, wdown = (w.reshape(-1, w.shape[-1]) for w in whole[:6])
    vecs = whole[6].astype(f32)
    bo, gone, sone, bdown, gtwo, stwo = (vecs[:, i].reshape(768) for i in range(2, 8))
    bup = vecs[:, 8:12].reshape(3072)
    seq_len = lengths[0]
    block = (lax.axis_index("ctx_0") * 4 + lax.axis_index("ctx_1")) * 4 + lax.axis_index("ctx_2")
    q = lax.dynamic_slice_in_dim(all_q, block * 128, 128)
    k = lax.dynamic_slice_in_dim(all_k, block * 128, 128)
    v = lax.dynamic_slice_in_dim(all_v, block * 128, 128)
    bias = jnp.where(jnp.arange(4096) < seq_len, 0.0, -1e30).astype(f32)[None]
    own_bias = jnp.where(jnp.arange(128) + block * 128 < seq_len, 0.0, -1e30).astype(f32)
    own_bias = jnp.broadcast_to(own_bias[:, None], (128, 128))
    attn, lse, lse_rows = attend(q, all_k, all_v, bias)
    mixed = attn.astype(bf16)
    resid_one = inputs.astype(f32) + jnp.dot(mixed, wo, preferred_element_type=f32) + bo
    first, pull_one = jax.vjp(layer_norm, resid_one, gone, sone)
    first_low = first.astype(bf16)
    pre = jnp.dot(first_low, wup, preferred_element_type=f32) + bup
    act, pull_gelu = jax.vjp(gelu_exact, pre)
    act_low = act.astype(bf16)
    resid_two = first + jnp.dot(act_low, wdown, preferred_element_type=f32) + bdown
    result, pull_two = jax.vjp(layer_norm, resid_two, gtwo, stwo)
    grad_resid_two, grad_gtwo, grad_stwo = pull_two(cotangent[0].astype(f32))
    grad_down_low = grad_resid_two.astype(bf16)
    grad_bdown = jnp.sum(grad_resid_two, axis=0)
    grad_wdown = jnp.einsum("tf,td->fd", act_low, grad_down_low, preferred_element_type=f32)
    grad_act = jnp.einsum("td,fd->tf", grad_down_low, wdown, preferred_element_type=f32)
    grad_pre_low = pull_gelu(grad_act)[0].astype(bf16)
    grad_bup = jnp.sum(grad_pre_low.astype(f32), axis=0)
    grad_wup = jnp.einsum("td,tf->df", first_low, grad_pre_low, preferred_element_type=f32)
    grad_first = grad_resid_two + jnp.einsum(
        "tf,df->td", grad_pre_low, wup, preferred_element_type=f32
    )
    grad_resid_one, grad_gone, grad_sone = pull_one(grad_first)
    grad_branch = grad_resid_one.astype(bf16)
    grad_bout = jnp.sum(grad_resid_one, axis=0)
    grad_mixed = jnp.einsum("te,de->td", grad_branch, wo, preferred_element_type=f32).astype(bf16)
    grad_query_low, delta_rows = query_grads(q, all_k, all_v, bias, grad_mixed, attn, lse)
    pad = jnp.zeros((4, 128), f32)
    stats = jnp.concatenate(
        [lse_rows[:, :4].reshape(12, 128), pad, delta_rows[:, :4].reshape(12, 128), pad], axis=0
    )
    (all_g, all_stats), _ = gather([grad_mixed, stats], [], 1)
    all_g = all_g.reshape(4096, D)
    all_stats = all_stats.reshape(32, 32, 128).transpose(1, 0, 2).reshape(32, 4096)
    all_lse = jnp.pad(all_stats[:12].reshape(3, 4, 4096), ((0, 0), (0, 4), (0, 0)))
    all_delta = jnp.pad(all_stats[16:28].reshape(3, 4, 4096), ((0, 0), (0, 4), (0, 0)))
    grad_keys_low, grad_values_low = key_grads(k, v, own_bias, all_q, all_g, all_lse, all_delta)
    lefts = jnp.stack([inputs, inputs, inputs, mixed])
    rights = jnp.stack([grad_query_low, grad_keys_low, grad_values_low, grad_branch])
    grad_four = jnp.einsum("ktd,kte->kde", lefts, rights, preferred_element_type=f32).astype(bf16)
    grad_bq = jnp.sum(grad_query_low.astype(f32), axis=0)
    grad_bv = jnp.sum(grad_values_low.astype(f32), axis=0)
    grad_inputs = grad_resid_one + jnp.einsum(
        "te,de->td", grad_query_low, wq, preferred_element_type=f32
    )
    grad_inputs = grad_inputs + jnp.einsum(
        "te,de->td", grad_keys_low, wk, preferred_element_type=f32
    )
    grad_inputs = grad_inputs + jnp.einsum(
        "te,de->td", grad_values_low, wv, preferred_element_type=f32
    )
    small = jnp.stack(
        [grad_bq, grad_bv, grad_bout, grad_gone, grad_sone, grad_bdown, grad_gtwo, grad_stwo]
    )
    small = small.reshape(8, 2, 384).transpose(1, 0, 2).reshape(2, 3072)
    small = jnp.concatenate(
        [small, grad_bup.reshape(2, 1536), jnp.zeros((2, 512), f32)], axis=1
    ).reshape(2, 40, 128)
    big, small = reduce_params(
        grad_four, grad_wup.astype(bf16), grad_wdown.astype(bf16), small, 2
    )
    small = small.reshape(5120)
    tot_bq, tot_bv, tot_bo, tot_gone, tot_sone, tot_bdown, tot_gtwo, tot_stwo = (
        small[i * 384 : (i + 1) * 384] for i in range(8)
    )
    tot_bup = small[3072:4608]
    tot_wq, tot_wk, tot_wv, tot_wo, tot_wup, tot_wdown = finish(big)
    return (
        result.astype(bf16)[None],
        grad_inputs[None],
        tot_wq,
        tot_bq,
        tot_wk,
        tot_wv,
        tot_bv,
        tot_wo,
        tot_bo,
        tot_gone,
        tot_sone,
        tot_wup,
        tot_bup,
        tot_wdown.reshape(1536, 768),
        tot_bdown,
        tot_gtwo,
        tot_stwo,
    )


def solution(mesh):
    split = Mesh(
        mesh.devices.reshape(mesh.shape["seq"], 2, 4, 4, mesh.shape["wsh"]),
        ("seq", "ctx_0", "ctx_1", "ctx_2", "wsh"),
    )
    rows = P(("seq", "wsh"), CTX, None)
    mat, vec = P("wsh", None), P("wsh")
    params = (mat, vec, mat, mat, vec, mat, vec, vec, vec, mat, vec, mat, vec, vec, vec)
    return jax.shard_map(
        local,
        mesh=split,
        in_specs=(rows, P(("seq", "wsh")), *params, rows),
        out_specs=(rows, rows, *params),
        check_vma=False,
    )
```

```python
import functools
import math

import jax
import jax.numpy as jnp
from jax import lax
from jax.experimental import pallas as pl
from jax.experimental.pallas import tpu as pltpu
from jax.sharding import Mesh
from jax.sharding import PartitionSpec as P

H = 12
HD = 64
D = 768
CTX = ("ctx_0", "ctx_1", "ctx_2")
f32 = jnp.float32
bf16 = jnp.bfloat16
MESH = pl.DeviceIdType.MESH
ANY = pl.ANY
MIB = 1024 * 1024


def place(axis):
    if axis == "x":
        return lax.axis_index("ctx_2")
    if axis == "z":
        return lax.axis_index("ctx_1")
    return lax.axis_index("ctx_0") * 2 + lax.axis_index("seq")


def away(axis, step):
    at = lax.rem(place(axis) + step + 4, 4)
    if axis == "x":
        return {"ctx_2": at}
    if axis == "z":
        return {"ctx_1": at}
    return {"ctx_0": at // 2, "seq": lax.rem(at, 2)}


def sibling():
    return {"wsh": 1 - lax.axis_index("wsh")}


def far():
    return {"ctx_0": 1 - lax.axis_index("ctx_0")}


def meet(devices):
    barrier = pltpu.get_barrier_semaphore()
    for d in devices:
        pl.semaphore_signal(barrier, inc=1, device_id=d, device_id_type=MESH)
    pl.semaphore_wait(barrier, len(devices))


class Sends:
    def __init__(self, send, recv):
        self.send, self.recv, self.used, self.all = send, recv, 0, []

    def start(self, src, dst, device):
        k = self.used
        self.used += 1
        copy = pltpu.make_async_remote_copy(
            src_ref=src,
            dst_ref=dst,
            send_sem=self.send.at[k],
            recv_sem=self.recv.at[k],
            device_id=device,
            device_id_type=MESH,
        )
        copy.start()
        self.all.append(copy)
        return copy

    def finish(self):
        for copy in self.all:
            copy.wait_send()


class Flow:
    def __init__(self, sends, ins, outs, layer, mine):
        self.sends, self.ins, self.outs, self.layer, self.mine = sends, ins, outs, layer, mine
        self.z, self.x = lax.axis_index("ctx_1"), lax.axis_index("ctx_2")
        self.flights = []

    def wait(self):
        for pair in self.flights:
            for copy in pair:
                copy.wait_recv()

    def near(self, axis):
        pos = place(axis)
        return lax.rem(pos + 3, 4), lax.rem(pos + 1, 4)

    def first(self):
        y, z, x = self.layer, self.z, self.x
        self.flights = []
        for i, o in zip(self.ins, self.outs):
            h = i.shape[0] // 2
            for axis, lo in (("x", 0), ("z", h)):
                src = i.at[pl.ds(lo, h)] if self.mine else o.at[y, z, x, pl.ds(lo, h)]
                dst = o.at[y, z, x, pl.ds(lo, h)]
                self.flights.append(
                    [self.sends.start(src, dst, away(axis, k)) for k in (1, -1)]
                )

    def first_on(self):
        y, z, x, at, later = self.layer, self.z, self.x, 0, []
        for i, o in zip(self.ins, self.outs):
            q = i.shape[0] // 4
            for axis, lo in (("x", 0), ("z", 2 * q)):
                right, left = self.flights[at]
                at += 1
                before, after = self.near(axis)
                if axis == "x":
                    a = o.at[y, z, before, pl.ds(lo, q)]
                    b = o.at[y, z, after, pl.ds(lo + q, q)]
                else:
                    a = o.at[y, before, x, pl.ds(lo, q)]
                    b = o.at[y, after, x, pl.ds(lo + q, q)]
                right.wait_recv()
                up = self.sends.start(a, a, away(axis, 1))
                left.wait_recv()
                later.append([up, self.sends.start(b, b, away(axis, -1))])
        self.flights = later

    def second(self):
        y, z, x, at, later = self.layer, self.z, self.x, 0, []
        for i, o in zip(self.ins, self.outs):
            h = i.shape[0] // 2
            for axis, lo in (("z", 0), ("x", h)):
                for copy in self.flights[at]:
                    copy.wait_recv()
                at += 1
                a = o.at[y, z, :, pl.ds(lo, h)] if axis == "z" else o.at[y, :, x, pl.ds(lo, h)]
                later.append([self.sends.start(a, a, away(axis, k)) for k in (1, -1)])
        self.flights = later

    def second_on(self):
        y, at, later = self.layer, 0, []
        for i, o in zip(self.ins, self.outs):
            h = i.shape[0] // 2
            for axis, lo in (("z", 0), ("x", h)):
                right, left = self.flights[at]
                at += 1
                before, after = self.near(axis)
                if axis == "z":
                    a = o.at[y, before, pl.ds(0, 2), pl.ds(lo, h)]
                    b = o.at[y, after, pl.ds(2, 2), pl.ds(lo, h)]
                else:
                    a = o.at[y, pl.ds(0, 2), before, pl.ds(lo, h)]
                    b = o.at[y, pl.ds(2, 2), after, pl.ds(lo, h)]
                right.wait_recv()
                up = self.sends.start(a, a, away(axis, 1))
                left.wait_recv()
                later.append([up, self.sends.start(b, b, away(axis, -1))])
        self.flights = later


def units(layer, steps):
    z, x = lax.axis_index("ctx_1"), lax.axis_index("ctx_2")
    picked = []
    for k in steps:
        picked.append(("A", layer, lax.rem(z + k + 4, 4)))
        picked.append(("B", layer, lax.rem(x + k + 4, 4)))
    return picked


def unit_at(unit):
    half, layer, i = unit
    if half == "A":
        return (layer, i, slice(None), pl.ds(0, 64))
    return (layer, slice(None), i, pl.ds(64, 64))


def start_kernel(*refs):
    x_in, pair_ins = refs[0], refs[1:8]
    outs, pair_outs = refs[8:11], refs[11:18]
    xs, held, made = refs[18], refs[19:26], refs[26:29]
    send, recv, local, leave = refs[29:]
    sends = Sends(send, recv)
    y, z, x = (lax.axis_index(a) for a in CTX)
    core = lax.axis_index("wsh")
    meet(
        [away("x", 1), away("x", -1), away("z", 1), away("z", -1), far(), sibling()]
    )
    crossing = sends.start(x_in, xs.at[y, z, x], far())
    mine = Flow(sends, [x_in], [xs], y, True)
    theirs = Flow(sends, [x_in], [xs], 1 - y, False)
    mine.first()
    own = pltpu.make_async_copy(x_in, xs.at[y, z, x], local.at[7])
    own.start()
    pairs, kept, left = [], [], []
    for n, (i, o) in enumerate(zip(pair_ins, held)):
        pairs.append(sends.start(i, o.at[core], sibling()))
        copy = pltpu.make_async_copy(i, o.at[core], local.at[n])
        copy.start()
        kept.append(copy)

    def depart(src, dst):
        copy = pltpu.make_async_copy(src, dst, leave.at[len(left)])
        copy.start()
        left.append(copy)

    def whole(n):
        kept[n].wait()
        pairs[n].wait_recv()
        depart(held[n], pair_outs[n])

    def project(unit):
        at = unit_at(unit)
        block = xs[at].reshape(256, D)
        for n, row in ((0, 0), (1, None), (2, 1)):
            value = nn(block, held[n][...].reshape(D, D))
            if row is not None:
                value = value + jnp.concatenate(
                    [held[6][c, row : row + 1] for c in range(2)], axis=1
                ).astype(f32)
            made[n][at] = value.astype(bf16).reshape(4, 64, D)
            depart(made[n].at[at], outs[n].at[at])

    mine.first_on()
    crossing.wait_recv()
    theirs.first()
    own.wait()
    mine.second()
    theirs.first_on()
    for n in (6, 0, 1, 2):
        whole(n)
    for unit in units(y, (0,)):
        project(unit)
    mine.second_on()
    theirs.second()
    for unit in units(y, (1, -1)):
        project(unit)
    mine.wait()
    for unit in units(y, (2,)):
        project(unit)
    for unit in units(1 - y, (0,)):
        project(unit)
    theirs.second_on()
    for n in (3, 4, 5):
        whole(n)
    for unit in units(1 - y, (1, -1)):
        project(unit)
    theirs.wait()
    for unit in units(1 - y, (2,)):
        project(unit)
    for copy in left:
        copy.wait()
    sends.finish()


def start(block, pairs, cid):
    n_send = 1 + 32 + 7
    return pl.pallas_call(
        start_kernel,
        out_shape=[jax.ShapeDtypeStruct((2, 4, 4, 128, D), bf16)] * 3
        + [jax.ShapeDtypeStruct((2, *a.shape), a.dtype) for a in pairs],
        in_specs=[pl.BlockSpec(memory_space=pltpu.HBM)] * 8,
        out_specs=[pl.BlockSpec(memory_space=pltpu.HBM)] * 10,
        scratch_shapes=[pltpu.VMEM((2, 4, 4, 128, D), bf16)]
        + [pltpu.VMEM((2, *a.shape), a.dtype) for a in pairs]
        + [pltpu.VMEM((2, 4, 4, 128, D), bf16)] * 3
        + [
            pltpu.SemaphoreType.DMA((n_send,)),
            pltpu.SemaphoreType.DMA((n_send,)),
            pltpu.SemaphoreType.DMA((8,)),
            pltpu.SemaphoreType.DMA((16 * 3 + 7,)),
        ],
        compiler_params=pltpu.CompilerParams(
            collective_id=cid, has_side_effects=True, vmem_limit_bytes=60 * MIB
        ),
    )(block, *pairs)


ORDERS = (("x", "y", "z"), ("y", "z", "x"), ("z", "x", "y"))
AXES = ("x", "y", "z")
SPLIT = ((192, 192), (48, 48), (32, 16))
CHUNK = ((384, 768), (96, 768), (48, 384))


def tn(a, b):
    return lax.dot_general(a, b, (((0,), (0,)), ((), ())), preferred_element_type=f32)


def reduce_kernel(
    left, right, first, grad_pre, act, grad_down, small, out, small_out,
    acc, twins, pair, t0, t1, t2, u0, u1, u2, cur, slots, send, recv, local,
):
    core = lax.axis_index("wsh")
    twin = 1 - core
    sends = Sends(send, recv)
    tt, uu = (t0, t1, t2), (u0, u1, u2)
    pos = {a: place(a) for a in AXES}
    meet([sibling()] + [away(a, k) for a in AXES for k in (1, 2, 3)])

    def product(s, m, half):
        if s == 0:
            return tn(left[m, :, pl.ds(pl.multiple_of(half * 384, 384), 384)], right[m])
        if s == 1:
            return tn(
                first[:, pl.ds(pl.multiple_of(half * 384, 384), 384)],
                grad_pre[:, pl.ds(pl.multiple_of(m * 768, 768), 768)],
            )
        return tn(
            act[:, pl.ds(pl.multiple_of(half * 1536 + m * 384, 384), 384)], grad_down[...]
        )

    small_pair = sends.start(small.at[twin], slots.at[3, 0], sibling())
    turns = [(s, k) for k in (2, 1, 3, 0) for s in range(3)]
    block = {(s, k): lax.rem(pos[ORDERS[s][0]] + k, 4) for s, k in turns}
    flights = {}
    for s, k in turns:
        m = block[s, k]
        twins[s, m] = product(s, m, twin).astype(bf16)
        flights[s, k] = sends.start(twins.at[s, m], pair.at[s, m], sibling())
    small_pair.wait_recv()
    cur[...] = small[core] + slots[3, 0]

    def own(s, k):
        m = block[s, k]
        mine = product(s, m, core)
        flights[s, k].wait_recv()
        acc[s, m] = (mine + pair[s, m].astype(f32)).astype(bf16)

    def add(dst, dst_at, src, src_at, shape):
        rows, cols = shape

        @pl.loop(0, rows // 16)
        def _(k):
            a = dst_at(pl.multiple_of(k * 16, 16))
            b = src_at(pl.multiple_of(k * 16, 16))
            dst[a] = (dst[a].astype(f32) + src[b].astype(f32)).astype(bf16)

    def region(ph, s, c, r, n):
        a, b, _ = (pos[k] for k in ORDERS[s])
        if ph == 0:
            return (s, c, pl.ds(r, n))
        if ph == 1:
            return (s, a, pl.ds(pl.multiple_of(96 * c + r, 16), n))
        return (
            s, a, pl.ds(pl.multiple_of(96 * b + 48 * (c // 2) + r, 16), n),
            pl.ds(pl.multiple_of(lax.rem(c, 2) * 384, 384), 384),
        )

    for ph in range(3):
        axis = AXES[ph]
        slots[ph, pos[axis]] = cur[...]
        rows, cols = CHUNK[ph]
        near, rest = SPLIT[ph]
        steps = []
        for s in range(3):
            axis_s = ORDERS[s][ph]
            p = pos[axis_s]
            c = lax.rem(p + 2, 4)
            if ph == 0:
                own(s, 2)
            steps.append((
                sends.start(
                    acc.at[region(ph, s, c, 0, near)], tt[ph].at[s, 0, pl.ds(0, near)], away(axis_s, 1)
                ),
                sends.start(
                    acc.at[region(ph, s, c, near, rest)], tt[ph].at[s, 1, pl.ds(0, rest)], away(axis_s, -1)
                ),
            ))
        small_axis = [
            sends.start(cur, slots.at[ph, pos[axis]], away(axis, k)) for k in (1, 2, 3)
        ]
        nexts = []
        for s in range(3):
            axis_s = ORDERS[s][ph]
            p = pos[axis_s]
            up, down = lax.rem(p + 1, 4), lax.rem(p + 3, 4)
            if ph == 0:
                own(s, 1)
            steps[s][0].wait_recv()
            add(
                acc, lambda r, s=s, up=up: region(ph, s, up, r, 16),
                tt[ph], lambda r, s=s: (s, 0, pl.ds(r, 16)), (near, cols),
            )
            a = sends.start(acc.at[region(ph, s, up, 0, rows)], uu[ph].at[s, 0], away(axis_s, 1))
            if ph == 0:
                own(s, 3)
            steps[s][1].wait_recv()
            add(
                acc, lambda r, s=s, down=down: region(ph, s, down, near + r, 16),
                tt[ph], lambda r, s=s: (s, 1, pl.ds(r, 16)), (rest, cols),
            )
            b = sends.start(acc.at[region(ph, s, down, 0, rows)], uu[ph].at[s, 1], away(axis_s, -1))
            nexts.append((a, b))
        if ph == 0:
            for s in range(3):
                own(s, 0)
        for s in range(3):
            p = pos[ORDERS[s][ph]]
            for k in range(2):
                nexts[s][k].wait_recv()
            uk = uu[ph]

            @pl.loop(0, rows // 16)
            def _(k, s=s, p=p, uk=uk):
                r = pl.multiple_of(k * 16, 16)
                a = region(ph, s, p, r, 16)
                acc[a] = (
                    acc[a].astype(f32)
                    + uk[s, 0, pl.ds(r, 16)].astype(f32)
                    + uk[s, 1, pl.ds(r, 16)].astype(f32)
                ).astype(bf16)

        for copy in small_axis:
            copy.wait()
        sends.all = [c for c in sends.all if all(c is not d for d in small_axis)]
        cur[...] = (slots[ph, 0] + slots[ph, 1]) + (slots[ph, 2] + slots[ph, 3])

    small_out[...] = cur[...]

    for ph in (2, 1, 0):
        rows, cols = CHUNK[ph]
        near, rest = SPLIT[ph]
        steps = []
        for s in range(3):
            axis_s = ORDERS[s][ph]
            p = pos[axis_s]
            here = region(ph, s, p, 0, rows)
            if ph == 2:
                kept_copy = pltpu.make_async_copy(acc.at[here], out.at[here], local.at[s])
                kept_copy.start()
                src = acc.at[here]
            else:
                kept_copy = None
                src = out.at[here]
            steps.append((
                sends.start(src, out.at[here], away(axis_s, 1)),
                sends.start(src, out.at[here], away(axis_s, -1)),
                kept_copy,
            ))
        nexts = []
        for s in range(3):
            axis_s = ORDERS[s][ph]
            p = pos[axis_s]
            up, down = lax.rem(p + 1, 4), lax.rem(p + 3, 4)
            steps[s][0].wait_recv()
            part = out.at[region(ph, s, down, 0, near)]
            a = sends.start(part, part, away(axis_s, 1))
            steps[s][1].wait_recv()
            part = out.at[region(ph, s, up, near, rest)]
            b = sends.start(part, part, away(axis_s, -1))
            nexts.append((a, b))
        for s in range(3):
            if steps[s][2] is not None:
                steps[s][2].wait()
            for copy in nexts[s]:
                copy.wait_recv()
    sends.finish()


def reduce_params(left, right, first, grad_pre, act, grad_down, small, cid):
    scratch = [pltpu.VMEM((3, 4, 384, 768), bf16)] * 3
    scratch += [pltpu.VMEM((3, 2, SPLIT[k][0], CHUNK[k][1]), bf16) for k in range(3)]
    scratch += [pltpu.VMEM((3, 2, *CHUNK[k]), bf16) for k in range(3)]
    scratch += [pltpu.VMEM((40, 128), f32), pltpu.VMEM((4, 4, 40, 128), f32)]
    count = 1 + 12 + 9 + 3 * 24
    scratch += [
        pltpu.SemaphoreType.DMA((count,)),
        pltpu.SemaphoreType.DMA((count,)),
        pltpu.SemaphoreType.DMA((3,)),
    ]
    vm = pl.BlockSpec(memory_space=pltpu.VMEM)
    return pl.pallas_call(
        reduce_kernel,
        out_shape=[
            jax.ShapeDtypeStruct((3, 4, 384, 768), bf16),
            jax.ShapeDtypeStruct((40, 128), f32),
        ],
        in_specs=[vm] * 7,
        out_specs=[pl.BlockSpec(memory_space=pltpu.HBM), vm],
        scratch_shapes=scratch,
        compiler_params=pltpu.CompilerParams(
            collective_id=cid, has_side_effects=True, vmem_limit_bytes=60 * MIB
        ),
    )(left, right, first, grad_pre, act, grad_down, small)


def finish_kernel(big_ref, q_ref, k_ref, v_ref, o_ref, up_ref, down_ref):
    for n, ref in enumerate((q_ref, k_ref, v_ref, o_ref)):
        ref[...] = big_ref[0, n].astype(f32)
        up_ref[:, n * 768 : (n + 1) * 768] = big_ref[1, n].astype(f32)
        down_ref[n] = big_ref[2, n].astype(f32)


def finish(big):
    mat = pl.BlockSpec((96, 768), lambda r: (r, 0))
    return pl.pallas_call(
        finish_kernel,
        grid=(4,),
        out_shape=[jax.ShapeDtypeStruct((384, 768), f32)] * 4
        + [
            jax.ShapeDtypeStruct((384, 3072), f32),
            jax.ShapeDtypeStruct((4, 384, 768), f32),
        ],
        in_specs=[pl.BlockSpec((3, 4, 96, 768), lambda r: (0, 0, r, 0))],
        out_specs=[mat] * 4
        + [
            pl.BlockSpec((96, 3072), lambda r: (r, 0)),
            pl.BlockSpec((4, 96, 768), lambda r: (0, r, 0)),
        ],
        compiler_params=pltpu.CompilerParams(vmem_limit_bytes=40 * MIB),
    )(big)


def nt(a, b):
    return lax.dot_general(a, b, (((1,), (1,)), ((), ())), preferred_element_type=f32)


def nn(a, b):
    return jnp.dot(a, b, preferred_element_type=f32)


def stacked(block):
    lane = lax.broadcasted_iota(jnp.int32, block.shape, 1) // HD
    zero = jnp.zeros_like(block)
    return jnp.concatenate([jnp.where(lane == i, block, zero) for i in range(4)], axis=0)


def unstacked(tall):
    n = tall.shape[0] // 4
    lane = lax.broadcasted_iota(jnp.int32, (n, tall.shape[1]), 1) // HD
    total = jnp.where(lane == 0, tall[:n], 0.0)
    for i in range(1, 4):
        total = total + jnp.where(lane == i, tall[i * n : (i + 1) * n], 0.0)
    return total


def as_rows(column):
    wide = jnp.broadcast_to(column, (column.shape[0], 128))
    return jnp.concatenate(
        [wide[i * 128 : (i + 1) * 128].T[:1] for i in range(4)] + [jnp.zeros((4, 128), f32)], axis=0
    )


TILE = 1024


def forward_kernel(q_ref, k_ref, v_ref, bias_ref, attn_ref, lse_ref, rows_ref, score):
    q = stacked(q_ref[...] * jnp.asarray(0.125, bf16))
    top = None
    for t in range(4096 // TILE):
        at = pl.ds(t * TILE, TILE)
        s = nt(q, k_ref[at, :]) + bias_ref[:, at]
        score[:, at] = s
        m = jnp.max(s, axis=-1, keepdims=True)
        top = m if top is None else jnp.maximum(top, m)
    total, out = 0.0, 0.0
    for t in range(4096 // TILE):
        at = pl.ds(t * TILE, TILE)
        p = jnp.exp(score[:, at] - top)
        total = total + jnp.sum(p, axis=-1, keepdims=True)
        out = out + nn(p.astype(bf16), v_ref[at, :])
    attn_ref[...] = unstacked(out * (1.0 / total))
    lse = top + jnp.log(total)
    lse_ref[0] = jnp.broadcast_to(lse, (512, 128))
    rows_ref[0] = as_rows(lse)


def attend(q, k, v, bias):
    wide = pl.BlockSpec((4096, 256), lambda g: (0, g))
    own = pl.BlockSpec((128, 256), lambda g: (0, g))
    return pl.pallas_call(
        forward_kernel,
        grid=(3,),
        out_shape=[
            jax.ShapeDtypeStruct((128, D), f32),
            jax.ShapeDtypeStruct((3, 512, 128), f32),
            jax.ShapeDtypeStruct((3, 8, 128), f32),
        ],
        in_specs=[own, wide, wide, pl.BlockSpec((1, 4096), lambda g: (0, 0))],
        out_specs=[
            own,
            pl.BlockSpec((1, 512, 128), lambda g: (g, 0, 0)),
            pl.BlockSpec((1, 8, 128), lambda g: (g, 0, 0)),
        ],
        scratch_shapes=[pltpu.VMEM((512, 4096), f32)],
        compiler_params=pltpu.CompilerParams(vmem_limit_bytes=56 * MIB),
    )(q, k, v, bias)


def back_kernel(
    q_hbm, k_hbm, v_hbm, g_in, attn_ref, lse_ref, rows_ref, bias_ref, keep_ref,
    dq_ref, dk_ref, dv_ref,
    qv, kv, vv, gv, stats, stat_own, q_own, k_own, v_own, g_own, delta, dq_acc, dk_acc, dv_acc,
    send, recv, local,
):
    sends = Sends(send, recv)
    y, z, x = (lax.axis_index(a) for a in CTX)
    meet([away("x", 1), away("x", -1), away("z", 1), away("z", -1), far()])
    loads = []
    for n, (src, dst) in enumerate(
        ((k_hbm, kv), (v_hbm, vv), (q_hbm, qv))
    ):
        copy = pltpu.make_async_copy(src, dst, local.at[n])
        copy.start()
        loads.append(copy)
    eighth = jnp.asarray(0.125, bf16)
    low = lax.broadcasted_iota(jnp.int32, (4, 128), 1) < 64
    stat_own[...] = jnp.zeros_like(stat_own)
    for n in range(3):
        cols = pl.ds(n * 256, 256)
        g = stacked(g_in[:, cols])
        g_own[n] = g
        tall = jnp.concatenate([attn_ref[:, cols]] * 4, axis=0)
        d = jnp.sum(g.astype(f32) * tall, axis=-1, keepdims=True)
        delta[n] = jnp.broadcast_to(d, (512, 128))
        d = as_rows(d)[:4]
        lse = rows_ref[n][:4]
        stat_own[pl.ds(4 * n, 4), :] = jnp.where(low, lse, pltpu.roll(d, 64, 1))
        stat_own[pl.ds(16 + 4 * n, 4), :] = jnp.where(low, pltpu.roll(lse, 64, 1), d)
        dq_acc[n] = jnp.zeros((512, 256), f32)
        dk_acc[n] = jnp.zeros((512, 256), f32)
        dv_acc[n] = jnp.zeros((512, 256), f32)
    ins, outs = [g_in, stat_own], [gv, stats]
    crossing = [sends.start(i, o.at[y, z, x], far()) for i, o in zip(ins, outs)]
    mine = Flow(sends, ins, outs, y, True)
    theirs = Flow(sends, ins, outs, 1 - y, False)
    mine.first()
    own = []
    for n, (i, o) in enumerate(zip(ins, outs)):
        copy = pltpu.make_async_copy(i, o.at[y, z, x], local.at[3 + n])
        copy.start()
        own.append(copy)
    for copy in loads:
        copy.wait()
    for n in range(3):
        cols = pl.ds(n * 256, 256)
        q_own[n] = stacked(qv[y, z, x, :, cols] * eighth)
        k_own[n] = stacked(kv[y, z, x, :, cols] * eighth)
        v_own[n] = stacked(vv[y, z, x, :, cols])

    def queries(lo, hi):
        @pl.loop(lo, hi)
        def _(c):
            n, t = c // 4, c % 4
            cols = pl.ds(pl.multiple_of(n * 256, 256), 256)
            k = kv[t // 2, pl.ds(2 * (t % 2), 2), :, :, cols].reshape(TILE, 256)
            v = vv[t // 2, pl.ds(2 * (t % 2), 2), :, :, cols].reshape(TILE, 256)
            bias = bias_ref[:, pl.ds(pl.multiple_of(t * TILE, TILE), TILE)]
            p = jnp.exp(nt(q_own[n], k) + bias - lse_ref[n][:, :1])
            dp = nt(g_own[n], v)
            ds = (p * (dp - delta[n][:, :1])).astype(bf16)
            dq_acc[n] = dq_acc[n] + nn(ds, k)

    low16 = lax.broadcasted_iota(jnp.int32, (16, 128), 1) < 64

    def keys(unit):
        half, layer, i = unit
        r = 0 if half == "A" else 64
        if half == "A":
            st = stats[layer, i, :, pl.ds(0, 16)]
        else:
            st = stats[layer, :, i, pl.ds(16, 16)]
        turned = [pltpu.roll(st[b], 64, 1) for b in range(4)]
        lse = jnp.concatenate(
            [jnp.where(low16, st[b], turned[b + 1]) for b in (0, 2)], axis=1
        )
        dlt = jnp.concatenate(
            [jnp.where(low16, turned[b], st[b + 1]) for b in (0, 2)], axis=1
        )
        for n in range(3):
            cols = pl.ds(n * 256, 256)
            if half == "A":
                at = (layer, i, slice(None), pl.ds(0, 64), cols)
            else:
                at = (layer, slice(None), i, pl.ds(64, 64), cols)
            q, g = qv[at].reshape(256, 256), gv[at].reshape(256, 256)

            def spread(rows):
                return jnp.concatenate(
                    [jnp.broadcast_to(rows[4 * n + h : 4 * n + h + 1], (128, 256)) for h in range(4)],
                    axis=0,
                )

            p = jnp.exp(nt(k_own[n], q) - spread(lse))
            ds = (p * (nt(v_own[n], g) - spread(dlt))).astype(bf16)
            dv_acc[n] = dv_acc[n] + nn(p.astype(bf16), g)
            dk_acc[n] = dk_acc[n] + nn(ds, q)

    queries(0, 2)
    mine.first_on()
    for copy in crossing:
        copy.wait_recv()
    theirs.first()
    queries(2, 4)
    for copy in own:
        copy.wait()
    mine.second()
    theirs.first_on()
    queries(4, 8)
    for unit in units(y, (0,)):
        keys(unit)
    mine.second_on()
    theirs.second()
    for unit in units(y, (1, -1)):
        keys(unit)
    queries(8, 12)
    mine.wait()
    for unit in units(y, (2,)):
        keys(unit)
    for unit in units(1 - y, (0,)):
        keys(unit)
    theirs.second_on()
    for n in range(3):
        dq_ref[:, pl.ds(n * 256, 256)] = (unstacked(dq_acc[n]) * 0.125).astype(bf16)
    for unit in units(1 - y, (1, -1)):
        keys(unit)
    theirs.wait()
    for unit in units(1 - y, (2,)):
        keys(unit)
    keep = keep_ref[:, :1] > 0.5
    for n in range(3):
        cols = pl.ds(n * 256, 256)
        dk_ref[:, cols] = jnp.where(keep, unstacked(dk_acc[n]) * 0.125, 0.0).astype(bf16)
        dv_ref[:, cols] = jnp.where(keep, unstacked(dv_acc[n]), 0.0).astype(bf16)
    sends.finish()


def attend_back(q, k, v, g, attn, lse, lse_rows, bias, keep, cid):
    n_send = 33 * 2
    vm = pl.BlockSpec(memory_space=pltpu.VMEM)
    wide = pltpu.VMEM((2, 4, 4, 128, D), bf16)
    tall = pltpu.VMEM((3, 512, 256), bf16)
    sums = pltpu.VMEM((3, 512, 256), f32)
    return pl.pallas_call(
        back_kernel,
        out_shape=[jax.ShapeDtypeStruct((128, D), bf16)] * 3,
        in_specs=[pl.BlockSpec(memory_space=pltpu.HBM)] * 3 + [vm] * 6,
        out_specs=[vm] * 3,
        scratch_shapes=[wide] * 4
        + [pltpu.VMEM((2, 4, 4, 32, 128), f32), pltpu.VMEM((32, 128), f32)]
        + [tall] * 4
        + [pltpu.VMEM((3, 512, 128), f32)]
        + [sums] * 3
        + [
            pltpu.SemaphoreType.DMA((n_send,)),
            pltpu.SemaphoreType.DMA((n_send,)),
            pltpu.SemaphoreType.DMA((5,)),
        ],
        compiler_params=pltpu.CompilerParams(
            collective_id=cid, has_side_effects=True, vmem_limit_bytes=60 * MIB
        ),
    )(q, k, v, g, attn, lse, lse_rows, bias, keep)


def layer_norm(resid, gain, shift):
    centre = resid - jnp.mean(resid, axis=-1, keepdims=True)
    spread = jnp.mean(centre * centre, axis=-1, keepdims=True)
    return centre * lax.rsqrt(spread + 1e-12) * gain + shift


def gelu_exact(value):
    return jax.nn.gelu(value, approximate=False)


def local(
    tokens, lengths, w_query, b_query, w_key, w_value, b_value, w_out, b_out, gain_one, shift_one,
    w_up, b_up, w_down, b_down, gain_two, shift_two, cotangent,
):
    inputs = tokens[0]
    vectors = jnp.stack(
        [b_query, b_value, b_out, gain_one, shift_one, b_down, gain_two, shift_two]
    )
    vectors = jnp.concatenate([vectors, b_up.reshape(4, 384), jnp.zeros((4, 384), bf16)], axis=0)
    all_q, all_k, all_v, *whole = start(
        inputs, [w_query, w_key, w_value, w_out, w_up, w_down, vectors], 0
    )
    wq, wk, wv, wo, wup, wdown = (w.reshape(-1, w.shape[-1]) for w in whole[:6])
    vecs = whole[6].astype(f32)
    bo, gone, sone, bdown, gtwo, stwo = (vecs[:, i].reshape(768) for i in range(2, 8))
    bup = vecs[:, 8:12].reshape(3072)
    seq_len = lengths[0]
    block = (lax.axis_index("ctx_0") * 4 + lax.axis_index("ctx_1")) * 4 + lax.axis_index("ctx_2")
    q = lax.dynamic_slice_in_dim(all_q.reshape(4096, D), block * 128, 128)
    bias = jnp.where(jnp.arange(4096) < seq_len, 0.0, -1e30).astype(f32)[None]
    keep = (jnp.arange(128) + block * 128 < seq_len).astype(f32)
    keep = jnp.broadcast_to(keep[:, None], (128, 128))
    attn, lse, lse_rows = attend(q, all_k.reshape(4096, D), all_v.reshape(4096, D), bias)
    mixed = attn.astype(bf16)
    resid_one = inputs.astype(f32) + jnp.dot(mixed, wo, preferred_element_type=f32) + bo
    first, pull_one = jax.vjp(layer_norm, resid_one, gone, sone)
    first_low = first.astype(bf16)
    pre = jnp.dot(first_low, wup, preferred_element_type=f32) + bup
    act, pull_gelu = jax.vjp(gelu_exact, pre)
    act_low = act.astype(bf16)
    resid_two = first + jnp.dot(act_low, wdown, preferred_element_type=f32) + bdown
    result, pull_two = jax.vjp(layer_norm, resid_two, gtwo, stwo)
    grad_resid_two, grad_gtwo, grad_stwo = pull_two(cotangent[0].astype(f32))
    grad_down_low = grad_resid_two.astype(bf16)
    grad_bdown = jnp.sum(grad_resid_two, axis=0)
    grad_act = jnp.einsum("td,fd->tf", grad_down_low, wdown, preferred_element_type=f32)
    grad_pre_low = pull_gelu(grad_act)[0].astype(bf16)
    grad_bup = jnp.sum(grad_pre_low.astype(f32), axis=0)
    grad_first = grad_resid_two + jnp.einsum(
        "tf,df->td", grad_pre_low, wup, preferred_element_type=f32
    )
    grad_resid_one, grad_gone, grad_sone = pull_one(grad_first)
    grad_branch = grad_resid_one.astype(bf16)
    grad_bout = jnp.sum(grad_resid_one, axis=0)
    grad_mixed = jnp.einsum("te,de->td", grad_branch, wo, preferred_element_type=f32).astype(bf16)
    grad_query_low, grad_keys_low, grad_values_low = attend_back(
        all_q, all_k, all_v, grad_mixed, attn, lse, lse_rows, bias, keep, 1
    )
    lefts = jnp.stack([inputs, inputs, inputs, mixed])
    rights = jnp.stack([grad_query_low, grad_keys_low, grad_values_low, grad_branch])
    grad_bq = jnp.sum(grad_query_low.astype(f32), axis=0)
    grad_bv = jnp.sum(grad_values_low.astype(f32), axis=0)
    grad_inputs = grad_resid_one + jnp.einsum(
        "te,de->td", grad_query_low, wq, preferred_element_type=f32
    )
    grad_inputs = grad_inputs + jnp.einsum(
        "te,de->td", grad_keys_low, wk, preferred_element_type=f32
    )
    grad_inputs = grad_inputs + jnp.einsum(
        "te,de->td", grad_values_low, wv, preferred_element_type=f32
    )
    small = jnp.stack(
        [grad_bq, grad_bv, grad_bout, grad_gone, grad_sone, grad_bdown, grad_gtwo, grad_stwo]
    )
    small = small.reshape(8, 2, 384).transpose(1, 0, 2).reshape(2, 3072)
    small = jnp.concatenate(
        [small, grad_bup.reshape(2, 1536), jnp.zeros((2, 512), f32)], axis=1
    ).reshape(2, 40, 128)
    big, small = reduce_params(
        lefts, rights, first_low, grad_pre_low, act_low, grad_down_low, small, 2
    )
    small = small.reshape(5120)
    tot_bq, tot_bv, tot_bo, tot_gone, tot_sone, tot_bdown, tot_gtwo, tot_stwo = (
        small[i * 384 : (i + 1) * 384] for i in range(8)
    )
    tot_bup = small[3072:4608]
    tot_wq, tot_wk, tot_wv, tot_wo, tot_wup, tot_wdown = finish(big)
    return (
        result.astype(bf16)[None],
        grad_inputs[None],
        tot_wq,
        tot_bq,
        tot_wk,
        tot_wv,
        tot_bv,
        tot_wo,
        tot_bo,
        tot_gone,
        tot_sone,
        tot_wup,
        tot_bup,
        tot_wdown.reshape(1536, 768),
        tot_bdown,
        tot_gtwo,
        tot_stwo,
    )


def solution(mesh):
    split = Mesh(
        mesh.devices.reshape(mesh.shape["seq"], 2, 4, 4, mesh.shape["wsh"]),
        ("seq", "ctx_0", "ctx_1", "ctx_2", "wsh"),
    )
    rows = P(("seq", "wsh"), CTX, None)
    mat, vec = P("wsh", None), P("wsh")
    params = (mat, vec, mat, mat, vec, mat, vec, vec, vec, mat, vec, mat, vec, vec, vec)
    return jax.shard_map(
        local,
        mesh=split,
        in_specs=(rows, P(("seq", "wsh")), *params, rows),
        out_specs=(rows, rows, *params),
        check_vma=False,
    )
```

```python
import functools
import math

import jax
import jax.numpy as jnp
from jax import lax
from jax.experimental import pallas as pl
from jax.experimental.pallas import tpu as pltpu
from jax.sharding import Mesh
from jax.sharding import PartitionSpec as P

H = 12
HD = 64
D = 768
CTX = ("ctx_0", "ctx_1", "ctx_2")
f32 = jnp.float32
bf16 = jnp.bfloat16
MESH = pl.DeviceIdType.MESH
ANY = pl.ANY
MIB = 1024 * 1024


def place(axis):
    if axis == "x":
        return lax.axis_index("ctx_2")
    if axis == "z":
        return lax.axis_index("ctx_1")
    return lax.axis_index("ctx_0") * 2 + lax.axis_index("seq")


def away(axis, step):
    at = lax.rem(place(axis) + step + 4, 4)
    if axis == "x":
        return {"ctx_2": at}
    if axis == "z":
        return {"ctx_1": at}
    return {"ctx_0": at // 2, "seq": lax.rem(at, 2)}


def sibling():
    return {"wsh": 1 - lax.axis_index("wsh")}


def far():
    return {"ctx_0": 1 - lax.axis_index("ctx_0")}


def meet(devices):
    barrier = pltpu.get_barrier_semaphore()
    for d in devices:
        pl.semaphore_signal(barrier, inc=1, device_id=d, device_id_type=MESH)
    pl.semaphore_wait(barrier, len(devices))


class Sends:
    def __init__(self, send, recv):
        self.send, self.recv, self.used, self.all = send, recv, 0, []

    def start(self, src, dst, device):
        k = self.used
        self.used += 1
        copy = pltpu.make_async_remote_copy(
            src_ref=src,
            dst_ref=dst,
            send_sem=self.send.at[k],
            recv_sem=self.recv.at[k],
            device_id=device,
            device_id_type=MESH,
        )
        copy.start()
        self.all.append(copy)
        return copy

    def finish(self):
        for copy in self.all:
            copy.wait_send()


class Flow:
    def __init__(self, sends, ins, outs, layer, mine):
        self.sends, self.ins, self.outs, self.layer, self.mine = sends, ins, outs, layer, mine
        self.z, self.x = lax.axis_index("ctx_1"), lax.axis_index("ctx_2")
        self.flights = []

    def wait(self):
        for pair in self.flights:
            for copy in pair:
                copy.wait_recv()

    def near(self, axis):
        pos = place(axis)
        return lax.rem(pos + 3, 4), lax.rem(pos + 1, 4)

    def first(self):
        y, z, x = self.layer, self.z, self.x
        self.flights = []
        for i, o in zip(self.ins, self.outs):
            h = i.shape[0] // 2
            for axis, lo in (("x", 0), ("z", h)):
                src = i.at[pl.ds(lo, h)] if self.mine else o.at[y, z, x, pl.ds(lo, h)]
                dst = o.at[y, z, x, pl.ds(lo, h)]
                self.flights.append(
                    [self.sends.start(src, dst, away(axis, k)) for k in (1, -1)]
                )

    def first_on(self):
        y, z, x, at, later = self.layer, self.z, self.x, 0, []
        for i, o in zip(self.ins, self.outs):
            q = i.shape[0] // 4
            for axis, lo in (("x", 0), ("z", 2 * q)):
                right, left = self.flights[at]
                at += 1
                before, after = self.near(axis)
                if axis == "x":
                    a = o.at[y, z, before, pl.ds(lo, q)]
                    b = o.at[y, z, after, pl.ds(lo + q, q)]
                else:
                    a = o.at[y, before, x, pl.ds(lo, q)]
                    b = o.at[y, after, x, pl.ds(lo + q, q)]
                right.wait_recv()
                up = self.sends.start(a, a, away(axis, 1))
                left.wait_recv()
                later.append([up, self.sends.start(b, b, away(axis, -1))])
        self.flights = later

    def second(self):
        y, z, x, at, later = self.layer, self.z, self.x, 0, []
        for i, o in zip(self.ins, self.outs):
            h = i.shape[0] // 2
            for axis, lo in (("z", 0), ("x", h)):
                for copy in self.flights[at]:
                    copy.wait_recv()
                at += 1
                a = o.at[y, z, :, pl.ds(lo, h)] if axis == "z" else o.at[y, :, x, pl.ds(lo, h)]
                later.append([self.sends.start(a, a, away(axis, k)) for k in (1, -1)])
        self.flights = later

    def second_on(self):
        y, at, later = self.layer, 0, []
        for i, o in zip(self.ins, self.outs):
            h = i.shape[0] // 2
            for axis, lo in (("z", 0), ("x", h)):
                right, left = self.flights[at]
                at += 1
                before, after = self.near(axis)
                if axis == "z":
                    a = o.at[y, before, pl.ds(0, 2), pl.ds(lo, h)]
                    b = o.at[y, after, pl.ds(2, 2), pl.ds(lo, h)]
                else:
                    a = o.at[y, pl.ds(0, 2), before, pl.ds(lo, h)]
                    b = o.at[y, pl.ds(2, 2), after, pl.ds(lo, h)]
                right.wait_recv()
                up = self.sends.start(a, a, away(axis, 1))
                left.wait_recv()
                later.append([up, self.sends.start(b, b, away(axis, -1))])
        self.flights = later


def units(layer, steps):
    z, x = lax.axis_index("ctx_1"), lax.axis_index("ctx_2")
    picked = []
    for k in steps:
        picked.append(("A", layer, lax.rem(z + k + 4, 4)))
        picked.append(("B", layer, lax.rem(x + k + 4, 4)))
    return picked


def unit_at(unit):
    half, layer, i = unit
    if half == "A":
        return (layer, i, slice(None), pl.ds(0, 64))
    return (layer, slice(None), i, pl.ds(64, 64))


def start_kernel(*refs):
    x_in, pair_ins = refs[0], refs[1:8]
    outs, pair_outs, q_out = refs[8:11], refs[11:18], refs[18]
    xs, held, made = refs[19], refs[20:27], refs[27:30]
    send, recv, local, leave = refs[30:]
    sends = Sends(send, recv)
    y, z, x = (lax.axis_index(a) for a in CTX)
    core = lax.axis_index("wsh")
    meet(
        [away("x", 1), away("x", -1), away("z", 1), away("z", -1), far(), sibling()]
    )
    crossing = sends.start(x_in, xs.at[y, z, x], far())
    mine = Flow(sends, [x_in], [xs], y, True)
    theirs = Flow(sends, [x_in], [xs], 1 - y, False)
    mine.first()
    own = pltpu.make_async_copy(x_in, xs.at[y, z, x], local.at[7])
    own.start()
    pairs, kept, left = [], [], []
    for n, (i, o) in enumerate(zip(pair_ins, held)):
        pairs.append(sends.start(i, o.at[core], sibling()))
        copy = pltpu.make_async_copy(i, o.at[core], local.at[n])
        copy.start()
        kept.append(copy)

    def depart(src, dst):
        copy = pltpu.make_async_copy(src, dst, leave.at[len(left)])
        copy.start()
        left.append(copy)

    def whole(n):
        kept[n].wait()
        pairs[n].wait_recv()
        depart(held[n], pair_outs[n])

    def project(unit):
        at = unit_at(unit)
        block = xs[at].reshape(256, D)
        for n, row in ((0, 0), (1, None), (2, 1)):
            value = nn(block, held[n][...].reshape(D, D))
            if row is not None:
                value = value + jnp.concatenate(
                    [held[6][c, row : row + 1] for c in range(2)], axis=1
                ).astype(f32)
            made[n][at] = value.astype(bf16).reshape(4, 64, D)
            depart(made[n].at[at], outs[n].at[at])

    mine.first_on()
    crossing.wait_recv()
    theirs.first()
    own.wait()
    mine.second()
    theirs.first_on()
    for n in (6, 0, 1, 2):
        whole(n)
    for unit in units(y, (0,)):
        project(unit)
    mine.second_on()
    theirs.second()
    for unit in units(y, (1, -1)):
        project(unit)
    mine.wait()
    for unit in units(y, (2,)):
        project(unit)
    for unit in units(1 - y, (0,)):
        project(unit)
    theirs.second_on()
    for n in (3, 4, 5):
        whole(n)
    for unit in units(1 - y, (1, -1)):
        project(unit)
    theirs.wait()
    for unit in units(1 - y, (2,)):
        project(unit)
    depart(made[0].at[y, z, x], q_out)
    for copy in left:
        copy.wait()
    sends.finish()


def start(block, pairs, cid):
    n_send = 1 + 32 + 7
    return pl.pallas_call(
        start_kernel,
        out_shape=[jax.ShapeDtypeStruct((2, 4, 4, 128, D), bf16)] * 3
        + [jax.ShapeDtypeStruct((2, *a.shape), a.dtype) for a in pairs]
        + [jax.ShapeDtypeStruct((128, D), bf16)],
        in_specs=[pl.BlockSpec(memory_space=pltpu.HBM)] * 8,
        out_specs=[pl.BlockSpec(memory_space=pltpu.HBM)] * 11,
        scratch_shapes=[pltpu.VMEM((2, 4, 4, 128, D), bf16)]
        + [pltpu.VMEM((2, *a.shape), a.dtype) for a in pairs]
        + [pltpu.VMEM((2, 4, 4, 128, D), bf16)] * 3
        + [
            pltpu.SemaphoreType.DMA((n_send,)),
            pltpu.SemaphoreType.DMA((n_send,)),
            pltpu.SemaphoreType.DMA((8,)),
            pltpu.SemaphoreType.DMA((16 * 3 + 8,)),
        ],
        compiler_params=pltpu.CompilerParams(
            collective_id=cid, has_side_effects=True, vmem_limit_bytes=60 * MIB
        ),
    )(block, *pairs)


ORDERS = (("x", "y", "z"), ("y", "z", "x"), ("z", "x", "y"))
AXES = ("x", "y", "z")
SPLIT = ((192, 192), (48, 48), (32, 16))
CHUNK = ((384, 768), (96, 768), (48, 384))


def tn(a, b):
    return lax.dot_general(a, b, (((0,), (0,)), ((), ())), preferred_element_type=f32)


def reduce_kernel(
    x_ref, mixed_ref, dq_ref, dk_ref, dv_ref, branch_ref, resid_ref, wq, wk, wv,
    first, grad_pre, act, grad_down, small_in, out, small_out, token_out,
    left, right, small, acc, twins, pair, t0, t1, t2, u0, u1, u2, cur, slots, send, recv, local,
):
    core = lax.axis_index("wsh")
    twin = 1 - core
    sends = Sends(send, recv)
    tt, uu = (t0, t1, t2), (u0, u1, u2)
    pos = {a: place(a) for a in AXES}
    meet([sibling()] + [away(a, k) for a in AXES for k in (1, 2, 3)])

    def product(s, m, half):
        if s == 0:
            return tn(left[m, :, pl.ds(pl.multiple_of(half * 384, 384), 384)], right[m])
        if s == 1:
            return tn(
                first[:, pl.ds(pl.multiple_of(half * 384, 384), 384)],
                grad_pre[:, pl.ds(pl.multiple_of(m * 768, 768), 768)],
            )
        return tn(
            act[:, pl.ds(pl.multiple_of(half * 1536 + m * 384, 384), 384)], grad_down[...]
        )

    for m in range(4):
        left[m] = (mixed_ref if m == 3 else x_ref)[...]
        right[m] = (dq_ref, dk_ref, dv_ref, branch_ref)[m][...]
    small[...] = small_in[...]
    for n, ref in enumerate((dq_ref, dv_ref)):
        sums = jnp.sum(ref[...].astype(f32), axis=0, keepdims=True)
        for c in range(2):
            small[c, n : n + 1, :] = sums[:, c * 384 : (c + 1) * 384]
    small_pair = sends.start(small.at[twin], slots.at[3, 0], sibling())
    turns = [(s, k) for k in (2, 1, 3, 0) for s in range(3)]
    block = {(s, k): lax.rem(pos[ORDERS[s][0]] + k, 4) for s, k in turns}
    flights = {}
    for s, k in turns:
        m = block[s, k]
        twins[s, m] = product(s, m, twin).astype(bf16)
        flights[s, k] = sends.start(twins.at[s, m], pair.at[s, m], sibling())
    small_pair.wait_recv()
    cur[...] = small[core] + slots[3, 0]

    def own(s, k):
        m = block[s, k]
        mine = product(s, m, core)
        flights[s, k].wait_recv()
        acc[s, m] = (mine + pair[s, m].astype(f32)).astype(bf16)

    def add(dst, dst_at, src, src_at, shape):
        rows, cols = shape

        @pl.loop(0, rows // 16)
        def _(k):
            a = dst_at(pl.multiple_of(k * 16, 16))
            b = src_at(pl.multiple_of(k * 16, 16))
            dst[a] = (dst[a].astype(f32) + src[b].astype(f32)).astype(bf16)

    def region(ph, s, c, r, n):
        a, b, _ = (pos[k] for k in ORDERS[s])
        if ph == 0:
            return (s, c, pl.ds(r, n))
        if ph == 1:
            return (s, a, pl.ds(pl.multiple_of(96 * c + r, 16), n))
        return (
            s, a, pl.ds(pl.multiple_of(96 * b + 48 * (c // 2) + r, 16), n),
            pl.ds(pl.multiple_of(lax.rem(c, 2) * 384, 384), 384),
        )

    for ph in range(3):
        axis = AXES[ph]
        slots[ph, pos[axis]] = cur[...]
        rows, cols = CHUNK[ph]
        near, rest = SPLIT[ph]
        steps = []
        for s in range(3):
            axis_s = ORDERS[s][ph]
            p = pos[axis_s]
            c = lax.rem(p + 2, 4)
            if ph == 0:
                own(s, 2)
            steps.append((
                sends.start(
                    acc.at[region(ph, s, c, 0, near)], tt[ph].at[s, 0, pl.ds(0, near)], away(axis_s, 1)
                ),
                sends.start(
                    acc.at[region(ph, s, c, near, rest)], tt[ph].at[s, 1, pl.ds(0, rest)], away(axis_s, -1)
                ),
            ))
        small_axis = [
            sends.start(cur, slots.at[ph, pos[axis]], away(axis, k)) for k in (1, 2, 3)
        ]
        nexts = []
        for s in range(3):
            axis_s = ORDERS[s][ph]
            p = pos[axis_s]
            up, down = lax.rem(p + 1, 4), lax.rem(p + 3, 4)
            if ph == 0:
                own(s, 1)
            steps[s][0].wait_recv()
            add(
                acc, lambda r, s=s, up=up: region(ph, s, up, r, 16),
                tt[ph], lambda r, s=s: (s, 0, pl.ds(r, 16)), (near, cols),
            )
            a = sends.start(acc.at[region(ph, s, up, 0, rows)], uu[ph].at[s, 0], away(axis_s, 1))
            if ph == 0:
                own(s, 3)
            steps[s][1].wait_recv()
            add(
                acc, lambda r, s=s, down=down: region(ph, s, down, near + r, 16),
                tt[ph], lambda r, s=s: (s, 1, pl.ds(r, 16)), (rest, cols),
            )
            b = sends.start(acc.at[region(ph, s, down, 0, rows)], uu[ph].at[s, 1], away(axis_s, -1))
            nexts.append((a, b))
        if ph == 0:
            for s in range(3):
                own(s, 0)
            token_out[...] = (
                resid_ref[...]
                + nt(dq_ref[...], wq[...].reshape(D, D))
                + nt(dk_ref[...], wk[...].reshape(D, D))
                + nt(dv_ref[...], wv[...].reshape(D, D))
            )
        for s in range(3):
            p = pos[ORDERS[s][ph]]
            for k in range(2):
                nexts[s][k].wait_recv()
            uk = uu[ph]

            @pl.loop(0, rows // 16)
            def _(k, s=s, p=p, uk=uk):
                r = pl.multiple_of(k * 16, 16)
                a = region(ph, s, p, r, 16)
                acc[a] = (
                    acc[a].astype(f32)
                    + uk[s, 0, pl.ds(r, 16)].astype(f32)
                    + uk[s, 1, pl.ds(r, 16)].astype(f32)
                ).astype(bf16)

        for copy in small_axis:
            copy.wait()
        sends.all = [c for c in sends.all if all(c is not d for d in small_axis)]
        cur[...] = (slots[ph, 0] + slots[ph, 1]) + (slots[ph, 2] + slots[ph, 3])

    small_out[...] = cur[...]

    for ph in (2, 1, 0):
        rows, cols = CHUNK[ph]
        near, rest = SPLIT[ph]
        steps = []
        for s in range(3):
            axis_s = ORDERS[s][ph]
            p = pos[axis_s]
            here = region(ph, s, p, 0, rows)
            if ph == 2:
                kept_copy = pltpu.make_async_copy(acc.at[here], out.at[here], local.at[s])
                kept_copy.start()
                src = acc.at[here]
            else:
                kept_copy = None
                src = out.at[here]
            steps.append((
                sends.start(src, out.at[here], away(axis_s, 1)),
                sends.start(src, out.at[here], away(axis_s, -1)),
                kept_copy,
            ))
        nexts = []
        for s in range(3):
            axis_s = ORDERS[s][ph]
            p = pos[axis_s]
            up, down = lax.rem(p + 1, 4), lax.rem(p + 3, 4)
            steps[s][0].wait_recv()
            part = out.at[region(ph, s, down, 0, near)]
            a = sends.start(part, part, away(axis_s, 1))
            steps[s][1].wait_recv()
            part = out.at[region(ph, s, up, near, rest)]
            b = sends.start(part, part, away(axis_s, -1))
            nexts.append((a, b))
        for s in range(3):
            if steps[s][2] is not None:
                steps[s][2].wait()
            for copy in nexts[s]:
                copy.wait_recv()
    sends.finish()


def reduce_params(arrays, cid):
    scratch = [pltpu.VMEM((4, 128, D), bf16)] * 2 + [pltpu.VMEM((2, 16, 384), f32)]
    scratch += [pltpu.VMEM((3, 4, 384, 768), bf16)] * 3
    scratch += [pltpu.VMEM((3, 2, SPLIT[k][0], CHUNK[k][1]), bf16) for k in range(3)]
    scratch += [pltpu.VMEM((3, 2, *CHUNK[k]), bf16) for k in range(3)]
    scratch += [pltpu.VMEM((16, 384), f32), pltpu.VMEM((4, 4, 16, 384), f32)]
    count = 1 + 12 + 9 + 3 * 24
    scratch += [
        pltpu.SemaphoreType.DMA((count,)),
        pltpu.SemaphoreType.DMA((count,)),
        pltpu.SemaphoreType.DMA((3,)),
    ]
    vm = pl.BlockSpec(memory_space=pltpu.VMEM)
    return pl.pallas_call(
        reduce_kernel,
        out_shape=[
            jax.ShapeDtypeStruct((3, 4, 384, 768), bf16),
            jax.ShapeDtypeStruct((16, 384), f32),
            jax.ShapeDtypeStruct((128, D), f32),
        ],
        in_specs=[vm] * 15,
        out_specs=[pl.BlockSpec(memory_space=pltpu.HBM), vm, vm],
        scratch_shapes=scratch,
        compiler_params=pltpu.CompilerParams(
            collective_id=cid, has_side_effects=True, vmem_limit_bytes=60 * MIB
        ),
    )(*arrays)


def finish_kernel(big_ref, q_ref, k_ref, v_ref, o_ref, up_ref, down_ref):
    for n, ref in enumerate((q_ref, k_ref, v_ref, o_ref)):
        ref[...] = big_ref[0, n].astype(f32)
        up_ref[:, n * 768 : (n + 1) * 768] = big_ref[1, n].astype(f32)
        down_ref[n] = big_ref[2, n].astype(f32)


def finish(big):
    mat = pl.BlockSpec((96, 768), lambda r: (r, 0))
    return pl.pallas_call(
        finish_kernel,
        grid=(4,),
        out_shape=[jax.ShapeDtypeStruct((384, 768), f32)] * 4
        + [
            jax.ShapeDtypeStruct((384, 3072), f32),
            jax.ShapeDtypeStruct((4, 384, 768), f32),
        ],
        in_specs=[pl.BlockSpec((3, 4, 96, 768), lambda r: (0, 0, r, 0))],
        out_specs=[mat] * 4
        + [
            pl.BlockSpec((96, 3072), lambda r: (r, 0)),
            pl.BlockSpec((4, 96, 768), lambda r: (0, r, 0)),
        ],
        compiler_params=pltpu.CompilerParams(vmem_limit_bytes=40 * MIB),
    )(big)


def nt(a, b):
    return lax.dot_general(a, b, (((1,), (1,)), ((), ())), preferred_element_type=f32)


def nn(a, b):
    return jnp.dot(a, b, preferred_element_type=f32)


def stacked(block):
    lane = lax.broadcasted_iota(jnp.int32, block.shape, 1) // HD
    zero = jnp.zeros_like(block)
    return jnp.concatenate([jnp.where(lane == i, block, zero) for i in range(4)], axis=0)


def unstacked(tall):
    n = tall.shape[0] // 4
    lane = lax.broadcasted_iota(jnp.int32, (n, tall.shape[1]), 1) // HD
    total = jnp.where(lane == 0, tall[:n], 0.0)
    for i in range(1, 4):
        total = total + jnp.where(lane == i, tall[i * n : (i + 1) * n], 0.0)
    return total


def as_rows(column):
    wide = jnp.broadcast_to(column, (column.shape[0], 128))
    return jnp.concatenate(
        [wide[i * 128 : (i + 1) * 128].T[:1] for i in range(4)] + [jnp.zeros((4, 128), f32)], axis=0
    )


TILE = 1024


def forward_kernel(q_ref, k_ref, v_ref, bias_ref, attn_ref, lse_ref, rows_ref, score):
    q = stacked(q_ref[...] * jnp.asarray(0.125, bf16))
    top = None
    for t in range(4096 // TILE):
        at = pl.ds(t * TILE, TILE)
        s = nt(q, k_ref[at, :]) + bias_ref[:, at]
        score[:, at] = s
        m = jnp.max(s, axis=-1, keepdims=True)
        top = m if top is None else jnp.maximum(top, m)
    total, out = 0.0, 0.0
    for t in range(4096 // TILE):
        at = pl.ds(t * TILE, TILE)
        p = jnp.exp(score[:, at] - top)
        total = total + jnp.sum(p, axis=-1, keepdims=True)
        out = out + nn(p.astype(bf16), v_ref[at, :])
    attn_ref[...] = unstacked(out * (1.0 / total))
    lse = top + jnp.log(total)
    lse_ref[0] = jnp.broadcast_to(lse, (512, 128))
    rows_ref[0] = as_rows(lse)


def attend(q, k, v, bias):
    wide = pl.BlockSpec((4096, 256), lambda g: (0, g))
    own = pl.BlockSpec((128, 256), lambda g: (0, g))
    return pl.pallas_call(
        forward_kernel,
        grid=(3,),
        out_shape=[
            jax.ShapeDtypeStruct((128, D), f32),
            jax.ShapeDtypeStruct((3, 512, 128), f32),
            jax.ShapeDtypeStruct((3, 8, 128), f32),
        ],
        in_specs=[own, wide, wide, pl.BlockSpec((1, 4096), lambda g: (0, 0))],
        out_specs=[
            own,
            pl.BlockSpec((1, 512, 128), lambda g: (g, 0, 0)),
            pl.BlockSpec((1, 8, 128), lambda g: (g, 0, 0)),
        ],
        scratch_shapes=[pltpu.VMEM((512, 4096), f32)],
        compiler_params=pltpu.CompilerParams(vmem_limit_bytes=56 * MIB),
    )(q, k, v, bias)


FC = 768


def norm_parts(resid):
    centre = resid - jnp.mean(resid, axis=-1, keepdims=True)
    spread = jnp.mean(centre * centre, axis=-1, keepdims=True)
    scale = lax.rsqrt(spread + 1e-12)
    return centre * scale, scale


def norm_back(grad, norm, scale):
    return scale * (
        grad
        - jnp.mean(grad, axis=-1, keepdims=True)
        - norm * jnp.mean(grad * norm, axis=-1, keepdims=True)
    )


def middle_kernel(
    attn_ref, x_ref, cot_ref, vec_ref, wo_hbm, wup_hbm, wdown_hbm,
    result_ref, resid_ref, mixed_grad_ref, mixed_ref, first_ref, act_ref, pre_grad_ref,
    down_grad_ref, branch_ref, small_ref,
    wo, wup, wdown, slope, arrive,
):
    copies = []
    for n, (src, dst) in enumerate(((wo_hbm, wo), (wup_hbm, wup), (wdown_hbm, wdown))):
        copy = pltpu.make_async_copy(src, dst, arrive.at[n])
        copy.start()
        copies.append(copy)

    def row(i):
        return jnp.concatenate([vec_ref[c, i : i + 1] for c in range(2)], axis=1).astype(f32)

    def put(i, value):
        for c in range(2):
            small_ref[c, i : i + 1, :] = value[:, c * 384 : (c + 1) * 384]

    def down(value):
        return jnp.sum(value, axis=0, keepdims=True)

    mixed = attn_ref[...].astype(bf16)
    mixed_ref[...] = mixed
    copies[0].wait()
    resid = x_ref[...].astype(f32) + nn(mixed, wo[...].reshape(D, D)) + row(2)
    norm_one, scale_one = norm_parts(resid)
    gain_one = row(3)
    first = norm_one * gain_one + row(4)
    first_low = first.astype(bf16)
    first_ref[...] = first_low
    copies[1].wait()
    copies[2].wait()
    total = first + row(5)
    for j in range(4):
        cols = slice(j * FC, (j + 1) * FC)
        bias = jnp.concatenate(
            [vec_ref[j // 2, 8 + 2 * (j % 2) + k : 9 + 2 * (j % 2) + k] for k in range(2)], axis=1
        ).astype(f32)
        pre = nn(first_low, wup[:, :, cols].reshape(D, FC)) + bias
        phi = 0.5 * (1.0 + lax.erf(pre * (0.5**0.5)))
        slope[:, cols] = phi + pre * jnp.exp(-0.5 * pre * pre) * (1.0 / math.sqrt(2.0 * math.pi))
        act = (pre * phi).astype(bf16)
        act_ref[:, cols] = act
        total = total + nn(act, wdown[j // 2, (j % 2) * FC : (j % 2 + 1) * FC, :])
    norm_two, scale_two = norm_parts(total)
    gain_two = row(6)
    result_ref[...] = (norm_two * gain_two + row(7)).astype(bf16)
    cot = cot_ref[...].astype(f32)
    put(6, down(cot * norm_two))
    put(7, down(cot))
    grad_two = norm_back(cot * gain_two, norm_two, scale_two)
    put(5, down(grad_two))
    grad_down = grad_two.astype(bf16)
    down_grad_ref[...] = grad_down
    grad_first = grad_two
    for j in range(4):
        cols = slice(j * FC, (j + 1) * FC)
        grad_act = nt(grad_down, wdown[j // 2, (j % 2) * FC : (j % 2 + 1) * FC, :])
        grad_pre = (grad_act * slope[:, cols]).astype(bf16)
        pre_grad_ref[:, cols] = grad_pre
        sums = down(grad_pre.astype(f32))
        for k in range(2):
            i = 8 + 2 * (j % 2) + k
            small_ref[j // 2, i : i + 1, :] = sums[:, k * 384 : (k + 1) * 384]
        grad_first = grad_first + nt(grad_pre, wup[:, :, cols].reshape(D, FC))
    put(3, down(grad_first * norm_one))
    put(4, down(grad_first))
    grad_one = norm_back(grad_first * gain_one, norm_one, scale_one)
    resid_ref[...] = grad_one
    put(2, down(grad_one))
    branch = grad_one.astype(bf16)
    branch_ref[...] = branch
    mixed_grad_ref[...] = nt(branch, wo[...].reshape(D, D)).astype(bf16)
    zero = jnp.zeros((1, D), f32)
    put(0, zero)
    put(1, zero)
    for c in range(2):
        small_ref[c, 12:16, :] = jnp.zeros((4, 384), f32)


def middle(attn, x, cot, vecs, wo, wup, wdown):
    vm = pl.BlockSpec(memory_space=pltpu.VMEM)
    hbm = pl.BlockSpec(memory_space=pltpu.HBM)
    thin, wide = jax.ShapeDtypeStruct((128, D), bf16), jax.ShapeDtypeStruct((128, 3072), bf16)
    return pl.pallas_call(
        middle_kernel,
        out_shape=[
            thin, jax.ShapeDtypeStruct((128, D), f32), thin, thin, thin, wide, wide, thin, thin,
            jax.ShapeDtypeStruct((2, 16, 384), f32),
        ],
        in_specs=[vm] * 4 + [hbm] * 3,
        out_specs=[vm] * 10,
        scratch_shapes=[
            pltpu.VMEM(wo.shape, bf16),
            pltpu.VMEM(wup.shape, bf16),
            pltpu.VMEM(wdown.shape, bf16),
            pltpu.VMEM((128, 3072), f32),
            pltpu.SemaphoreType.DMA((3,)),
        ],
        compiler_params=pltpu.CompilerParams(vmem_limit_bytes=48 * MIB),
    )(attn, x, cot, vecs, wo, wup, wdown)


def back_kernel(
    q_hbm, k_hbm, v_hbm, g_in, attn_ref, lse_ref, rows_ref, bias_ref,
    dq_ref, dk_ref, dv_ref,
    qv, kv, vv, gv, stats, stat_own, q_own, k_own, v_own, g_own, delta, dq_acc, dk_acc, dv_acc,
    send, recv, local,
):
    sends = Sends(send, recv)
    y, z, x = (lax.axis_index(a) for a in CTX)
    meet([away("x", 1), away("x", -1), away("z", 1), away("z", -1), far()])
    loads = []
    for n, (src, dst) in enumerate(
        ((k_hbm, kv), (v_hbm, vv), (q_hbm, qv))
    ):
        copy = pltpu.make_async_copy(src, dst, local.at[n])
        copy.start()
        loads.append(copy)
    eighth = jnp.asarray(0.125, bf16)
    low = lax.broadcasted_iota(jnp.int32, (4, 128), 1) < 64
    stat_own[...] = jnp.zeros_like(stat_own)
    for n in range(3):
        cols = pl.ds(n * 256, 256)
        g = stacked(g_in[:, cols])
        g_own[n] = g
        tall = jnp.concatenate([attn_ref[:, cols]] * 4, axis=0)
        d = jnp.sum(g.astype(f32) * tall, axis=-1, keepdims=True)
        delta[n] = jnp.broadcast_to(d, (512, 128))
        d = as_rows(d)[:4]
        lse = rows_ref[n][:4]
        stat_own[pl.ds(4 * n, 4), :] = jnp.where(low, lse, pltpu.roll(d, 64, 1))
        stat_own[pl.ds(16 + 4 * n, 4), :] = jnp.where(low, pltpu.roll(lse, 64, 1), d)
        dq_acc[n] = jnp.zeros((512, 256), f32)
        dk_acc[n] = jnp.zeros((512, 256), f32)
        dv_acc[n] = jnp.zeros((512, 256), f32)
    ins, outs = [g_in, stat_own], [gv, stats]
    crossing = [sends.start(i, o.at[y, z, x], far()) for i, o in zip(ins, outs)]
    mine = Flow(sends, ins, outs, y, True)
    theirs = Flow(sends, ins, outs, 1 - y, False)
    mine.first()
    own = []
    for n, (i, o) in enumerate(zip(ins, outs)):
        copy = pltpu.make_async_copy(i, o.at[y, z, x], local.at[3 + n])
        copy.start()
        own.append(copy)
    for copy in loads:
        copy.wait()
    for n in range(3):
        cols = pl.ds(n * 256, 256)
        q_own[n] = stacked(qv[y, z, x, :, cols] * eighth)
        k_own[n] = stacked(kv[y, z, x, :, cols] * eighth)
        v_own[n] = stacked(vv[y, z, x, :, cols])

    def queries(lo, hi):
        @pl.loop(lo, hi)
        def _(c):
            n, t = c // 4, c % 4
            cols = pl.ds(pl.multiple_of(n * 256, 256), 256)
            k = kv[t // 2, pl.ds(2 * (t % 2), 2), :, :, cols].reshape(TILE, 256)
            v = vv[t // 2, pl.ds(2 * (t % 2), 2), :, :, cols].reshape(TILE, 256)
            bias = bias_ref[:, pl.ds(pl.multiple_of(t * TILE, TILE), TILE)]
            p = jnp.exp(nt(q_own[n], k) + bias - lse_ref[n][:, :1])
            dp = nt(g_own[n], v)
            ds = (p * (dp - delta[n][:, :1])).astype(bf16)
            dq_acc[n] = dq_acc[n] + nn(ds, k)

    low16 = lax.broadcasted_iota(jnp.int32, (16, 128), 1) < 64

    def keys(unit):
        half, layer, i = unit
        r = 0 if half == "A" else 64
        if half == "A":
            st = stats[layer, i, :, pl.ds(0, 16)]
        else:
            st = stats[layer, :, i, pl.ds(16, 16)]
        turned = [pltpu.roll(st[b], 64, 1) for b in range(4)]
        lse = jnp.concatenate(
            [jnp.where(low16, st[b], turned[b + 1]) for b in (0, 2)], axis=1
        )
        dlt = jnp.concatenate(
            [jnp.where(low16, turned[b], st[b + 1]) for b in (0, 2)], axis=1
        )
        for n in range(3):
            cols = pl.ds(n * 256, 256)
            if half == "A":
                at = (layer, i, slice(None), pl.ds(0, 64), cols)
            else:
                at = (layer, slice(None), i, pl.ds(64, 64), cols)
            q, g = qv[at].reshape(256, 256), gv[at].reshape(256, 256)

            def spread(rows):
                return jnp.concatenate(
                    [jnp.broadcast_to(rows[4 * n + h : 4 * n + h + 1], (128, 256)) for h in range(4)],
                    axis=0,
                )

            p = jnp.exp(nt(k_own[n], q) - spread(lse))
            ds = (p * (nt(v_own[n], g) - spread(dlt))).astype(bf16)
            dv_acc[n] = dv_acc[n] + nn(p.astype(bf16), g)
            dk_acc[n] = dk_acc[n] + nn(ds, q)

    queries(0, 2)
    mine.first_on()
    for copy in crossing:
        copy.wait_recv()
    theirs.first()
    queries(2, 4)
    for copy in own:
        copy.wait()
    mine.second()
    theirs.first_on()
    queries(4, 8)
    for unit in units(y, (0,)):
        keys(unit)
    mine.second_on()
    theirs.second()
    for unit in units(y, (1, -1)):
        keys(unit)
    queries(8, 12)
    mine.wait()
    for unit in units(y, (2,)):
        keys(unit)
    for unit in units(1 - y, (0,)):
        keys(unit)
    theirs.second_on()
    for n in range(3):
        dq_ref[:, pl.ds(n * 256, 256)] = (unstacked(dq_acc[n]) * 0.125).astype(bf16)
    for unit in units(1 - y, (1, -1)):
        keys(unit)
    theirs.wait()
    for unit in units(1 - y, (2,)):
        keys(unit)
    at = pl.multiple_of(((y * 4 + z) * 4 + x) * 128, 128)
    keep = jnp.broadcast_to(bias_ref[:, pl.ds(at, 128)], (128, 128)).T[:, :1] > -1.0
    for n in range(3):
        cols = pl.ds(n * 256, 256)
        dk_ref[:, cols] = jnp.where(keep, unstacked(dk_acc[n]) * 0.125, 0.0).astype(bf16)
        dv_ref[:, cols] = jnp.where(keep, unstacked(dv_acc[n]), 0.0).astype(bf16)
    sends.finish()


def attend_back(q, k, v, g, attn, lse, lse_rows, bias, cid):
    n_send = 33 * 2
    vm = pl.BlockSpec(memory_space=pltpu.VMEM)
    wide = pltpu.VMEM((2, 4, 4, 128, D), bf16)
    tall = pltpu.VMEM((3, 512, 256), bf16)
    sums = pltpu.VMEM((3, 512, 256), f32)
    return pl.pallas_call(
        back_kernel,
        out_shape=[jax.ShapeDtypeStruct((128, D), bf16)] * 3,
        in_specs=[pl.BlockSpec(memory_space=pltpu.HBM)] * 3 + [vm] * 5,
        out_specs=[vm] * 3,
        scratch_shapes=[wide] * 4
        + [pltpu.VMEM((2, 4, 4, 32, 128), f32), pltpu.VMEM((32, 128), f32)]
        + [tall] * 4
        + [pltpu.VMEM((3, 512, 128), f32)]
        + [sums] * 3
        + [
            pltpu.SemaphoreType.DMA((n_send,)),
            pltpu.SemaphoreType.DMA((n_send,)),
            pltpu.SemaphoreType.DMA((5,)),
        ],
        compiler_params=pltpu.CompilerParams(
            collective_id=cid, has_side_effects=True, vmem_limit_bytes=60 * MIB
        ),
    )(q, k, v, g, attn, lse, lse_rows, bias)


def local(
    tokens, lengths, w_query, b_query, w_key, w_value, b_value, w_out, b_out, gain_one, shift_one,
    w_up, b_up, w_down, b_down, gain_two, shift_two, cotangent,
):
    inputs = tokens[0]
    vectors = jnp.concatenate(
        [b_query, b_value, b_out, gain_one, shift_one, b_down, gain_two, shift_two, b_up]
        + [jnp.zeros((1536,), bf16)]
    ).reshape(16, 384)
    all_q, all_k, all_v, wq, wk, wv, wo, wup, wdown, vecs, q = start(
        inputs, [w_query, w_key, w_value, w_out, w_up, w_down, vectors], 0
    )
    bias = jnp.where(jnp.arange(4096) < lengths[0], 0.0, -1e30).astype(f32)[None]
    attn, lse, lse_rows = attend(q, all_k.reshape(4096, D), all_v.reshape(4096, D), bias)
    (
        result, grad_resid, grad_mixed, mixed, first, act, grad_pre, grad_down, branch, small
    ) = middle(attn, inputs, cotangent[0], vecs, wo, wup, wdown)
    dq, dk, dv = attend_back(all_q, all_k, all_v, grad_mixed, attn, lse, lse_rows, bias, 1)
    big, small, grad_inputs = reduce_params(
        [
            inputs, mixed, dq, dk, dv, branch, grad_resid, wq, wk, wv,
            first, grad_pre, act, grad_down, small,
        ],
        2,
    )
    tot_wq, tot_wk, tot_wv, tot_wo, tot_wup, tot_wdown = finish(big)
    tot_bq, tot_bv, tot_bo, tot_gone, tot_sone, tot_bdown, tot_gtwo, tot_stwo = (
        small[i] for i in range(8)
    )
    return (
        result[None],
        grad_inputs[None],
        tot_wq,
        tot_bq,
        tot_wk,
        tot_wv,
        tot_bv,
        tot_wo,
        tot_bo,
        tot_gone,
        tot_sone,
        tot_wup,
        small[8:12].reshape(1536),
        tot_wdown.reshape(1536, 768),
        tot_bdown,
        tot_gtwo,
        tot_stwo,
    )


def solution(mesh):
    split = Mesh(
        mesh.devices.reshape(mesh.shape["seq"], 2, 4, 4, mesh.shape["wsh"]),
        ("seq", "ctx_0", "ctx_1", "ctx_2", "wsh"),
    )
    rows = P(("seq", "wsh"), CTX, None)
    mat, vec = P("wsh", None), P("wsh")
    params = (mat, vec, mat, mat, vec, mat, vec, vec, vec, mat, vec, mat, vec, vec, vec)
    return jax.shard_map(
        local,
        mesh=split,
        in_specs=(rows, P(("seq", "wsh")), *params, rows),
        out_specs=(rows, rows, *params),
        check_vma=False,
    )
```

```python
import functools
import math

import jax
import jax.numpy as jnp
from jax import lax
from jax.experimental import pallas as pl
from jax.experimental.pallas import tpu as pltpu
from jax.sharding import Mesh
from jax.sharding import PartitionSpec as P

H = 12
HD = 64
D = 768
CTX = ("ctx_0", "ctx_1", "ctx_2")
f32 = jnp.float32
bf16 = jnp.bfloat16
MESH = pl.DeviceIdType.MESH
ANY = pl.ANY
MIB = 1024 * 1024


def place(axis):
    if axis == "x":
        return lax.axis_index("ctx_2")
    if axis == "z":
        return lax.axis_index("ctx_1")
    return lax.axis_index("ctx_0") * 2 + lax.axis_index("seq")


def away(axis, step):
    at = lax.rem(place(axis) + step + 4, 4)
    if axis == "x":
        return {"ctx_2": at}
    if axis == "z":
        return {"ctx_1": at}
    return {"ctx_0": at // 2, "seq": lax.rem(at, 2)}


def sibling():
    return {"wsh": 1 - lax.axis_index("wsh")}


def far():
    return {"ctx_0": 1 - lax.axis_index("ctx_0")}


def meet(devices):
    barrier = pltpu.get_barrier_semaphore()
    for d in devices:
        pl.semaphore_signal(barrier, inc=1, device_id=d, device_id_type=MESH)
    pl.semaphore_wait(barrier, len(devices))


class Sends:
    def __init__(self, send, recv):
        self.send, self.recv, self.used, self.all = send, recv, 0, []

    def start(self, src, dst, device):
        k = self.used
        self.used += 1
        copy = pltpu.make_async_remote_copy(
            src_ref=src,
            dst_ref=dst,
            send_sem=self.send.at[k],
            recv_sem=self.recv.at[k],
            device_id=device,
            device_id_type=MESH,
        )
        copy.start()
        self.all.append(copy)
        return copy

    def finish(self):
        for copy in self.all:
            copy.wait_send()


class Flow:
    def __init__(self, sends, ins, outs, layer, mine):
        self.sends, self.ins, self.outs, self.layer, self.mine = sends, ins, outs, layer, mine
        self.z, self.x = lax.axis_index("ctx_1"), lax.axis_index("ctx_2")
        self.flights = []

    def wait(self):
        for pair in self.flights:
            for copy in pair:
                copy.wait_recv()

    def near(self, axis):
        pos = place(axis)
        return lax.rem(pos + 3, 4), lax.rem(pos + 1, 4)

    def first(self):
        y, z, x = self.layer, self.z, self.x
        self.flights = []
        for i, o in zip(self.ins, self.outs):
            h = i.shape[0] // 2
            for axis, lo in (("x", 0), ("z", h)):
                src = i.at[pl.ds(lo, h)] if self.mine else o.at[y, z, x, pl.ds(lo, h)]
                dst = o.at[y, z, x, pl.ds(lo, h)]
                self.flights.append(
                    [self.sends.start(src, dst, away(axis, k)) for k in (1, -1)]
                )

    def first_on(self):
        y, z, x, at, later = self.layer, self.z, self.x, 0, []
        for i, o in zip(self.ins, self.outs):
            q = i.shape[0] // 4
            for axis, lo in (("x", 0), ("z", 2 * q)):
                right, left = self.flights[at]
                at += 1
                before, after = self.near(axis)
                if axis == "x":
                    a = o.at[y, z, before, pl.ds(lo, q)]
                    b = o.at[y, z, after, pl.ds(lo + q, q)]
                else:
                    a = o.at[y, before, x, pl.ds(lo, q)]
                    b = o.at[y, after, x, pl.ds(lo + q, q)]
                right.wait_recv()
                up = self.sends.start(a, a, away(axis, 1))
                left.wait_recv()
                later.append([up, self.sends.start(b, b, away(axis, -1))])
        self.flights = later

    def second(self):
        y, z, x, at, later = self.layer, self.z, self.x, 0, []
        for i, o in zip(self.ins, self.outs):
            h = i.shape[0] // 2
            for axis, lo in (("z", 0), ("x", h)):
                for copy in self.flights[at]:
                    copy.wait_recv()
                at += 1
                a = o.at[y, z, :, pl.ds(lo, h)] if axis == "z" else o.at[y, :, x, pl.ds(lo, h)]
                later.append([self.sends.start(a, a, away(axis, k)) for k in (1, -1)])
        self.flights = later

    def second_on(self):
        y, at, later = self.layer, 0, []
        for i, o in zip(self.ins, self.outs):
            h = i.shape[0] // 2
            for axis, lo in (("z", 0), ("x", h)):
                right, left = self.flights[at]
                at += 1
                before, after = self.near(axis)
                if axis == "z":
                    a = o.at[y, before, pl.ds(0, 2), pl.ds(lo, h)]
                    b = o.at[y, after, pl.ds(2, 2), pl.ds(lo, h)]
                else:
                    a = o.at[y, pl.ds(0, 2), before, pl.ds(lo, h)]
                    b = o.at[y, pl.ds(2, 2), after, pl.ds(lo, h)]
                right.wait_recv()
                up = self.sends.start(a, a, away(axis, 1))
                left.wait_recv()
                later.append([up, self.sends.start(b, b, away(axis, -1))])
        self.flights = later


def units(layer, steps):
    z, x = lax.axis_index("ctx_1"), lax.axis_index("ctx_2")
    picked = []
    for k in steps:
        picked.append(("A", layer, lax.rem(z + k + 4, 4)))
        picked.append(("B", layer, lax.rem(x + k + 4, 4)))
    return picked


def unit_at(unit):
    half, layer, i = unit
    if half == "A":
        return (layer, i, slice(None), pl.ds(0, 64))
    return (layer, slice(None), i, pl.ds(64, 64))


def start_kernel(*refs):
    x_in, vectors = refs[0], refs[7:16]
    outs, pair_outs, q_out = refs[16:19], refs[19:26], refs[26]
    xs, held, made, packed = refs[27], refs[28:35], refs[35:38], refs[38]
    send, recv, local, leave = refs[39:]
    pair_ins = (*refs[1:7], packed)
    sends = Sends(send, recv)
    y, z, x = (lax.axis_index(a) for a in CTX)
    core = lax.axis_index("wsh")
    meet(
        [away("x", 1), away("x", -1), away("z", 1), away("z", -1), far(), sibling()]
    )
    crossing = sends.start(x_in, xs.at[y, z, x], far())
    packed[...] = jnp.zeros_like(packed)
    for n, ref in enumerate(vectors):
        value = ref[...].astype(f32).reshape(1, -1)
        for k in range(value.shape[1] // 384):
            packed[n + k : n + k + 1, :] = value[:, k * 384 : (k + 1) * 384]
    mine = Flow(sends, [x_in], [xs], y, True)
    theirs = Flow(sends, [x_in], [xs], 1 - y, False)
    mine.first()
    own = pltpu.make_async_copy(x_in, xs.at[y, z, x], local.at[7])
    own.start()
    pairs, kept, left = [], [], []
    for n, (i, o) in enumerate(zip(pair_ins, held)):
        pairs.append(sends.start(i, o.at[core], sibling()))
        copy = pltpu.make_async_copy(i, o.at[core], local.at[n])
        copy.start()
        kept.append(copy)

    def depart(src, dst):
        copy = pltpu.make_async_copy(src, dst, leave.at[len(left)])
        copy.start()
        left.append(copy)

    def whole(n):
        kept[n].wait()
        pairs[n].wait_recv()
        depart(held[n], pair_outs[n])

    def project(unit):
        at = unit_at(unit)
        block = xs[at].reshape(256, D)
        for n, row in ((0, 0), (1, None), (2, 1)):
            value = nn(block, held[n][...].reshape(D, D))
            if row is not None:
                value = value + jnp.concatenate(
                    [held[6][c, row : row + 1] for c in range(2)], axis=1
                ).astype(f32)
            made[n][at] = value.astype(bf16).reshape(4, 64, D)
            depart(made[n].at[at], outs[n].at[at])

    mine.first_on()
    crossing.wait_recv()
    theirs.first()
    own.wait()
    mine.second()
    theirs.first_on()
    for n in (6, 0, 1, 2):
        whole(n)
    for unit in units(y, (0,)):
        project(unit)
    mine.second_on()
    theirs.second()
    for unit in units(y, (1, -1)):
        project(unit)
    mine.wait()
    for unit in units(y, (2,)):
        project(unit)
    for unit in units(1 - y, (0,)):
        project(unit)
    theirs.second_on()
    for n in (3, 4, 5):
        whole(n)
    for unit in units(1 - y, (1, -1)):
        project(unit)
    theirs.wait()
    for unit in units(1 - y, (2,)):
        project(unit)
    depart(made[0].at[y, z, x], q_out)
    for copy in left:
        copy.wait()
    sends.finish()


def start(block, pairs, vectors, cid):
    packed = jax.ShapeDtypeStruct((16, 384), f32)
    lands = [*pairs, packed]
    n_send = 1 + 32 + 7
    return pl.pallas_call(
        start_kernel,
        out_shape=[jax.ShapeDtypeStruct((2, 4, 4, 128, D), bf16)] * 3
        + [jax.ShapeDtypeStruct((2, *a.shape), a.dtype) for a in lands]
        + [jax.ShapeDtypeStruct((128, D), bf16)],
        in_specs=[pl.BlockSpec(memory_space=pltpu.HBM)] * 7
        + [pl.BlockSpec(memory_space=pltpu.VMEM)] * 9,
        out_specs=[pl.BlockSpec(memory_space=pltpu.HBM)] * 11,
        scratch_shapes=[pltpu.VMEM((2, 4, 4, 128, D), bf16)]
        + [pltpu.VMEM((2, *a.shape), a.dtype) for a in lands]
        + [pltpu.VMEM((2, 4, 4, 128, D), bf16)] * 3
        + [pltpu.VMEM(packed.shape, f32)]
        + [
            pltpu.SemaphoreType.DMA((n_send,)),
            pltpu.SemaphoreType.DMA((n_send,)),
            pltpu.SemaphoreType.DMA((8,)),
            pltpu.SemaphoreType.DMA((16 * 3 + 8,)),
        ],
        compiler_params=pltpu.CompilerParams(
            collective_id=cid, has_side_effects=True, vmem_limit_bytes=60 * MIB
        ),
    )(block, *pairs, *vectors)


def tn(a, b):
    return lax.dot_general(a, b, (((0,), (0,)), ((), ())), preferred_element_type=f32)


class Part:
    def __init__(self, sends, axes, lo, width):
        self.sends, self.axes, self.lo, self.width = sends, axes, lo, width
        self.pos = [place(a) for a in axes]

    def region(self, free, dim=None, c=None, half=None):
        at = [self.pos[d] for d in range(3)]
        if dim is not None:
            at[dim] = c
        sel = []
        for d in (0, 1):
            sel.append((0, 4) if d in free and d != dim else (at[d], 1))
        if 2 in free and dim != 2:
            sel.append((0, 2))
            cols = (self.lo, self.width)
        else:
            sel.append((at[2] // 2, 1))
            w = self.width // 2
            cols = (pl.multiple_of(self.lo + lax.rem(at[2], 2) * w, 128), w)
        sel.append((0, 48))
        if half is not None:
            for d in range(3):
                n = sel[d][1]
                if n > 1:
                    sel[d] = (half * (n // 2), n // 2)
                    break
            else:
                sel[3] = ((0, 32), (32, 16))[half]
        sel.append(cols)
        return tuple(pl.ds(a, n) for a, n in sel)

    def shape(self, free, dim, half=None):
        return tuple(s.size for s in self.region(free, dim, 0, half))


def add_into(dst, at, sources):
    first = [s.start for s in at]
    n = [s.size for s in at]
    for a in range(n[0]):
        for b in range(n[1]):

            @pl.loop(0, n[2])
            def _(c, a=a, b=b):
                here = (
                    first[0] + a, first[1] + b, first[2] + c, pl.ds(first[3], n[3]),
                    pl.ds(first[4], n[4]),
                )
                value = dst[here].astype(f32)
                for src in sources:
                    value = value + src[a, b, c].astype(f32)
                dst[here] = value.astype(bf16)


class Scatter:
    def __init__(self, part, acc, free, dim, t0, t1, u):
        self.part, self.acc, self.free, self.dim = part, acc, free, dim
        self.t0, self.t1, self.u = t0, t1, u
        self.axis, self.p = part.axes[dim], part.pos[dim]

    def at(self, k, half=None):
        return self.part.region(self.free, self.dim, lax.rem(self.p + k + 4, 4), half)

    def one(self):
        start = self.part.sends.start
        self.first = (
            start(self.acc.at[self.at(2, 0)], self.t0, away(self.axis, 1)),
            start(self.acc.at[self.at(2, 1)], self.t1, away(self.axis, -1)),
        )

    def two(self):
        start = self.part.sends.start
        self.first[0].wait_recv()
        add_into(self.acc, self.at(1, 0), [self.t0])
        a = start(self.acc.at[self.at(1)], self.u.at[0], away(self.axis, 1))
        self.first[1].wait_recv()
        add_into(self.acc, self.at(-1, 1), [self.t1])
        b = start(self.acc.at[self.at(-1)], self.u.at[1], away(self.axis, -1))
        self.second = (a, b)

    def end(self):
        for copy in self.second:
            copy.wait_recv()
        add_into(self.acc, self.at(0), [self.u.at[0], self.u.at[1]])


def scatters(part, acc, bufs):
    free, steps = [0, 1, 2], []
    for dim in (0, 1, 2):
        t0, t1, u = bufs[3 * dim : 3 * dim + 3]
        steps.append(Scatter(part, acc, tuple(free), dim, t0, t1, u))
        free.remove(dim)
    return steps


def scatter_buffers(width):
    part = Part.__new__(Part)
    part.lo, part.width, part.pos = 0, width, [0, 0, 0]
    free, shapes = [0, 1, 2], []
    for dim in (0, 1, 2):
        shapes += [part.shape(free, dim, 0), part.shape(free, dim, 1), (2, *part.shape(free, dim))]
        free.remove(dim)
    return [pltpu.VMEM(s, bf16) for s in shapes]


class Spread:
    def __init__(self, part, out, done, dim):
        self.part, self.out, self.done, self.dim = part, out, done, dim
        self.axis, self.p = part.axes[dim], part.pos[dim]

    def at(self, k, half=None):
        return self.part.region(self.done, self.dim, lax.rem(self.p + k + 4, 4), half)

    def one(self, src=None):
        src = self.out.at[self.at(0)] if src is None else src
        self.first = [
            self.part.sends.start(src, self.out.at[self.at(0)], away(self.axis, k)) for k in (1, -1)
        ]

    def two(self):
        self.first[0].wait_recv()
        a = self.out.at[self.at(-1, 0)]
        up = self.part.sends.start(a, a, away(self.axis, 1))
        self.first[1].wait_recv()
        b = self.out.at[self.at(1, 1)]
        self.second = [up, self.part.sends.start(b, b, away(self.axis, -1))]

    def end(self):
        for copy in self.second:
            copy.wait_recv()


def spreads(part, out, order):
    done, steps = [], []
    for dim in order:
        steps.append(Spread(part, out, tuple(done), dim))
        done.append(dim)
    return steps


THIRD = (4, 4, 2, 48, D)
ROUNDS = ("x", "y", "z")


def reduce_kernel(
    x_ref, mixed_ref, dq_ref, dk_ref, dv_ref, branch_ref, resid_ref, wq, wk, wv, chunks,
    small_in, out, small_out, token_out, left, right, small, acc, twins, cur, slots, *rest
):
    bufs, (send, recv, local) = rest[:27], rest[27:]
    core = lax.axis_index("wsh")
    twin = 1 - core
    sends = Sends(send, recv)
    pos = {a: place(a) for a in ROUNDS}
    meet([sibling()] + [away(a, k) for a in ROUNDS for k in (1, 2, 3)])
    up = spreads(Part(sends, ("y", "x", "z"), 0, D), out.at[1], (2, 0, 1))
    down = spreads(Part(sends, ("y", "z", "x"), 0, D), out.at[2], (2, 0, 1))
    kept = []

    def keep(src, dst):
        copy = pltpu.make_async_copy(src, dst, local.at[len(kept)])
        copy.start()
        kept.append(copy)

    for n, flow in enumerate((up, down)):
        flow[0].one(chunks.at[n])
        keep(chunks.at[n], flow[0].out.at[flow[0].at(0)])
    for m in range(4):
        left[m] = (mixed_ref if m == 3 else x_ref)[...]
        right[m] = (dq_ref, dk_ref, dv_ref, branch_ref)[m][...]

    def product(m, half):
        at = pl.ds(pl.multiple_of(half * 384, 384), 384)
        return tn(left[m, :, at], right[m]).reshape(4, 2, 48, D)

    flights = []
    for m in range(4):
        twins[m] = product(m, twin).astype(bf16)
        flights.append(sends.start(twins.at[m], acc.at[m], sibling()))
    small[...] = small_in[...]
    for n, ref in enumerate((dq_ref, dv_ref)):
        sums = jnp.sum(ref[...].astype(f32), axis=0, keepdims=True)
        for c in range(2):
            small[c, n : n + 1, :] = sums[:, c * 384 : (c + 1) * 384]
    small_pair = sends.start(small.at[twin], slots.at[3, 0], sibling())
    for flow in (up, down):
        flow[0].two()
    for m in range(4):
        mine = product(m, core)
        flights[m].wait_recv()
        acc[m] = (mine + acc[m].astype(f32)).astype(bf16)
    parts = [
        Part(sends, axes, 256 * n, 256)
        for n, axes in enumerate((("x", "y", "z"), ("y", "z", "x"), ("z", "x", "y")))
    ]
    sums = [scatters(p, acc, bufs[9 * n : 9 * n + 9]) for n, p in enumerate(parts)]
    backs = [spreads(p, out.at[0], (2, 1, 0)) for p in parts]
    for s in sums:
        s[0].one()
    small_pair.wait_recv()
    cur[...] = small[core] + slots[3, 0]
    for n, flow in enumerate((up, down)):
        flow[0].end()
        kept[n].wait()
        flow[1].one()

    def small_go(ph):
        slots[ph, pos[ROUNDS[ph]]] = cur[...]
        return [
            sends.start(cur, slots.at[ph, pos[ROUNDS[ph]]], away(ROUNDS[ph], k)) for k in (1, 2, 3)
        ]

    def small_end(ph, copies):
        for copy in copies:
            copy.wait()
        sends.all = [c for c in sends.all if all(c is not d for d in copies)]
        cur[...] = (slots[ph, 0] + slots[ph, 1]) + (slots[ph, 2] + slots[ph, 3])

    going = small_go(0)
    for s in sums:
        s[0].two()
    for flow in (up, down):
        flow[1].two()
    for s in sums:
        s[0].end()
        s[1].one()
    small_end(0, going)
    going = small_go(1)
    for flow in (up, down):
        flow[1].end()
        flow[2].one()
    for s in sums:
        s[1].two()
    for s in sums:
        s[1].end()
        s[2].one()
    small_end(1, going)
    going = small_go(2)
    for s in sums:
        s[2].two()
    small_end(2, going)
    small_out[...] = cur[...]
    for n, (s, b) in enumerate(zip(sums, backs)):
        s[2].end()
        here = b[0].at(0)
        b[0].one(acc.at[here])
        keep(acc.at[here], out.at[(0, *here)])
    for b in backs:
        b[0].two()
    for n, b in enumerate(backs):
        b[0].end()
        kept[2 + n].wait()
        b[1].one()
    for b in backs:
        b[1].two()
    for flow in (up, down):
        flow[2].two()
    for b in backs:
        b[1].end()
        b[2].one()
    token_out[...] = (
        resid_ref[...]
        + nt(dq_ref[...], wq[...].reshape(D, D))
        + nt(dk_ref[...], wk[...].reshape(D, D))
        + nt(dv_ref[...], wv[...].reshape(D, D))
    )
    for b in backs:
        b[2].two()
    for flow in (up, down, *backs):
        flow[2].end()
    sends.finish()


def reduce_params(arrays, cid):
    scratch = [pltpu.VMEM((4, 128, D), bf16)] * 2 + [pltpu.VMEM((2, 16, 384), f32)]
    scratch += [pltpu.VMEM(THIRD, bf16)] * 2
    scratch += [pltpu.VMEM((16, 384), f32), pltpu.VMEM((4, 4, 16, 384), f32)]
    scratch += scatter_buffers(256) * 3
    count = 4 + 1 + 9 + 2 * 12 + 3 * 24
    scratch += [
        pltpu.SemaphoreType.DMA((count,)),
        pltpu.SemaphoreType.DMA((count,)),
        pltpu.SemaphoreType.DMA((5,)),
    ]
    vm = pl.BlockSpec(memory_space=pltpu.VMEM)
    return pl.pallas_call(
        reduce_kernel,
        out_shape=[
            jax.ShapeDtypeStruct((3, *THIRD), bf16),
            jax.ShapeDtypeStruct((16, 384), f32),
            jax.ShapeDtypeStruct((128, D), f32),
        ],
        in_specs=[vm] * 12,
        out_specs=[pl.BlockSpec(memory_space=pltpu.HBM), vm, vm],
        scratch_shapes=scratch,
        compiler_params=pltpu.CompilerParams(
            collective_id=cid, has_side_effects=True, vmem_limit_bytes=60 * MIB
        ),
    )(*arrays)


def finish_kernel(big_ref, q_ref, k_ref, v_ref, o_ref, up_ref, down_ref):
    for n, ref in enumerate((q_ref, k_ref, v_ref, o_ref)):
        ref[...] = big_ref[0, n].astype(f32)
        up_ref[:, n * 768 : (n + 1) * 768] = big_ref[1, n].astype(f32)
        down_ref[n] = big_ref[2, n].astype(f32)


def finish(big):
    mat = pl.BlockSpec((96, 768), lambda r: (r, 0))
    return pl.pallas_call(
        finish_kernel,
        grid=(4,),
        out_shape=[jax.ShapeDtypeStruct((384, 768), f32)] * 4
        + [
            jax.ShapeDtypeStruct((384, 3072), f32),
            jax.ShapeDtypeStruct((4, 384, 768), f32),
        ],
        in_specs=[pl.BlockSpec((3, 4, 96, 768), lambda r: (0, 0, r, 0))],
        out_specs=[mat] * 4
        + [
            pl.BlockSpec((96, 3072), lambda r: (r, 0)),
            pl.BlockSpec((4, 96, 768), lambda r: (0, r, 0)),
        ],
        compiler_params=pltpu.CompilerParams(vmem_limit_bytes=60 * MIB),
    )(big)


def nt(a, b):
    return lax.dot_general(a, b, (((1,), (1,)), ((), ())), preferred_element_type=f32)


def nn(a, b):
    return jnp.dot(a, b, preferred_element_type=f32)


def stacked(block):
    lane = lax.broadcasted_iota(jnp.int32, block.shape, 1) // HD
    zero = jnp.zeros_like(block)
    return jnp.concatenate([jnp.where(lane == i, block, zero) for i in range(4)], axis=0)


def unstacked(tall):
    n = tall.shape[0] // 4
    lane = lax.broadcasted_iota(jnp.int32, (n, tall.shape[1]), 1) // HD
    total = jnp.where(lane == 0, tall[:n], 0.0)
    for i in range(1, 4):
        total = total + jnp.where(lane == i, tall[i * n : (i + 1) * n], 0.0)
    return total


def as_rows(column):
    wide = jnp.broadcast_to(column, (column.shape[0], 128))
    return jnp.concatenate(
        [wide[i * 128 : (i + 1) * 128].T[:1] for i in range(4)] + [jnp.zeros((4, 128), f32)], axis=0
    )


TILE = 1024


def forward_kernel(q_ref, k_ref, v_ref, bias_ref, attn_ref, lse_ref, rows_ref, score):
    q = stacked(q_ref[...] * jnp.asarray(0.125, bf16))
    top = None
    for t in range(4096 // TILE):
        at = pl.ds(t * TILE, TILE)
        s = nt(q, k_ref[at, :]) + bias_ref[:, at]
        score[:, at] = s
        m = jnp.max(s, axis=-1, keepdims=True)
        top = m if top is None else jnp.maximum(top, m)
    total, out = 0.0, 0.0
    for t in range(4096 // TILE):
        at = pl.ds(t * TILE, TILE)
        p = jnp.exp(score[:, at] - top)
        total = total + jnp.sum(p, axis=-1, keepdims=True)
        out = out + nn(p.astype(bf16), v_ref[at, :])
    attn_ref[...] = unstacked(out * (1.0 / total))
    lse = top + jnp.log(total)
    lse_ref[0] = jnp.broadcast_to(lse, (512, 128))
    rows_ref[0] = as_rows(lse)


def attend(q, k, v, bias):
    wide = pl.BlockSpec((4096, 256), lambda g: (0, g))
    own = pl.BlockSpec((128, 256), lambda g: (0, g))
    return pl.pallas_call(
        forward_kernel,
        grid=(3,),
        out_shape=[
            jax.ShapeDtypeStruct((128, D), f32),
            jax.ShapeDtypeStruct((3, 512, 128), f32),
            jax.ShapeDtypeStruct((3, 8, 128), f32),
        ],
        in_specs=[own, wide, wide, pl.BlockSpec((1, 4096), lambda g: (0, 0))],
        out_specs=[
            own,
            pl.BlockSpec((1, 512, 128), lambda g: (g, 0, 0)),
            pl.BlockSpec((1, 8, 128), lambda g: (g, 0, 0)),
        ],
        scratch_shapes=[pltpu.VMEM((512, 4096), f32)],
        compiler_params=pltpu.CompilerParams(vmem_limit_bytes=60 * MIB),
    )(q, k, v, bias)


FC = 768


def norm_parts(resid):
    centre = resid - jnp.mean(resid, axis=-1, keepdims=True)
    spread = jnp.mean(centre * centre, axis=-1, keepdims=True)
    scale = lax.rsqrt(spread + 1e-12)
    return centre * scale, scale


def norm_back(grad, norm, scale):
    return scale * (
        grad
        - jnp.mean(grad, axis=-1, keepdims=True)
        - norm * jnp.mean(grad * norm, axis=-1, keepdims=True)
    )


def middle_kernel(
    attn_ref, x_ref, cot_ref, vec_ref, wo_hbm, wup_hbm, wdown_hbm,
    result_ref, resid_ref, mixed_grad_ref, mixed_ref, first_ref, act_ref, pre_grad_ref,
    down_grad_ref, branch_ref, small_ref,
    wo, wup, wdown, slope, arrive,
):
    copies = []
    for n, (src, dst) in enumerate(((wo_hbm, wo), (wup_hbm, wup), (wdown_hbm, wdown))):
        copy = pltpu.make_async_copy(src, dst, arrive.at[n])
        copy.start()
        copies.append(copy)

    def row(i):
        return jnp.concatenate([vec_ref[c, i : i + 1] for c in range(2)], axis=1).astype(f32)

    def put(i, value):
        for c in range(2):
            small_ref[c, i : i + 1, :] = value[:, c * 384 : (c + 1) * 384]

    def down(value):
        return jnp.sum(value, axis=0, keepdims=True)

    mixed = attn_ref[...].astype(bf16)
    mixed_ref[...] = mixed
    copies[0].wait()
    resid = x_ref[...].astype(f32) + nn(mixed, wo[...].reshape(D, D)) + row(2)
    norm_one, scale_one = norm_parts(resid)
    gain_one = row(3)
    first = norm_one * gain_one + row(4)
    first_low = first.astype(bf16)
    first_ref[...] = first_low
    copies[1].wait()
    copies[2].wait()
    total = first + row(5)
    for j in range(4):
        cols = slice(j * FC, (j + 1) * FC)
        bias = jnp.concatenate(
            [vec_ref[j // 2, 8 + 2 * (j % 2) + k : 9 + 2 * (j % 2) + k] for k in range(2)], axis=1
        ).astype(f32)
        pre = nn(first_low, wup[:, :, cols].reshape(D, FC)) + bias
        phi = 0.5 * (1.0 + lax.erf(pre * (0.5**0.5)))
        slope[:, cols] = phi + pre * jnp.exp(-0.5 * pre * pre) * (1.0 / math.sqrt(2.0 * math.pi))
        act = (pre * phi).astype(bf16)
        act_ref[:, cols] = act
        total = total + nn(act, wdown[j // 2, (j % 2) * FC : (j % 2 + 1) * FC, :])
    norm_two, scale_two = norm_parts(total)
    gain_two = row(6)
    result_ref[...] = (norm_two * gain_two + row(7)).astype(bf16)
    cot = cot_ref[...].astype(f32)
    put(6, down(cot * norm_two))
    put(7, down(cot))
    grad_two = norm_back(cot * gain_two, norm_two, scale_two)
    put(5, down(grad_two))
    grad_down = grad_two.astype(bf16)
    down_grad_ref[...] = grad_down
    grad_first = grad_two
    for j in range(4):
        cols = slice(j * FC, (j + 1) * FC)
        grad_act = nt(grad_down, wdown[j // 2, (j % 2) * FC : (j % 2 + 1) * FC, :])
        grad_pre = (grad_act * slope[:, cols]).astype(bf16)
        pre_grad_ref[:, cols] = grad_pre
        sums = down(grad_pre.astype(f32))
        for k in range(2):
            i = 8 + 2 * (j % 2) + k
            small_ref[j // 2, i : i + 1, :] = sums[:, k * 384 : (k + 1) * 384]
        grad_first = grad_first + nt(grad_pre, wup[:, :, cols].reshape(D, FC))
    put(3, down(grad_first * norm_one))
    put(4, down(grad_first))
    grad_one = norm_back(grad_first * gain_one, norm_one, scale_one)
    resid_ref[...] = grad_one
    put(2, down(grad_one))
    branch = grad_one.astype(bf16)
    branch_ref[...] = branch
    mixed_grad_ref[...] = nt(branch, wo[...].reshape(D, D)).astype(bf16)
    zero = jnp.zeros((1, D), f32)
    put(0, zero)
    put(1, zero)
    for c in range(2):
        small_ref[c, 12:16, :] = jnp.zeros((4, 384), f32)


def middle(attn, x, cot, vecs, wo, wup, wdown):
    vm = pl.BlockSpec(memory_space=pltpu.VMEM)
    hbm = pl.BlockSpec(memory_space=pltpu.HBM)
    thin, wide = jax.ShapeDtypeStruct((128, D), bf16), jax.ShapeDtypeStruct((128, 3072), bf16)
    return pl.pallas_call(
        middle_kernel,
        out_shape=[
            thin, jax.ShapeDtypeStruct((128, D), f32), thin, thin, thin, wide, wide, thin, thin,
            jax.ShapeDtypeStruct((2, 16, 384), f32),
        ],
        in_specs=[vm] * 4 + [hbm] * 3,
        out_specs=[vm] * 10,
        scratch_shapes=[
            pltpu.VMEM(wo.shape, bf16),
            pltpu.VMEM(wup.shape, bf16),
            pltpu.VMEM(wdown.shape, bf16),
            pltpu.VMEM((128, 3072), f32),
            pltpu.SemaphoreType.DMA((3,)),
        ],
        compiler_params=pltpu.CompilerParams(vmem_limit_bytes=60 * MIB),
    )(attn, x, cot, vecs, wo, wup, wdown)


def back_kernel(
    q_hbm, k_hbm, v_hbm, g_in, attn_ref, lse_ref, rows_ref, bias_ref,
    first_ref, pre_grad_ref, act_ref, down_grad_ref, dq_ref, dk_ref, dv_ref, chunk_ref,
    qv, kv, vv, gv, stats, stat_own, q_own, k_own, v_own, g_own, delta, dq_acc, dk_acc, dv_acc,
    acc, twins, *rest
):
    bufs, (send, recv, local) = rest[:18], rest[18:]
    sends = Sends(send, recv)
    y, z, x = (lax.axis_index(a) for a in CTX)
    core = lax.axis_index("wsh")
    meet([sibling(), far()] + [away(a, k) for a in ROUNDS for k in (1, -1)])
    loads = []
    for n, (src, dst) in enumerate(
        ((k_hbm, kv), (v_hbm, vv), (q_hbm, qv))
    ):
        copy = pltpu.make_async_copy(src, dst, local.at[n])
        copy.start()
        loads.append(copy)
    eighth = jnp.asarray(0.125, bf16)
    low = lax.broadcasted_iota(jnp.int32, (4, 128), 1) < 64
    stat_own[...] = jnp.zeros_like(stat_own)
    for n in range(3):
        cols = pl.ds(n * 256, 256)
        g = stacked(g_in[:, cols])
        g_own[n] = g
        tall = jnp.concatenate([attn_ref[:, cols]] * 4, axis=0)
        d = jnp.sum(g.astype(f32) * tall, axis=-1, keepdims=True)
        delta[n] = jnp.broadcast_to(d, (512, 128))
        d = as_rows(d)[:4]
        lse = rows_ref[n][:4]
        stat_own[pl.ds(4 * n, 4), :] = jnp.where(low, lse, pltpu.roll(d, 64, 1))
        stat_own[pl.ds(16 + 4 * n, 4), :] = jnp.where(low, pltpu.roll(lse, 64, 1), d)
        dq_acc[n] = jnp.zeros((512, 256), f32)
        dk_acc[n] = jnp.zeros((512, 256), f32)
        dv_acc[n] = jnp.zeros((512, 256), f32)
    ins, outs = [g_in, stat_own], [gv, stats]
    crossing = [sends.start(i, o.at[y, z, x], far()) for i, o in zip(ins, outs)]
    mine = Flow(sends, ins, outs, y, True)
    theirs = Flow(sends, ins, outs, 1 - y, False)
    mine.first()
    own = []
    for n, (i, o) in enumerate(zip(ins, outs)):
        copy = pltpu.make_async_copy(i, o.at[y, z, x], local.at[3 + n])
        copy.start()
        own.append(copy)
    for copy in loads:
        copy.wait()
    for n in range(3):
        cols = pl.ds(n * 256, 256)
        q_own[n] = stacked(qv[y, z, x, :, cols] * eighth)
        k_own[n] = stacked(kv[y, z, x, :, cols] * eighth)
        v_own[n] = stacked(vv[y, z, x, :, cols])

    def queries(lo, hi):
        @pl.loop(lo, hi)
        def _(c):
            n, t = c // 4, c % 4
            cols = pl.ds(pl.multiple_of(n * 256, 256), 256)
            k = kv[t // 2, pl.ds(2 * (t % 2), 2), :, :, cols].reshape(TILE, 256)
            v = vv[t // 2, pl.ds(2 * (t % 2), 2), :, :, cols].reshape(TILE, 256)
            bias = bias_ref[:, pl.ds(pl.multiple_of(t * TILE, TILE), TILE)]
            p = jnp.exp(nt(q_own[n], k) + bias - lse_ref[n][:, :1])
            dp = nt(g_own[n], v)
            ds = (p * (dp - delta[n][:, :1])).astype(bf16)
            dq_acc[n] = dq_acc[n] + nn(ds, k)

    low16 = lax.broadcasted_iota(jnp.int32, (16, 128), 1) < 64

    def keys(unit):
        half, layer, i = unit
        r = 0 if half == "A" else 64
        if half == "A":
            st = stats[layer, i, :, pl.ds(0, 16)]
        else:
            st = stats[layer, :, i, pl.ds(16, 16)]
        turned = [pltpu.roll(st[b], 64, 1) for b in range(4)]
        lse = jnp.concatenate(
            [jnp.where(low16, st[b], turned[b + 1]) for b in (0, 2)], axis=1
        )
        dlt = jnp.concatenate(
            [jnp.where(low16, turned[b], st[b + 1]) for b in (0, 2)], axis=1
        )
        for n in range(3):
            cols = pl.ds(n * 256, 256)
            if half == "A":
                at = (layer, i, slice(None), pl.ds(0, 64), cols)
            else:
                at = (layer, slice(None), i, pl.ds(64, 64), cols)
            q, g = qv[at].reshape(256, 256), gv[at].reshape(256, 256)

            def spread(rows):
                return jnp.concatenate(
                    [jnp.broadcast_to(rows[4 * n + h : 4 * n + h + 1], (128, 256)) for h in range(4)],
                    axis=0,
                )

            p = jnp.exp(nt(k_own[n], q) - spread(lse))
            ds = (p * (nt(v_own[n], g) - spread(dlt))).astype(bf16)
            dv_acc[n] = dv_acc[n] + nn(p.astype(bf16), g)
            dk_acc[n] = dk_acc[n] + nn(ds, q)

    def product(s, m, half):
        if s == 0:
            value = tn(
                first_ref[:, pl.ds(pl.multiple_of(half * 384, 384), 384)],
                pre_grad_ref[:, pl.ds(pl.multiple_of(m * 768, 768), 768)],
            )
        else:
            value = tn(
                act_ref[:, pl.ds(pl.multiple_of(half * 1536 + m * 384, 384), 384)],
                down_grad_ref[...],
            )
        return value.reshape(4, 2, 48, D)

    row = place("y")
    flights = {}
    for k in (2, 1, 3, 0):
        m = lax.rem(row + k, 4)
        for s in range(2):
            twins[s, m] = product(s, m, 1 - core).astype(bf16)
            flights[s, k] = sends.start(twins.at[s, m], acc.at[s, m], sibling())

    def settle(k):
        m = lax.rem(row + k, 4)
        for s in range(2):
            value = product(s, m, core)
            flights[s, k].wait_recv()
            acc[s, m] = (value + acc[s, m].astype(f32)).astype(bf16)

    sums = [
        scatters(Part(sends, axes, 0, D), acc.at[n], bufs[9 * n : 9 * n + 9])
        for n, axes in enumerate((("y", "x", "z"), ("y", "z", "x")))
    ]

    def step(ph, name):
        for s in sums:
            getattr(s[ph], name)()

    mine.first_on()
    for copy in crossing:
        copy.wait_recv()
    theirs.first()
    settle(2)
    step(0, "one")
    queries(0, 2)
    for copy in own:
        copy.wait()
    mine.second()
    theirs.first_on()
    settle(1)
    settle(3)
    queries(2, 4)
    step(0, "two")
    queries(4, 8)
    for unit in units(y, (0,)):
        keys(unit)
    mine.second_on()
    theirs.second()
    settle(0)
    for unit in units(y, (1, -1)):
        keys(unit)
    queries(8, 10)
    step(0, "end")
    step(1, "one")
    mine.wait()
    for unit in units(y, (2,)):
        keys(unit)
    step(1, "two")
    theirs.second_on()
    queries(10, 12)
    for unit in units(1 - y, (0,)):
        keys(unit)
    step(1, "end")
    step(2, "one")
    for n in range(3):
        dq_ref[:, pl.ds(n * 256, 256)] = (unstacked(dq_acc[n]) * 0.125).astype(bf16)
    for unit in units(1 - y, (1, -1)):
        keys(unit)
    step(2, "two")
    theirs.wait()
    for unit in units(1 - y, (2,)):
        keys(unit)
    step(2, "end")
    for n, s in enumerate(sums):
        chunk_ref[n] = acc[(n, *s[2].at(0))]
    at = pl.multiple_of(((y * 4 + z) * 4 + x) * 128, 128)
    keep = jnp.broadcast_to(bias_ref[:, pl.ds(at, 128)], (128, 128)).T[:, :1] > -1.0
    for n in range(3):
        cols = pl.ds(n * 256, 256)
        dk_ref[:, cols] = jnp.where(keep, unstacked(dk_acc[n]) * 0.125, 0.0).astype(bf16)
        dv_ref[:, cols] = jnp.where(keep, unstacked(dv_acc[n]), 0.0).astype(bf16)
    sends.finish()


def attend_back(q, k, v, g, attn, lse, lse_rows, bias, extra, cid):
    n_send = 33 * 2 + 8 + 24
    vm = pl.BlockSpec(memory_space=pltpu.VMEM)
    wide = pltpu.VMEM((2, 4, 4, 128, D), bf16)
    tall = pltpu.VMEM((3, 512, 256), bf16)
    sums = pltpu.VMEM((3, 512, 256), f32)
    return pl.pallas_call(
        back_kernel,
        out_shape=[jax.ShapeDtypeStruct((128, D), bf16)] * 3
        + [jax.ShapeDtypeStruct((2, 1, 1, 1, 48, 384), bf16)],
        in_specs=[pl.BlockSpec(memory_space=pltpu.HBM)] * 3 + [vm] * 9,
        out_specs=[vm] * 4,
        scratch_shapes=[wide] * 4
        + [pltpu.VMEM((2, 4, 4, 32, 128), f32), pltpu.VMEM((32, 128), f32)]
        + [tall] * 4
        + [pltpu.VMEM((3, 512, 128), f32)]
        + [sums] * 3
        + [pltpu.VMEM((2, *THIRD), bf16)] * 2
        + scatter_buffers(D) * 2
        + [
            pltpu.SemaphoreType.DMA((n_send,)),
            pltpu.SemaphoreType.DMA((n_send,)),
            pltpu.SemaphoreType.DMA((5,)),
        ],
        compiler_params=pltpu.CompilerParams(
            collective_id=cid, has_side_effects=True, vmem_limit_bytes=60 * MIB
        ),
    )(q, k, v, g, attn, lse, lse_rows, bias, *extra)


def local(
    tokens, lengths, w_query, b_query, w_key, w_value, b_value, w_out, b_out, gain_one, shift_one,
    w_up, b_up, w_down, b_down, gain_two, shift_two, cotangent,
):
    inputs = tokens[0]
    all_q, all_k, all_v, wq, wk, wv, wo, wup, wdown, vecs, q = start(
        inputs,
        [w_query, w_key, w_value, w_out, w_up, w_down],
        [b_query, b_value, b_out, gain_one, shift_one, b_down, gain_two, shift_two, b_up],
        0,
    )
    bias = jnp.where(jnp.arange(4096) < lengths[0], 0.0, -1e30).astype(f32)[None]
    attn, lse, lse_rows = attend(q, all_k.reshape(4096, D), all_v.reshape(4096, D), bias)
    (
        result, grad_resid, grad_mixed, mixed, first, act, grad_pre, grad_down, branch, small
    ) = middle(attn, inputs, cotangent[0], vecs, wo, wup, wdown)
    dq, dk, dv, chunks = attend_back(
        all_q, all_k, all_v, grad_mixed, attn, lse, lse_rows, bias,
        [first, grad_pre, act, grad_down], 1,
    )
    big, small, grad_inputs = reduce_params(
        [
            inputs, mixed, dq, dk, dv, branch, grad_resid, wq, wk, wv,
            chunks, small,
        ],
        2,
    )
    tot_wq, tot_wk, tot_wv, tot_wo, tot_wup, tot_wdown = finish(
        big.reshape(3, 4, 384, D)
    )
    tot_bq, tot_bv, tot_bo, tot_gone, tot_sone, tot_bdown, tot_gtwo, tot_stwo = (
        small[i] for i in range(8)
    )
    return (
        result[None],
        grad_inputs[None],
        tot_wq,
        tot_bq,
        tot_wk,
        tot_wv,
        tot_bv,
        tot_wo,
        tot_bo,
        tot_gone,
        tot_sone,
        tot_wup,
        small[8:12].reshape(1536),
        tot_wdown.reshape(1536, 768),
        tot_bdown,
        tot_gtwo,
        tot_stwo,
    )


def solution(mesh):
    split = Mesh(
        mesh.devices.reshape(mesh.shape["seq"], 2, 4, 4, mesh.shape["wsh"]),
        ("seq", "ctx_0", "ctx_1", "ctx_2", "wsh"),
    )
    rows = P(("seq", "wsh"), CTX, None)
    mat, vec = P("wsh", None), P("wsh")
    params = (mat, vec, mat, mat, vec, mat, vec, vec, vec, mat, vec, mat, vec, vec, vec)
    return jax.shard_map(
        local,
        mesh=split,
        in_specs=(rows, P(("seq", "wsh")), *params, rows),
        out_specs=(rows, rows, *params),
        check_vma=False,
    )
```

```python
import functools
import math

import jax
import jax.numpy as jnp
from jax import lax
from jax.experimental import pallas as pl
from jax.experimental.pallas import tpu as pltpu
from jax.sharding import Mesh
from jax.sharding import PartitionSpec as P

H = 12
HD = 64
D = 768
CTX = ("ctx_0", "ctx_1", "ctx_2")
f32 = jnp.float32
bf16 = jnp.bfloat16
MESH = pl.DeviceIdType.MESH
ANY = pl.ANY
MIB = 1024 * 1024


def place(axis):
    if axis == "x":
        return lax.axis_index("ctx_2")
    if axis == "z":
        return lax.axis_index("ctx_1")
    return lax.axis_index("ctx_0") * 2 + lax.axis_index("seq")


def away(axis, step):
    at = lax.rem(place(axis) + step + 4, 4)
    if axis == "x":
        return {"ctx_2": at}
    if axis == "z":
        return {"ctx_1": at}
    return {"ctx_0": at // 2, "seq": lax.rem(at, 2)}


def sibling():
    return {"wsh": 1 - lax.axis_index("wsh")}


def far():
    return {"ctx_0": 1 - lax.axis_index("ctx_0")}


def meet(devices):
    barrier = pltpu.get_barrier_semaphore()
    for d in devices:
        pl.semaphore_signal(barrier, inc=1, device_id=d, device_id_type=MESH)
    pl.semaphore_wait(barrier, len(devices))


class Sends:
    def __init__(self, send, recv):
        self.send, self.recv, self.used, self.all = send, recv, 0, []

    def start(self, src, dst, device):
        k = self.used
        self.used += 1
        copy = pltpu.make_async_remote_copy(
            src_ref=src,
            dst_ref=dst,
            send_sem=self.send.at[k],
            recv_sem=self.recv.at[k],
            device_id=device,
            device_id_type=MESH,
        )
        copy.start()
        self.all.append(copy)
        return copy

    def finish(self):
        for copy in self.all:
            copy.wait_send()


class Flow:
    def __init__(self, sends, ins, outs, layer, mine):
        self.sends, self.ins, self.outs, self.layer, self.mine = sends, ins, outs, layer, mine
        self.z, self.x = lax.axis_index("ctx_1"), lax.axis_index("ctx_2")
        self.flights = []

    def wait(self):
        for pair in self.flights:
            for copy in pair:
                copy.wait_recv()

    def near(self, axis):
        pos = place(axis)
        return lax.rem(pos + 3, 4), lax.rem(pos + 1, 4)

    def first(self):
        y, z, x = self.layer, self.z, self.x
        self.flights = []
        for i, o in zip(self.ins, self.outs):
            h = i.shape[0] // 2
            for axis, lo in (("x", 0), ("z", h)):
                src = i.at[pl.ds(lo, h)] if self.mine else o.at[y, z, x, pl.ds(lo, h)]
                dst = o.at[y, z, x, pl.ds(lo, h)]
                self.flights.append(
                    [self.sends.start(src, dst, away(axis, k)) for k in (1, -1)]
                )

    def first_on(self):
        y, z, x, at, later = self.layer, self.z, self.x, 0, []
        for i, o in zip(self.ins, self.outs):
            q = i.shape[0] // 4
            for axis, lo in (("x", 0), ("z", 2 * q)):
                right, left = self.flights[at]
                at += 1
                before, after = self.near(axis)
                if axis == "x":
                    a = o.at[y, z, before, pl.ds(lo, q)]
                    b = o.at[y, z, after, pl.ds(lo + q, q)]
                else:
                    a = o.at[y, before, x, pl.ds(lo, q)]
                    b = o.at[y, after, x, pl.ds(lo + q, q)]
                right.wait_recv()
                up = self.sends.start(a, a, away(axis, 1))
                left.wait_recv()
                later.append([up, self.sends.start(b, b, away(axis, -1))])
        self.flights = later

    def second(self):
        y, z, x, at, later = self.layer, self.z, self.x, 0, []
        for i, o in zip(self.ins, self.outs):
            h = i.shape[0] // 2
            for axis, lo in (("z", 0), ("x", h)):
                for copy in self.flights[at]:
                    copy.wait_recv()
                at += 1
                a = o.at[y, z, :, pl.ds(lo, h)] if axis == "z" else o.at[y, :, x, pl.ds(lo, h)]
                later.append([self.sends.start(a, a, away(axis, k)) for k in (1, -1)])
        self.flights = later

    def second_on(self):
        y, at, later = self.layer, 0, []
        for i, o in zip(self.ins, self.outs):
            h = i.shape[0] // 2
            for axis, lo in (("z", 0), ("x", h)):
                right, left = self.flights[at]
                at += 1
                before, after = self.near(axis)
                if axis == "z":
                    a = o.at[y, before, pl.ds(0, 2), pl.ds(lo, h)]
                    b = o.at[y, after, pl.ds(2, 2), pl.ds(lo, h)]
                else:
                    a = o.at[y, pl.ds(0, 2), before, pl.ds(lo, h)]
                    b = o.at[y, pl.ds(2, 2), after, pl.ds(lo, h)]
                right.wait_recv()
                up = self.sends.start(a, a, away(axis, 1))
                left.wait_recv()
                later.append([up, self.sends.start(b, b, away(axis, -1))])
        self.flights = later


def units(layer, steps):
    z, x = lax.axis_index("ctx_1"), lax.axis_index("ctx_2")
    picked = []
    for k in steps:
        picked.append(("A", layer, lax.rem(z + k + 4, 4)))
        picked.append(("B", layer, lax.rem(x + k + 4, 4)))
    return picked


def unit_at(unit):
    half, layer, i = unit
    if half == "A":
        return (layer, i, slice(None), pl.ds(0, 64))
    return (layer, slice(None), i, pl.ds(64, 64))


def start_kernel(*refs):
    x_in, vectors = refs[0], refs[7:16]
    outs, pair_outs, q_out = refs[16:19], refs[19:26], refs[26]
    xs, held, made, packed = refs[27], refs[28:35], refs[35:38], refs[38]
    send, recv, local, leave = refs[39:]
    pair_ins = (*refs[1:7], packed)
    sends = Sends(send, recv)
    y, z, x = (lax.axis_index(a) for a in CTX)
    core = lax.axis_index("wsh")
    meet(
        [away("x", 1), away("x", -1), away("z", 1), away("z", -1), far(), sibling()]
    )
    crossing = sends.start(x_in, xs.at[y, z, x], far())
    packed[...] = jnp.zeros_like(packed)
    for n, ref in enumerate(vectors):
        value = ref[...].astype(f32).reshape(1, -1)
        for k in range(value.shape[1] // 384):
            packed[n + k : n + k + 1, :] = value[:, k * 384 : (k + 1) * 384]
    mine = Flow(sends, [x_in], [xs], y, True)
    theirs = Flow(sends, [x_in], [xs], 1 - y, False)
    mine.first()
    own = pltpu.make_async_copy(x_in, xs.at[y, z, x], local.at[7])
    own.start()
    pairs, kept, left = [], [], []
    for n, (i, o) in enumerate(zip(pair_ins, held)):
        pairs.append(sends.start(i, o.at[core], sibling()))
        copy = pltpu.make_async_copy(i, o.at[core], local.at[n])
        copy.start()
        kept.append(copy)

    def depart(src, dst):
        copy = pltpu.make_async_copy(src, dst, leave.at[len(left)])
        copy.start()
        left.append(copy)

    def whole(n):
        kept[n].wait()
        pairs[n].wait_recv()
        depart(held[n], pair_outs[n])

    def project(unit):
        at = unit_at(unit)
        block = xs[at].reshape(256, D)
        for n, row in ((0, 0), (1, None), (2, 1)):
            value = nn(block, held[n][...].reshape(D, D))
            if row is not None:
                value = value + jnp.concatenate(
                    [held[6][c, row : row + 1] for c in range(2)], axis=1
                ).astype(f32)
            made[n][at] = value.astype(bf16).reshape(4, 64, D)
            depart(made[n].at[at], outs[n].at[at])

    mine.first_on()
    crossing.wait_recv()
    theirs.first()
    own.wait()
    mine.second()
    theirs.first_on()
    for n in (6, 0, 1, 2):
        whole(n)
    for unit in units(y, (0,)):
        project(unit)
    mine.second_on()
    theirs.second()
    for unit in units(y, (1, -1)):
        project(unit)
    mine.wait()
    for unit in units(y, (2,)):
        project(unit)
    for unit in units(1 - y, (0,)):
        project(unit)
    theirs.second_on()
    for n in (3, 4, 5):
        whole(n)
    for unit in units(1 - y, (1, -1)):
        project(unit)
    theirs.wait()
    for unit in units(1 - y, (2,)):
        project(unit)
    depart(made[0].at[y, z, x], q_out)
    for copy in left:
        copy.wait()
    sends.finish()


def start(block, pairs, vectors, cid):
    packed = jax.ShapeDtypeStruct((16, 384), f32)
    lands = [*pairs, packed]
    n_send = 1 + 32 + 7
    return pl.pallas_call(
        start_kernel,
        out_shape=[jax.ShapeDtypeStruct((2, 4, 4, 128, D), bf16)] * 3
        + [jax.ShapeDtypeStruct((2, *a.shape), a.dtype) for a in lands]
        + [jax.ShapeDtypeStruct((128, D), bf16)],
        in_specs=[pl.BlockSpec(memory_space=pltpu.HBM)] * 7
        + [pl.BlockSpec(memory_space=pltpu.VMEM)] * 9,
        out_specs=[pl.BlockSpec(memory_space=pltpu.HBM)] * 11,
        scratch_shapes=[pltpu.VMEM((2, 4, 4, 128, D), bf16)]
        + [pltpu.VMEM((2, *a.shape), a.dtype) for a in lands]
        + [pltpu.VMEM((2, 4, 4, 128, D), bf16)] * 3
        + [pltpu.VMEM(packed.shape, f32)]
        + [
            pltpu.SemaphoreType.DMA((n_send,)),
            pltpu.SemaphoreType.DMA((n_send,)),
            pltpu.SemaphoreType.DMA((8,)),
            pltpu.SemaphoreType.DMA((16 * 3 + 8,)),
        ],
        compiler_params=pltpu.CompilerParams(
            collective_id=cid, has_side_effects=True, vmem_limit_bytes=60 * MIB
        ),
    )(block, *pairs, *vectors)


def tn(a, b):
    return lax.dot_general(a, b, (((0,), (0,)), ((), ())), preferred_element_type=f32)


class Part:
    def __init__(self, sends, axes, lo, width):
        self.sends, self.axes, self.lo, self.width = sends, axes, lo, width
        self.pos = [place(a) for a in axes]

    def region(self, free, dim=None, c=None, half=None):
        at = [self.pos[d] for d in range(3)]
        if dim is not None:
            at[dim] = c
        sel = []
        for d in (0, 1):
            sel.append((0, 4) if d in free and d != dim else (at[d], 1))
        if 2 in free and dim != 2:
            sel.append((0, 2))
            cols = (self.lo, self.width)
        else:
            sel.append((at[2] // 2, 1))
            w = self.width // 2
            cols = (pl.multiple_of(self.lo + lax.rem(at[2], 2) * w, 128), w)
        sel.append((0, 48))
        if half is not None:
            for d in range(3):
                n = sel[d][1]
                if n > 1:
                    sel[d] = (half * (n // 2), n // 2)
                    break
            else:
                sel[3] = ((0, 32), (32, 16))[half]
        sel.append(cols)
        return tuple(pl.ds(a, n) for a, n in sel)

    def shape(self, free, dim, half=None):
        return tuple(s.size for s in self.region(free, dim, 0, half))


def add_into(dst, at, sources):
    first = [s.start for s in at]
    n = [s.size for s in at]
    for a in range(n[0]):
        for b in range(n[1]):

            @pl.loop(0, n[2])
            def _(c, a=a, b=b):
                here = (
                    first[0] + a, first[1] + b, first[2] + c, pl.ds(first[3], n[3]),
                    pl.ds(first[4], n[4]),
                )
                value = dst[here].astype(f32)
                for src in sources:
                    value = value + src[a, b, c].astype(f32)
                dst[here] = value.astype(bf16)


class Scatter:
    def __init__(self, part, acc, free, dim, t0, t1, u):
        self.part, self.acc, self.free, self.dim = part, acc, free, dim
        self.t0, self.t1, self.u = t0, t1, u
        self.axis, self.p = part.axes[dim], part.pos[dim]

    def at(self, k, half=None):
        return self.part.region(self.free, self.dim, lax.rem(self.p + k + 4, 4), half)

    def one(self):
        start = self.part.sends.start
        self.first = (
            start(self.acc.at[self.at(2, 0)], self.t0, away(self.axis, 1)),
            start(self.acc.at[self.at(2, 1)], self.t1, away(self.axis, -1)),
        )

    def two(self):
        start = self.part.sends.start
        self.first[0].wait_recv()
        add_into(self.acc, self.at(1, 0), [self.t0])
        a = start(self.acc.at[self.at(1)], self.u.at[0], away(self.axis, 1))
        self.first[1].wait_recv()
        add_into(self.acc, self.at(-1, 1), [self.t1])
        b = start(self.acc.at[self.at(-1)], self.u.at[1], away(self.axis, -1))
        self.second = (a, b)

    def end(self):
        for copy in self.second:
            copy.wait_recv()
        add_into(self.acc, self.at(0), [self.u.at[0], self.u.at[1]])


def scatters(part, acc, bufs):
    free, steps = [0, 1, 2], []
    for dim in (0, 1, 2):
        t0, t1, u = bufs[3 * dim : 3 * dim + 3]
        steps.append(Scatter(part, acc, tuple(free), dim, t0, t1, u))
        free.remove(dim)
    return steps


def scatter_buffers(width):
    part = Part.__new__(Part)
    part.lo, part.width, part.pos = 0, width, [0, 0, 0]
    free, shapes = [0, 1, 2], []
    for dim in (0, 1, 2):
        shapes += [part.shape(free, dim, 0), part.shape(free, dim, 1), (2, *part.shape(free, dim))]
        free.remove(dim)
    return [pltpu.VMEM(s, bf16) for s in shapes]


class Spread:
    def __init__(self, part, out, done, dim):
        self.part, self.out, self.done, self.dim = part, out, done, dim
        self.axis, self.p = part.axes[dim], part.pos[dim]

    def at(self, k, half=None):
        return self.part.region(self.done, self.dim, lax.rem(self.p + k + 4, 4), half)

    def one(self, src=None):
        src = self.out.at[self.at(0)] if src is None else src
        self.first = [
            self.part.sends.start(src, self.out.at[self.at(0)], away(self.axis, k)) for k in (1, -1)
        ]

    def two(self):
        self.first[0].wait_recv()
        a = self.out.at[self.at(-1, 0)]
        up = self.part.sends.start(a, a, away(self.axis, 1))
        self.first[1].wait_recv()
        b = self.out.at[self.at(1, 1)]
        self.second = [up, self.part.sends.start(b, b, away(self.axis, -1))]

    def end(self):
        for copy in self.second:
            copy.wait_recv()


def spreads(part, out, order):
    done, steps = [], []
    for dim in order:
        steps.append(Spread(part, out, tuple(done), dim))
        done.append(dim)
    return steps


THIRD = (4, 4, 2, 48, D)
FEED = (
    (0, ("y", "x", "z"), 0, 768),
    (1, ("x", "y", "z"), 0, 512),
    (1, ("z", "y", "x"), 512, 256),
)
ROUNDS = ("x", "y", "z")


def reduce_kernel(
    x_ref, mixed_ref, dq_ref, dk_ref, dv_ref, branch_ref, resid_ref, wq, wk, wv, *more
):
    chunks, small_in, out, small_out, token_out = more[:3], *more[3:7]
    left, right, small, acc, twins, cur, slots, *rest = more[7:]
    bufs, (send, recv, local) = rest[:27], rest[27:]
    core = lax.axis_index("wsh")
    twin = 1 - core
    sends = Sends(send, recv)
    pos = {a: place(a) for a in ROUNDS}
    meet([sibling()] + [away(a, k) for a in ROUNDS for k in (1, 2, 3)])
    feeds = [
        spreads(Part(sends, axes, lo, width), out.at[1 + s], (2, 1, 0))
        for s, axes, lo, width in FEED
    ]
    kept = []

    def keep(src, dst):
        copy = pltpu.make_async_copy(src, dst, local.at[len(kept)])
        copy.start()
        kept.append(copy)

    for flow, chunk in zip(feeds, chunks):
        flow[0].one(chunk)
        keep(chunk, flow[0].out.at[flow[0].at(0)])
    for m in range(4):
        left[m] = (mixed_ref if m == 3 else x_ref)[...]
        right[m] = (dq_ref, dk_ref, dv_ref, branch_ref)[m][...]

    def product(m, half):
        at = pl.ds(pl.multiple_of(half * 384, 384), 384)
        return tn(left[m, :, at], right[m]).reshape(4, 2, 48, D)

    flights = []
    for m in range(4):
        twins[m] = product(m, twin).astype(bf16)
        flights.append(sends.start(twins.at[m], acc.at[m], sibling()))
    small[...] = small_in[...]
    for n, ref in enumerate((dq_ref, dv_ref)):
        sums = jnp.sum(ref[...].astype(f32), axis=0, keepdims=True)
        for c in range(2):
            small[c, n : n + 1, :] = sums[:, c * 384 : (c + 1) * 384]
    small_pair = sends.start(small.at[twin], slots.at[3, 0], sibling())
    for flow in feeds:
        flow[0].two()
    for m in range(4):
        mine = product(m, core)
        flights[m].wait_recv()
        acc[m] = (mine + acc[m].astype(f32)).astype(bf16)
        if m == 1:
            for n, flow in enumerate(feeds):
                flow[0].end()
                kept[n].wait()
                flow[1].one()
    parts = [
        Part(sends, axes, 256 * n, 256)
        for n, axes in enumerate((("x", "y", "z"), ("y", "z", "x"), ("z", "x", "y")))
    ]
    sums = [scatters(p, acc, bufs[9 * n : 9 * n + 9]) for n, p in enumerate(parts)]
    backs = [spreads(p, out.at[0], (2, 1, 0)) for p in parts]
    for s in sums:
        s[0].one()
    small_pair.wait_recv()
    cur[...] = small[core] + slots[3, 0]
    for flow in feeds:
        flow[1].two()

    def small_go(ph):
        slots[ph, pos[ROUNDS[ph]]] = cur[...]
        return [
            sends.start(cur, slots.at[ph, pos[ROUNDS[ph]]], away(ROUNDS[ph], k)) for k in (1, 2, 3)
        ]

    def small_end(ph, copies):
        for copy in copies:
            copy.wait()
        sends.all = [c for c in sends.all if all(c is not d for d in copies)]
        cur[...] = (slots[ph, 0] + slots[ph, 1]) + (slots[ph, 2] + slots[ph, 3])

    going = small_go(0)
    for s in sums:
        s[0].two()
    for flow in feeds:
        flow[1].end()
        flow[2].one()
    for s in sums:
        s[0].end()
        s[1].one()
    small_end(0, going)
    going = small_go(1)
    for s in sums:
        s[1].two()
    for s in sums:
        s[1].end()
        s[2].one()
    small_end(1, going)
    going = small_go(2)
    for s in sums:
        s[2].two()
    small_end(2, going)
    small_out[...] = cur[...]
    for n, (s, b) in enumerate(zip(sums, backs)):
        s[2].end()
        here = b[0].at(0)
        b[0].one(acc.at[here])
        keep(acc.at[here], out.at[(0, *here)])
    for b in backs:
        b[0].two()
    for n, b in enumerate(backs):
        b[0].end()
        kept[3 + n].wait()
        b[1].one()
    for b in backs:
        b[1].two()
    for flow in feeds:
        flow[2].two()
    for b in backs:
        b[1].end()
        b[2].one()
    token_out[...] = (
        resid_ref[...]
        + nt(dq_ref[...], wq[...].reshape(D, D))
        + nt(dk_ref[...], wk[...].reshape(D, D))
        + nt(dv_ref[...], wv[...].reshape(D, D))
    )
    for b in backs:
        b[2].two()
    for flow in (*feeds, *backs):
        flow[2].end()
    sends.finish()


def reduce_params(arrays, cid):
    scratch = [pltpu.VMEM((4, 128, D), bf16)] * 2 + [pltpu.VMEM((2, 16, 384), f32)]
    scratch += [pltpu.VMEM(THIRD, bf16)] * 2
    scratch += [pltpu.VMEM((16, 384), f32), pltpu.VMEM((4, 4, 16, 384), f32)]
    scratch += scatter_buffers(256) * 3
    count = 4 + 1 + 9 + 3 * 12 + 3 * 24
    scratch += [
        pltpu.SemaphoreType.DMA((count,)),
        pltpu.SemaphoreType.DMA((count,)),
        pltpu.SemaphoreType.DMA((6,)),
    ]
    vm = pl.BlockSpec(memory_space=pltpu.VMEM)
    return pl.pallas_call(
        reduce_kernel,
        out_shape=[
            jax.ShapeDtypeStruct((3, *THIRD), bf16),
            jax.ShapeDtypeStruct((16, 384), f32),
            jax.ShapeDtypeStruct((128, D), f32),
        ],
        in_specs=[vm] * 14,
        out_specs=[pl.BlockSpec(memory_space=pltpu.HBM), vm, vm],
        scratch_shapes=scratch,
        compiler_params=pltpu.CompilerParams(
            collective_id=cid, has_side_effects=True, vmem_limit_bytes=60 * MIB
        ),
    )(*arrays)


def finish_kernel(big_ref, q_ref, k_ref, v_ref, o_ref, up_ref, down_ref):
    for n, ref in enumerate((q_ref, k_ref, v_ref, o_ref)):
        ref[...] = big_ref[0, n].astype(f32)
        up_ref[:, n * 768 : (n + 1) * 768] = big_ref[1, n].astype(f32)
        down_ref[n] = big_ref[2, n].astype(f32)


def finish(big):
    mat = pl.BlockSpec((96, 768), lambda r: (r, 0))
    return pl.pallas_call(
        finish_kernel,
        grid=(4,),
        out_shape=[jax.ShapeDtypeStruct((384, 768), f32)] * 4
        + [
            jax.ShapeDtypeStruct((384, 3072), f32),
            jax.ShapeDtypeStruct((4, 384, 768), f32),
        ],
        in_specs=[pl.BlockSpec((3, 4, 96, 768), lambda r: (0, 0, r, 0))],
        out_specs=[mat] * 4
        + [
            pl.BlockSpec((96, 3072), lambda r: (r, 0)),
            pl.BlockSpec((4, 96, 768), lambda r: (0, r, 0)),
        ],
        compiler_params=pltpu.CompilerParams(vmem_limit_bytes=60 * MIB),
    )(big)


def nt(a, b):
    return lax.dot_general(a, b, (((1,), (1,)), ((), ())), preferred_element_type=f32)


def nn(a, b):
    return jnp.dot(a, b, preferred_element_type=f32)


def stacked(block):
    lane = lax.broadcasted_iota(jnp.int32, block.shape, 1) // HD
    zero = jnp.zeros_like(block)
    return jnp.concatenate([jnp.where(lane == i, block, zero) for i in range(4)], axis=0)


def unstacked(tall):
    n = tall.shape[0] // 4
    lane = lax.broadcasted_iota(jnp.int32, (n, tall.shape[1]), 1) // HD
    total = jnp.where(lane == 0, tall[:n], 0.0)
    for i in range(1, 4):
        total = total + jnp.where(lane == i, tall[i * n : (i + 1) * n], 0.0)
    return total


def as_rows(column):
    wide = jnp.broadcast_to(column, (column.shape[0], 128))
    return jnp.concatenate(
        [wide[i * 128 : (i + 1) * 128].T[:1] for i in range(4)] + [jnp.zeros((4, 128), f32)], axis=0
    )


TILE = 1024


def forward_kernel(q_ref, k_ref, v_ref, bias_ref, attn_ref, lse_ref, rows_ref, score):
    q = stacked(q_ref[...] * jnp.asarray(0.125, bf16))
    top = None
    for t in range(4096 // TILE):
        at = pl.ds(t * TILE, TILE)
        s = nt(q, k_ref[at, :]) + bias_ref[:, at]
        score[:, at] = s
        m = jnp.max(s, axis=-1, keepdims=True)
        top = m if top is None else jnp.maximum(top, m)
    total, out = 0.0, 0.0
    for t in range(4096 // TILE):
        at = pl.ds(t * TILE, TILE)
        p = jnp.exp(score[:, at] - top)
        total = total + jnp.sum(p, axis=-1, keepdims=True)
        out = out + nn(p.astype(bf16), v_ref[at, :])
    attn_ref[...] = unstacked(out * (1.0 / total))
    lse = top + jnp.log(total)
    lse_ref[0] = jnp.broadcast_to(lse, (512, 128))
    rows_ref[0] = as_rows(lse)


def attend(q, k, v, bias):
    wide = pl.BlockSpec((4096, 256), lambda g: (0, g))
    own = pl.BlockSpec((128, 256), lambda g: (0, g))
    return pl.pallas_call(
        forward_kernel,
        grid=(3,),
        out_shape=[
            jax.ShapeDtypeStruct((128, D), f32),
            jax.ShapeDtypeStruct((3, 512, 128), f32),
            jax.ShapeDtypeStruct((3, 8, 128), f32),
        ],
        in_specs=[own, wide, wide, pl.BlockSpec((1, 4096), lambda g: (0, 0))],
        out_specs=[
            own,
            pl.BlockSpec((1, 512, 128), lambda g: (g, 0, 0)),
            pl.BlockSpec((1, 8, 128), lambda g: (g, 0, 0)),
        ],
        scratch_shapes=[pltpu.VMEM((512, 4096), f32)],
        compiler_params=pltpu.CompilerParams(vmem_limit_bytes=60 * MIB),
    )(q, k, v, bias)


FC = 768


def norm_parts(resid):
    centre = resid - jnp.mean(resid, axis=-1, keepdims=True)
    spread = jnp.mean(centre * centre, axis=-1, keepdims=True)
    scale = lax.rsqrt(spread + 1e-12)
    return centre * scale, scale


def norm_back(grad, norm, scale):
    return scale * (
        grad
        - jnp.mean(grad, axis=-1, keepdims=True)
        - norm * jnp.mean(grad * norm, axis=-1, keepdims=True)
    )


def middle_kernel(
    attn_ref, x_ref, cot_ref, vec_ref, wo_hbm, wup_hbm, wdown_hbm,
    result_ref, resid_ref, mixed_grad_ref, mixed_ref, first_ref, act_ref, pre_grad_ref,
    down_grad_ref, branch_ref, small_ref,
    wo, wup, wdown, slope, arrive,
):
    copies = []
    for n, (src, dst) in enumerate(((wo_hbm, wo), (wup_hbm, wup), (wdown_hbm, wdown))):
        copy = pltpu.make_async_copy(src, dst, arrive.at[n])
        copy.start()
        copies.append(copy)

    def row(i):
        return jnp.concatenate([vec_ref[c, i : i + 1] for c in range(2)], axis=1).astype(f32)

    def put(i, value):
        for c in range(2):
            small_ref[c, i : i + 1, :] = value[:, c * 384 : (c + 1) * 384]

    def down(value):
        return jnp.sum(value, axis=0, keepdims=True)

    mixed = attn_ref[...].astype(bf16)
    mixed_ref[...] = mixed
    copies[0].wait()
    resid = x_ref[...].astype(f32) + nn(mixed, wo[...].reshape(D, D)) + row(2)
    norm_one, scale_one = norm_parts(resid)
    gain_one = row(3)
    first = norm_one * gain_one + row(4)
    first_low = first.astype(bf16)
    first_ref[...] = first_low
    copies[1].wait()
    copies[2].wait()
    total = first + row(5)
    for j in range(4):
        cols = slice(j * FC, (j + 1) * FC)
        bias = jnp.concatenate(
            [vec_ref[j // 2, 8 + 2 * (j % 2) + k : 9 + 2 * (j % 2) + k] for k in range(2)], axis=1
        ).astype(f32)
        pre = nn(first_low, wup[:, :, cols].reshape(D, FC)) + bias
        phi = 0.5 * (1.0 + lax.erf(pre * (0.5**0.5)))
        slope[:, cols] = phi + pre * jnp.exp(-0.5 * pre * pre) * (1.0 / math.sqrt(2.0 * math.pi))
        act = (pre * phi).astype(bf16)
        act_ref[:, cols] = act
        total = total + nn(act, wdown[j // 2, (j % 2) * FC : (j % 2 + 1) * FC, :])
    norm_two, scale_two = norm_parts(total)
    gain_two = row(6)
    result_ref[...] = (norm_two * gain_two + row(7)).astype(bf16)
    cot = cot_ref[...].astype(f32)
    put(6, down(cot * norm_two))
    put(7, down(cot))
    grad_two = norm_back(cot * gain_two, norm_two, scale_two)
    put(5, down(grad_two))
    grad_down = grad_two.astype(bf16)
    down_grad_ref[...] = grad_down
    grad_first = grad_two
    for j in range(4):
        cols = slice(j * FC, (j + 1) * FC)
        grad_act = nt(grad_down, wdown[j // 2, (j % 2) * FC : (j % 2 + 1) * FC, :])
        grad_pre = (grad_act * slope[:, cols]).astype(bf16)
        pre_grad_ref[:, cols] = grad_pre
        sums = down(grad_pre.astype(f32))
        for k in range(2):
            i = 8 + 2 * (j % 2) + k
            small_ref[j // 2, i : i + 1, :] = sums[:, k * 384 : (k + 1) * 384]
        grad_first = grad_first + nt(grad_pre, wup[:, :, cols].reshape(D, FC))
    put(3, down(grad_first * norm_one))
    put(4, down(grad_first))
    grad_one = norm_back(grad_first * gain_one, norm_one, scale_one)
    resid_ref[...] = grad_one
    put(2, down(grad_one))
    branch = grad_one.astype(bf16)
    branch_ref[...] = branch
    mixed_grad_ref[...] = nt(branch, wo[...].reshape(D, D)).astype(bf16)
    zero = jnp.zeros((1, D), f32)
    put(0, zero)
    put(1, zero)
    for c in range(2):
        small_ref[c, 12:16, :] = jnp.zeros((4, 384), f32)


def middle(attn, x, cot, vecs, wo, wup, wdown):
    vm = pl.BlockSpec(memory_space=pltpu.VMEM)
    hbm = pl.BlockSpec(memory_space=pltpu.HBM)
    thin, wide = jax.ShapeDtypeStruct((128, D), bf16), jax.ShapeDtypeStruct((128, 3072), bf16)
    return pl.pallas_call(
        middle_kernel,
        out_shape=[
            thin, jax.ShapeDtypeStruct((128, D), f32), thin, thin, thin, wide, wide, thin, thin,
            jax.ShapeDtypeStruct((2, 16, 384), f32),
        ],
        in_specs=[vm] * 4 + [hbm] * 3,
        out_specs=[vm] * 10,
        scratch_shapes=[
            pltpu.VMEM(wo.shape, bf16),
            pltpu.VMEM(wup.shape, bf16),
            pltpu.VMEM(wdown.shape, bf16),
            pltpu.VMEM((128, 3072), f32),
            pltpu.SemaphoreType.DMA((3,)),
        ],
        compiler_params=pltpu.CompilerParams(vmem_limit_bytes=60 * MIB),
    )(attn, x, cot, vecs, wo, wup, wdown)


def back_kernel(
    q_hbm, k_hbm, v_hbm, g_in, attn_ref, lse_ref, rows_ref, bias_ref,
    first_ref, pre_grad_ref, act_ref, down_grad_ref, dq_ref, dk_ref, dv_ref, chunk_0, chunk_1, chunk_2,
    qv, kv, vv, gv, stats, stat_own, q_own, k_own, v_own, g_own, delta, dq_acc, dk_acc, dv_acc,
    acc, twins, *rest
):
    bufs, (send, recv, local) = rest[:27], rest[27:]
    sends = Sends(send, recv)
    y, z, x = (lax.axis_index(a) for a in CTX)
    core = lax.axis_index("wsh")
    meet([sibling(), far()] + [away(a, k) for a in ROUNDS for k in (1, -1)])
    loads = []
    for n, (src, dst) in enumerate(
        ((k_hbm, kv), (v_hbm, vv), (q_hbm, qv))
    ):
        copy = pltpu.make_async_copy(src, dst, local.at[n])
        copy.start()
        loads.append(copy)
    eighth = jnp.asarray(0.125, bf16)
    low = lax.broadcasted_iota(jnp.int32, (4, 128), 1) < 64
    stat_own[...] = jnp.zeros_like(stat_own)
    for n in range(3):
        cols = pl.ds(n * 256, 256)
        g = stacked(g_in[:, cols])
        g_own[n] = g
        tall = jnp.concatenate([attn_ref[:, cols]] * 4, axis=0)
        d = jnp.sum(g.astype(f32) * tall, axis=-1, keepdims=True)
        delta[n] = jnp.broadcast_to(d, (512, 128))
        d = as_rows(d)[:4]
        lse = rows_ref[n][:4]
        stat_own[pl.ds(4 * n, 4), :] = jnp.where(low, lse, pltpu.roll(d, 64, 1))
        stat_own[pl.ds(16 + 4 * n, 4), :] = jnp.where(low, pltpu.roll(lse, 64, 1), d)
        dq_acc[n] = jnp.zeros((512, 256), f32)
        dk_acc[n] = jnp.zeros((512, 256), f32)
        dv_acc[n] = jnp.zeros((512, 256), f32)
    ins, outs = [g_in, stat_own], [gv, stats]
    crossing = [sends.start(i, o.at[y, z, x], far()) for i, o in zip(ins, outs)]
    mine = Flow(sends, ins, outs, y, True)
    theirs = Flow(sends, ins, outs, 1 - y, False)
    mine.first()
    own = []
    for n, (i, o) in enumerate(zip(ins, outs)):
        copy = pltpu.make_async_copy(i, o.at[y, z, x], local.at[3 + n])
        copy.start()
        own.append(copy)
    for copy in loads:
        copy.wait()
    for n in range(3):
        cols = pl.ds(n * 256, 256)
        q_own[n] = stacked(qv[y, z, x, :, cols] * eighth)
        k_own[n] = stacked(kv[y, z, x, :, cols] * eighth)
        v_own[n] = stacked(vv[y, z, x, :, cols])

    def queries(lo, hi):
        @pl.loop(lo, hi)
        def _(c):
            n, t = c // 4, c % 4
            cols = pl.ds(pl.multiple_of(n * 256, 256), 256)
            k = kv[t // 2, pl.ds(2 * (t % 2), 2), :, :, cols].reshape(TILE, 256)
            v = vv[t // 2, pl.ds(2 * (t % 2), 2), :, :, cols].reshape(TILE, 256)
            bias = bias_ref[:, pl.ds(pl.multiple_of(t * TILE, TILE), TILE)]
            p = jnp.exp(nt(q_own[n], k) + bias - lse_ref[n][:, :1])
            dp = nt(g_own[n], v)
            ds = (p * (dp - delta[n][:, :1])).astype(bf16)
            dq_acc[n] = dq_acc[n] + nn(ds, k)

    low16 = lax.broadcasted_iota(jnp.int32, (16, 128), 1) < 64

    def keys(unit):
        half, layer, i = unit
        r = 0 if half == "A" else 64
        if half == "A":
            st = stats[layer, i, :, pl.ds(0, 16)]
        else:
            st = stats[layer, :, i, pl.ds(16, 16)]
        turned = [pltpu.roll(st[b], 64, 1) for b in range(4)]
        lse = jnp.concatenate(
            [jnp.where(low16, st[b], turned[b + 1]) for b in (0, 2)], axis=1
        )
        dlt = jnp.concatenate(
            [jnp.where(low16, turned[b], st[b + 1]) for b in (0, 2)], axis=1
        )
        for n in range(3):
            cols = pl.ds(n * 256, 256)
            if half == "A":
                at = (layer, i, slice(None), pl.ds(0, 64), cols)
            else:
                at = (layer, slice(None), i, pl.ds(64, 64), cols)
            q, g = qv[at].reshape(256, 256), gv[at].reshape(256, 256)

            def spread(rows):
                return jnp.concatenate(
                    [jnp.broadcast_to(rows[4 * n + h : 4 * n + h + 1], (128, 256)) for h in range(4)],
                    axis=0,
                )

            p = jnp.exp(nt(k_own[n], q) - spread(lse))
            ds = (p * (nt(v_own[n], g) - spread(dlt))).astype(bf16)
            dv_acc[n] = dv_acc[n] + nn(p.astype(bf16), g)
            dk_acc[n] = dk_acc[n] + nn(ds, q)

    def product(s, m, half, lo, width):
        if s == 0:
            value = tn(
                first_ref[:, pl.ds(pl.multiple_of(half * 384, 384), 384)],
                pre_grad_ref[:, pl.ds(pl.multiple_of(m * 768, 768), 768)],
            )
        else:
            value = tn(
                act_ref[:, pl.ds(pl.multiple_of(half * 1536 + m * 384, 384), 384)],
                down_grad_ref[:, lo : lo + width],
            )
        return value.reshape(4, 2, 48, width)

    flights = {}
    order = {}
    for n, (s, axes, lo, width) in enumerate(FEED):
        for k in range(4):
            order[n, k] = lax.rem(place(axes[0]) + k, 4)
    for k in (2, 1, 3, 0):
        for n, (s, axes, lo, width) in enumerate(FEED):
            m, cols = order[n, k], pl.ds(lo, width)
            twins[s, m, :, :, :, cols] = product(s, m, 1 - core, lo, width).astype(bf16)
            flights[n, k] = sends.start(
                twins.at[s, m, :, :, :, cols], acc.at[s, m, :, :, :, cols], sibling()
            )

    def settle(k):
        for n, (s, axes, lo, width) in enumerate(FEED):
            m, cols = order[n, k], pl.ds(lo, width)
            value = product(s, m, core, lo, width)
            flights[n, k].wait_recv()
            total = value + acc[s, m, :, :, :, cols].astype(f32)
            acc[s, m, :, :, :, cols] = total.astype(bf16)

    sums = [
        scatters(Part(sends, axes, lo, width), acc.at[s], bufs[9 * n : 9 * n + 9])
        for n, (s, axes, lo, width) in enumerate(FEED)
    ]

    def step(ph, name):
        for s in sums:
            getattr(s[ph], name)()

    mine.first_on()
    for copy in crossing:
        copy.wait_recv()
    theirs.first()
    settle(2)
    step(0, "one")
    queries(0, 2)
    for copy in own:
        copy.wait()
    mine.second()
    theirs.first_on()
    settle(1)
    settle(3)
    queries(2, 4)
    step(0, "two")
    queries(4, 8)
    for unit in units(y, (0,)):
        keys(unit)
    mine.second_on()
    theirs.second()
    settle(0)
    for unit in units(y, (1, -1)):
        keys(unit)
    queries(8, 10)
    step(0, "end")
    step(1, "one")
    mine.wait()
    for unit in units(y, (2,)):
        keys(unit)
    step(1, "two")
    theirs.second_on()
    queries(10, 12)
    for unit in units(1 - y, (0,)):
        keys(unit)
    step(1, "end")
    step(2, "one")
    for n in range(3):
        dq_ref[:, pl.ds(n * 256, 256)] = (unstacked(dq_acc[n]) * 0.125).astype(bf16)
    for unit in units(1 - y, (1, -1)):
        keys(unit)
    step(2, "two")
    theirs.wait()
    for unit in units(1 - y, (2,)):
        keys(unit)
    step(2, "end")
    for s, ref in zip(sums, (chunk_0, chunk_1, chunk_2)):
        ref[...] = s[2].acc[s[2].at(0)]
    at = pl.multiple_of(((y * 4 + z) * 4 + x) * 128, 128)
    keep = jnp.broadcast_to(bias_ref[:, pl.ds(at, 128)], (128, 128)).T[:, :1] > -1.0
    for n in range(3):
        cols = pl.ds(n * 256, 256)
        dk_ref[:, cols] = jnp.where(keep, unstacked(dk_acc[n]) * 0.125, 0.0).astype(bf16)
        dv_ref[:, cols] = jnp.where(keep, unstacked(dv_acc[n]), 0.0).astype(bf16)
    sends.finish()


def attend_back(q, k, v, g, attn, lse, lse_rows, bias, extra, cid):
    n_send = 33 * 2 + 12 + 36
    vm = pl.BlockSpec(memory_space=pltpu.VMEM)
    wide = pltpu.VMEM((2, 4, 4, 128, D), bf16)
    tall = pltpu.VMEM((3, 512, 256), bf16)
    sums = pltpu.VMEM((3, 512, 256), f32)
    return pl.pallas_call(
        back_kernel,
        out_shape=[jax.ShapeDtypeStruct((128, D), bf16)] * 3
        + [jax.ShapeDtypeStruct((1, 1, 1, 48, f[3] // 2), bf16) for f in FEED],
        in_specs=[pl.BlockSpec(memory_space=pltpu.HBM)] * 3 + [vm] * 9,
        out_specs=[vm] * 6,
        scratch_shapes=[wide] * 4
        + [pltpu.VMEM((2, 4, 4, 32, 128), f32), pltpu.VMEM((32, 128), f32)]
        + [tall] * 4
        + [pltpu.VMEM((3, 512, 128), f32)]
        + [sums] * 3
        + [pltpu.VMEM((2, *THIRD), bf16)] * 2
        + [b for f in FEED for b in scatter_buffers(f[3])]
        + [
            pltpu.SemaphoreType.DMA((n_send,)),
            pltpu.SemaphoreType.DMA((n_send,)),
            pltpu.SemaphoreType.DMA((5,)),
        ],
        compiler_params=pltpu.CompilerParams(
            collective_id=cid, has_side_effects=True, vmem_limit_bytes=60 * MIB
        ),
    )(q, k, v, g, attn, lse, lse_rows, bias, *extra)


def local(
    tokens, lengths, w_query, b_query, w_key, w_value, b_value, w_out, b_out, gain_one, shift_one,
    w_up, b_up, w_down, b_down, gain_two, shift_two, cotangent,
):
    inputs = tokens[0]
    all_q, all_k, all_v, wq, wk, wv, wo, wup, wdown, vecs, q = start(
        inputs,
        [w_query, w_key, w_value, w_out, w_up, w_down],
        [b_query, b_value, b_out, gain_one, shift_one, b_down, gain_two, shift_two, b_up],
        0,
    )
    bias = jnp.where(jnp.arange(4096) < lengths[0], 0.0, -1e30).astype(f32)[None]
    attn, lse, lse_rows = attend(q, all_k.reshape(4096, D), all_v.reshape(4096, D), bias)
    (
        result, grad_resid, grad_mixed, mixed, first, act, grad_pre, grad_down, branch, small
    ) = middle(attn, inputs, cotangent[0], vecs, wo, wup, wdown)
    dq, dk, dv, *chunks = attend_back(
        all_q, all_k, all_v, grad_mixed, attn, lse, lse_rows, bias,
        [first, grad_pre, act, grad_down], 1,
    )
    big, small, grad_inputs = reduce_params(
        [
            inputs, mixed, dq, dk, dv, branch, grad_resid, wq, wk, wv,
            *chunks, small,
        ],
        2,
    )
    tot_wq, tot_wk, tot_wv, tot_wo, tot_wup, tot_wdown = finish(
        big.reshape(3, 4, 384, D)
    )
    tot_bq, tot_bv, tot_bo, tot_gone, tot_sone, tot_bdown, tot_gtwo, tot_stwo = (
        small[i] for i in range(8)
    )
    return (
        result[None],
        grad_inputs[None],
        tot_wq,
        tot_bq,
        tot_wk,
        tot_wv,
        tot_bv,
        tot_wo,
        tot_bo,
        tot_gone,
        tot_sone,
        tot_wup,
        small[8:12].reshape(1536),
        tot_wdown.reshape(1536, 768),
        tot_bdown,
        tot_gtwo,
        tot_stwo,
    )


def solution(mesh):
    split = Mesh(
        mesh.devices.reshape(mesh.shape["seq"], 2, 4, 4, mesh.shape["wsh"]),
        ("seq", "ctx_0", "ctx_1", "ctx_2", "wsh"),
    )
    rows = P(("seq", "wsh"), CTX, None)
    mat, vec = P("wsh", None), P("wsh")
    params = (mat, vec, mat, mat, vec, mat, vec, vec, vec, mat, vec, mat, vec, vec, vec)
    return jax.shard_map(
        local,
        mesh=split,
        in_specs=(rows, P(("seq", "wsh")), *params, rows),
        out_specs=(rows, rows, *params),
        check_vma=False,
    )
```

```python
import functools
import math

import jax
import jax.numpy as jnp
from jax import lax
from jax.experimental import pallas as pl
from jax.experimental.pallas import tpu as pltpu
from jax.sharding import Mesh
from jax.sharding import PartitionSpec as P

H = 12
HD = 64
D = 768
CTX = ("ctx_0", "ctx_1", "ctx_2")
f32 = jnp.float32
bf16 = jnp.bfloat16
MESH = pl.DeviceIdType.MESH
ANY = pl.ANY
MIB = 1024 * 1024


def place(axis):
    if axis == "x":
        return lax.axis_index("ctx_2")
    if axis == "z":
        return lax.axis_index("ctx_1")
    return lax.axis_index("ctx_0") * 2 + lax.axis_index("seq")


def away(axis, step):
    at = lax.rem(place(axis) + step + 4, 4)
    if axis == "x":
        return {"ctx_2": at}
    if axis == "z":
        return {"ctx_1": at}
    return {"ctx_0": at // 2, "seq": lax.rem(at, 2)}


def sibling():
    return {"wsh": 1 - lax.axis_index("wsh")}


def far():
    return {"ctx_0": 1 - lax.axis_index("ctx_0")}


def meet(devices):
    barrier = pltpu.get_barrier_semaphore()
    for d in devices:
        pl.semaphore_signal(barrier, inc=1, device_id=d, device_id_type=MESH)
    pl.semaphore_wait(barrier, len(devices))


class Sends:
    def __init__(self, send, recv):
        self.send, self.recv, self.used, self.all = send, recv, 0, []

    def start(self, src, dst, device):
        k = self.used
        self.used += 1
        copy = pltpu.make_async_remote_copy(
            src_ref=src,
            dst_ref=dst,
            send_sem=self.send.at[k],
            recv_sem=self.recv.at[k],
            device_id=device,
            device_id_type=MESH,
        )
        copy.start()
        self.all.append(copy)
        return copy

    def finish(self):
        for copy in self.all:
            copy.wait_send()


class Flow:
    def __init__(self, sends, ins, outs, layer, mine):
        self.sends, self.ins, self.outs, self.layer, self.mine = sends, ins, outs, layer, mine
        self.z, self.x = lax.axis_index("ctx_1"), lax.axis_index("ctx_2")
        self.flights = []

    def wait(self):
        for pair in self.flights:
            for copy in pair:
                copy.wait_recv()

    def near(self, axis):
        pos = place(axis)
        return lax.rem(pos + 3, 4), lax.rem(pos + 1, 4)

    def first(self):
        y, z, x = self.layer, self.z, self.x
        self.flights = []
        for i, o in zip(self.ins, self.outs):
            h = i.shape[0] // 2
            for axis, lo in (("x", 0), ("z", h)):
                src = i.at[pl.ds(lo, h)] if self.mine else o.at[y, z, x, pl.ds(lo, h)]
                dst = o.at[y, z, x, pl.ds(lo, h)]
                self.flights.append(
                    [self.sends.start(src, dst, away(axis, k)) for k in (1, -1)]
                )

    def first_on(self):
        y, z, x, at, later = self.layer, self.z, self.x, 0, []
        for i, o in zip(self.ins, self.outs):
            q = i.shape[0] // 4
            for axis, lo in (("x", 0), ("z", 2 * q)):
                right, left = self.flights[at]
                at += 1
                before, after = self.near(axis)
                if axis == "x":
                    a = o.at[y, z, before, pl.ds(lo, q)]
                    b = o.at[y, z, after, pl.ds(lo + q, q)]
                else:
                    a = o.at[y, before, x, pl.ds(lo, q)]
                    b = o.at[y, after, x, pl.ds(lo + q, q)]
                right.wait_recv()
                up = self.sends.start(a, a, away(axis, 1))
                left.wait_recv()
                later.append([up, self.sends.start(b, b, away(axis, -1))])
        self.flights = later

    def second(self):
        y, z, x, at, later = self.layer, self.z, self.x, 0, []
        for i, o in zip(self.ins, self.outs):
            h = i.shape[0] // 2
            for axis, lo in (("z", 0), ("x", h)):
                for copy in self.flights[at]:
                    copy.wait_recv()
                at += 1
                a = o.at[y, z, :, pl.ds(lo, h)] if axis == "z" else o.at[y, :, x, pl.ds(lo, h)]
                later.append([self.sends.start(a, a, away(axis, k)) for k in (1, -1)])
        self.flights = later

    def second_on(self):
        y, at, later = self.layer, 0, []
        for i, o in zip(self.ins, self.outs):
            h = i.shape[0] // 2
            for axis, lo in (("z", 0), ("x", h)):
                right, left = self.flights[at]
                at += 1
                before, after = self.near(axis)
                if axis == "z":
                    a = o.at[y, before, pl.ds(0, 2), pl.ds(lo, h)]
                    b = o.at[y, after, pl.ds(2, 2), pl.ds(lo, h)]
                else:
                    a = o.at[y, pl.ds(0, 2), before, pl.ds(lo, h)]
                    b = o.at[y, pl.ds(2, 2), after, pl.ds(lo, h)]
                right.wait_recv()
                up = self.sends.start(a, a, away(axis, 1))
                left.wait_recv()
                later.append([up, self.sends.start(b, b, away(axis, -1))])
        self.flights = later


def units(layer, steps):
    z, x = lax.axis_index("ctx_1"), lax.axis_index("ctx_2")
    picked = []
    for k in steps:
        picked.append(("A", layer, lax.rem(z + k + 4, 4)))
        picked.append(("B", layer, lax.rem(x + k + 4, 4)))
    return picked


def unit_at(unit):
    half, layer, i = unit
    if half == "A":
        return (layer, i, slice(None), pl.ds(0, 64))
    return (layer, slice(None), i, pl.ds(64, 64))


def start_kernel(*refs):
    x_in, vectors = refs[0], refs[7:16]
    outs, pair_outs, q_out = refs[16:19], refs[19:26], refs[26]
    xs, held, made, packed = refs[27], refs[28:35], refs[35:38], refs[38]
    send, recv, local, leave = refs[39:]
    pair_ins = (*refs[1:7], packed)
    sends = Sends(send, recv)
    y, z, x = (lax.axis_index(a) for a in CTX)
    core = lax.axis_index("wsh")
    meet(
        [away("x", 1), away("x", -1), away("z", 1), away("z", -1), far(), sibling()]
    )
    crossing = sends.start(x_in, xs.at[y, z, x], far())
    packed[...] = jnp.zeros_like(packed)
    for n, ref in enumerate(vectors):
        value = ref[...].astype(f32).reshape(1, -1)
        for k in range(value.shape[1] // 384):
            packed[n + k : n + k + 1, :] = value[:, k * 384 : (k + 1) * 384]
    mine = Flow(sends, [x_in], [xs], y, True)
    theirs = Flow(sends, [x_in], [xs], 1 - y, False)
    mine.first()
    own = pltpu.make_async_copy(x_in, xs.at[y, z, x], local.at[7])
    own.start()
    pairs, kept, left = [], [], []
    for n, (i, o) in enumerate(zip(pair_ins, held)):
        pairs.append(sends.start(i, o.at[core], sibling()))
        copy = pltpu.make_async_copy(i, o.at[core], local.at[n])
        copy.start()
        kept.append(copy)

    def depart(src, dst):
        copy = pltpu.make_async_copy(src, dst, leave.at[len(left)])
        copy.start()
        left.append(copy)

    def whole(n):
        kept[n].wait()
        pairs[n].wait_recv()
        depart(held[n], pair_outs[n])

    def project(unit):
        at = unit_at(unit)
        block = xs[at].reshape(256, D)
        for n, row in ((0, 0), (1, None), (2, 1)):
            value = nn(block, held[n][...].reshape(D, D))
            if row is not None:
                value = value + jnp.concatenate(
                    [held[6][c, row : row + 1] for c in range(2)], axis=1
                ).astype(f32)
            made[n][at] = value.astype(bf16).reshape(4, 64, D)
            depart(made[n].at[at], outs[n].at[at])

    mine.first_on()
    crossing.wait_recv()
    theirs.first()
    own.wait()
    mine.second()
    theirs.first_on()
    for n in (6, 0, 1, 2):
        whole(n)
    for unit in units(y, (0,)):
        project(unit)
    mine.second_on()
    theirs.second()
    for unit in units(y, (1, -1)):
        project(unit)
    mine.wait()
    for unit in units(y, (2,)):
        project(unit)
    for unit in units(1 - y, (0,)):
        project(unit)
    theirs.second_on()
    for n in (3, 4, 5):
        whole(n)
    for unit in units(1 - y, (1, -1)):
        project(unit)
    theirs.wait()
    for unit in units(1 - y, (2,)):
        project(unit)
    depart(made[0].at[y, z, x], q_out)
    for copy in left:
        copy.wait()
    sends.finish()


def start(block, pairs, vectors, cid):
    packed = jax.ShapeDtypeStruct((16, 384), f32)
    lands = [*pairs, packed]
    n_send = 1 + 32 + 7
    return pl.pallas_call(
        start_kernel,
        out_shape=[jax.ShapeDtypeStruct((2, 4, 4, 128, D), bf16)] * 3
        + [jax.ShapeDtypeStruct((2, *a.shape), a.dtype) for a in lands]
        + [jax.ShapeDtypeStruct((128, D), bf16)],
        in_specs=[pl.BlockSpec(memory_space=pltpu.HBM)] * 7
        + [pl.BlockSpec(memory_space=pltpu.VMEM)] * 9,
        out_specs=[pl.BlockSpec(memory_space=pltpu.HBM)] * 11,
        scratch_shapes=[pltpu.VMEM((2, 4, 4, 128, D), bf16)]
        + [pltpu.VMEM((2, *a.shape), a.dtype) for a in lands]
        + [pltpu.VMEM((2, 4, 4, 128, D), bf16)] * 3
        + [pltpu.VMEM(packed.shape, f32)]
        + [
            pltpu.SemaphoreType.DMA((n_send,)),
            pltpu.SemaphoreType.DMA((n_send,)),
            pltpu.SemaphoreType.DMA((8,)),
            pltpu.SemaphoreType.DMA((16 * 3 + 8,)),
        ],
        compiler_params=pltpu.CompilerParams(
            collective_id=cid, has_side_effects=True, vmem_limit_bytes=60 * MIB
        ),
    )(block, *pairs, *vectors)


ORDERS = (("x", "y", "z"), ("y", "z", "x"), ("z", "x", "y"))
AXES = ("x", "y", "z")
SPLIT = ((192, 192), (48, 48), (32, 16))
CHUNK = ((384, 768), (96, 768), (48, 384))


def tn(a, b):
    return lax.dot_general(a, b, (((0,), (0,)), ((), ())), preferred_element_type=f32)


def reduce_kernel(
    x_ref, mixed_ref, dq_ref, dk_ref, dv_ref, branch_ref, resid_ref, wq, wk, wv,
    first, grad_pre, act, grad_down, small_in, out, small_out, token_out,
    left, right, small, acc, twins, pair, t0, t1, t2, u0, u1, u2, cur, slots, send, recv, local,
):
    core = lax.axis_index("wsh")
    twin = 1 - core
    sends = Sends(send, recv)
    tt, uu = (t0, t1, t2), (u0, u1, u2)
    pos = {a: place(a) for a in AXES}
    meet([sibling()] + [away(a, k) for a in AXES for k in (1, 2, 3)])

    def product(s, m, half):
        if s == 0:
            return tn(left[m, :, pl.ds(pl.multiple_of(half * 384, 384), 384)], right[m])
        if s == 1:
            return tn(
                first[:, pl.ds(pl.multiple_of(half * 384, 384), 384)],
                grad_pre[:, pl.ds(pl.multiple_of(m * 768, 768), 768)],
            )
        return tn(
            act[:, pl.ds(pl.multiple_of(half * 1536 + m * 384, 384), 384)], grad_down[...]
        )

    for m in range(4):
        left[m] = (mixed_ref if m == 3 else x_ref)[...]
        right[m] = (dq_ref, dk_ref, dv_ref, branch_ref)[m][...]
    small[...] = small_in[...]
    for n, ref in enumerate((dq_ref, dv_ref)):
        sums = jnp.sum(ref[...].astype(f32), axis=0, keepdims=True)
        for c in range(2):
            small[c, n : n + 1, :] = sums[:, c * 384 : (c + 1) * 384]
    small_pair = sends.start(small.at[twin], slots.at[3, 0], sibling())
    turns = [(s, k) for k in (2, 1, 3, 0) for s in range(3)]
    block = {(s, k): lax.rem(pos[ORDERS[s][0]] + k, 4) for s, k in turns}
    flights = {}
    for s, k in turns:
        m = block[s, k]
        twins[s, m] = product(s, m, twin).astype(bf16)
        flights[s, k] = sends.start(twins.at[s, m], pair.at[s, m], sibling())
    small_pair.wait_recv()
    cur[...] = small[core] + slots[3, 0]

    def own(s, k):
        m = block[s, k]
        mine = product(s, m, core)
        flights[s, k].wait_recv()
        acc[s, m] = (mine + pair[s, m].astype(f32)).astype(bf16)

    def add(dst, dst_at, src, src_at, shape):
        rows, cols = shape

        @pl.loop(0, rows // 16)
        def _(k):
            a = dst_at(pl.multiple_of(k * 16, 16))
            b = src_at(pl.multiple_of(k * 16, 16))
            dst[a] = (dst[a].astype(f32) + src[b].astype(f32)).astype(bf16)

    def region(ph, s, c, r, n):
        a, b, _ = (pos[k] for k in ORDERS[s])
        if ph == 0:
            return (s, c, pl.ds(r, n))
        if ph == 1:
            return (s, a, pl.ds(pl.multiple_of(96 * c + r, 16), n))
        return (
            s, a, pl.ds(pl.multiple_of(96 * b + 48 * (c // 2) + r, 16), n),
            pl.ds(pl.multiple_of(lax.rem(c, 2) * 384, 384), 384),
        )

    for ph in range(3):
        axis = AXES[ph]
        slots[ph, pos[axis]] = cur[...]
        rows, cols = CHUNK[ph]
        near, rest = SPLIT[ph]
        steps = []
        for s in range(3):
            axis_s = ORDERS[s][ph]
            p = pos[axis_s]
            c = lax.rem(p + 2, 4)
            if ph == 0:
                own(s, 2)
            steps.append((
                sends.start(
                    acc.at[region(ph, s, c, 0, near)], tt[ph].at[s, 0, pl.ds(0, near)], away(axis_s, 1)
                ),
                sends.start(
                    acc.at[region(ph, s, c, near, rest)], tt[ph].at[s, 1, pl.ds(0, rest)], away(axis_s, -1)
                ),
            ))
        small_axis = [
            sends.start(cur, slots.at[ph, pos[axis]], away(axis, k)) for k in (1, 2, 3)
        ]
        nexts = []
        for s in range(3):
            axis_s = ORDERS[s][ph]
            p = pos[axis_s]
            up, down = lax.rem(p + 1, 4), lax.rem(p + 3, 4)
            if ph == 0:
                own(s, 1)
            steps[s][0].wait_recv()
            add(
                acc, lambda r, s=s, up=up: region(ph, s, up, r, 16),
                tt[ph], lambda r, s=s: (s, 0, pl.ds(r, 16)), (near, cols),
            )
            a = sends.start(acc.at[region(ph, s, up, 0, rows)], uu[ph].at[s, 0], away(axis_s, 1))
            if ph == 0:
                own(s, 3)
            steps[s][1].wait_recv()
            add(
                acc, lambda r, s=s, down=down: region(ph, s, down, near + r, 16),
                tt[ph], lambda r, s=s: (s, 1, pl.ds(r, 16)), (rest, cols),
            )
            b = sends.start(acc.at[region(ph, s, down, 0, rows)], uu[ph].at[s, 1], away(axis_s, -1))
            nexts.append((a, b))
        if ph == 0:
            for s in range(3):
                own(s, 0)
            token_out[...] = (
                resid_ref[...]
                + nt(dq_ref[...], wq[...].reshape(D, D))
                + nt(dk_ref[...], wk[...].reshape(D, D))
                + nt(dv_ref[...], wv[...].reshape(D, D))
            )
        for s in range(3):
            p = pos[ORDERS[s][ph]]
            for k in range(2):
                nexts[s][k].wait_recv()
            uk = uu[ph]

            @pl.loop(0, rows // 16)
            def _(k, s=s, p=p, uk=uk):
                r = pl.multiple_of(k * 16, 16)
                a = region(ph, s, p, r, 16)
                acc[a] = (
                    acc[a].astype(f32)
                    + uk[s, 0, pl.ds(r, 16)].astype(f32)
                    + uk[s, 1, pl.ds(r, 16)].astype(f32)
                ).astype(bf16)

        for copy in small_axis:
            copy.wait()
        sends.all = [c for c in sends.all if all(c is not d for d in small_axis)]
        cur[...] = (slots[ph, 0] + slots[ph, 1]) + (slots[ph, 2] + slots[ph, 3])

    small_out[...] = cur[...]

    for ph in (2, 1, 0):
        rows, cols = CHUNK[ph]
        near, rest = SPLIT[ph]
        steps = []
        for s in range(3):
            axis_s = ORDERS[s][ph]
            p = pos[axis_s]
            here = region(ph, s, p, 0, rows)
            if ph == 2:
                kept_copy = pltpu.make_async_copy(acc.at[here], out.at[here], local.at[s])
                kept_copy.start()
                src = acc.at[here]
            else:
                kept_copy = None
                src = out.at[here]
            steps.append((
                sends.start(src, out.at[here], away(axis_s, 1)),
                sends.start(src, out.at[here], away(axis_s, -1)),
                kept_copy,
            ))
        nexts = []
        for s in range(3):
            axis_s = ORDERS[s][ph]
            p = pos[axis_s]
            up, down = lax.rem(p + 1, 4), lax.rem(p + 3, 4)
            steps[s][0].wait_recv()
            part = out.at[region(ph, s, down, 0, near)]
            a = sends.start(part, part, away(axis_s, 1))
            steps[s][1].wait_recv()
            part = out.at[region(ph, s, up, near, rest)]
            b = sends.start(part, part, away(axis_s, -1))
            nexts.append((a, b))
        for s in range(3):
            if steps[s][2] is not None:
                steps[s][2].wait()
            for copy in nexts[s]:
                copy.wait_recv()
    sends.finish()


def reduce_params(arrays, cid):
    scratch = [pltpu.VMEM((4, 128, D), bf16)] * 2 + [pltpu.VMEM((2, 16, 384), f32)]
    scratch += [pltpu.VMEM((3, 4, 384, 768), bf16)] * 3
    scratch += [pltpu.VMEM((3, 2, SPLIT[k][0], CHUNK[k][1]), bf16) for k in range(3)]
    scratch += [pltpu.VMEM((3, 2, *CHUNK[k]), bf16) for k in range(3)]
    scratch += [pltpu.VMEM((16, 384), f32), pltpu.VMEM((4, 4, 16, 384), f32)]
    count = 1 + 12 + 9 + 3 * 24
    scratch += [
        pltpu.SemaphoreType.DMA((count,)),
        pltpu.SemaphoreType.DMA((count,)),
        pltpu.SemaphoreType.DMA((3,)),
    ]
    vm = pl.BlockSpec(memory_space=pltpu.VMEM)
    return pl.pallas_call(
        reduce_kernel,
        out_shape=[
            jax.ShapeDtypeStruct((3, 4, 384, 768), bf16),
            jax.ShapeDtypeStruct((16, 384), f32),
            jax.ShapeDtypeStruct((128, D), f32),
        ],
        in_specs=[vm] * 15,
        out_specs=[pl.BlockSpec(memory_space=pltpu.HBM), vm, vm],
        scratch_shapes=scratch,
        compiler_params=pltpu.CompilerParams(
            collective_id=cid, has_side_effects=True, vmem_limit_bytes=60 * MIB
        ),
    )(*arrays)


def finish_kernel(big_ref, small_ref, q_ref, k_ref, v_ref, o_ref, up_ref, down_ref, *vectors):
    for n, ref in enumerate(vectors):
        for k in range(ref.shape[0] // 384):
            ref[k * 384 : (k + 1) * 384] = small_ref[n + k : n + k + 1, :].reshape(384)
    for n, ref in enumerate((q_ref, k_ref, v_ref, o_ref)):
        ref[...] = big_ref[0, n].astype(f32)
        up_ref[:, n * 768 : (n + 1) * 768] = big_ref[1, n].astype(f32)
        down_ref[n] = big_ref[2, n].astype(f32)


def finish(big, small):
    lengths = [384] * 8 + [1536]
    mat = pl.BlockSpec((96, 768), lambda r: (r, 0))
    return pl.pallas_call(
        finish_kernel,
        grid=(4,),
        out_shape=[jax.ShapeDtypeStruct((384, 768), f32)] * 4
        + [
            jax.ShapeDtypeStruct((384, 3072), f32),
            jax.ShapeDtypeStruct((4, 384, 768), f32),
        ]
        + [jax.ShapeDtypeStruct((n,), f32) for n in lengths],
        in_specs=[
            pl.BlockSpec((3, 4, 96, 768), lambda r: (0, 0, r, 0)),
            pl.BlockSpec((16, 384), lambda r: (0, 0)),
        ],
        out_specs=[mat] * 4
        + [
            pl.BlockSpec((96, 3072), lambda r: (r, 0)),
            pl.BlockSpec((4, 96, 768), lambda r: (0, r, 0)),
        ]
        + [pl.BlockSpec((n,), lambda r: (0,)) for n in lengths],
        compiler_params=pltpu.CompilerParams(vmem_limit_bytes=60 * MIB),
    )(big, small)


def nt(a, b):
    return lax.dot_general(a, b, (((1,), (1,)), ((), ())), preferred_element_type=f32)


def nn(a, b):
    return jnp.dot(a, b, preferred_element_type=f32)


def stacked(block):
    lane = lax.broadcasted_iota(jnp.int32, block.shape, 1) // HD
    zero = jnp.zeros_like(block)
    return jnp.concatenate([jnp.where(lane == i, block, zero) for i in range(4)], axis=0)


def unstacked(tall):
    n = tall.shape[0] // 4
    lane = lax.broadcasted_iota(jnp.int32, (n, tall.shape[1]), 1) // HD
    total = jnp.where(lane == 0, tall[:n], 0.0)
    for i in range(1, 4):
        total = total + jnp.where(lane == i, tall[i * n : (i + 1) * n], 0.0)
    return total


def as_rows(column):
    wide = jnp.broadcast_to(column, (column.shape[0], 128))
    return jnp.concatenate(
        [wide[i * 128 : (i + 1) * 128].T[:1] for i in range(4)] + [jnp.zeros((4, 128), f32)], axis=0
    )


TILE = 1024


def forward_kernel(q_ref, k_ref, v_ref, bias_ref, attn_ref, lse_ref, rows_ref, score):
    q = stacked(q_ref[...] * jnp.asarray(0.125, bf16))
    top = None
    for t in range(4096 // TILE):
        at = pl.ds(t * TILE, TILE)
        s = nt(q, k_ref[at, :]) + bias_ref[:, at]
        score[:, at] = s
        m = jnp.max(s, axis=-1, keepdims=True)
        top = m if top is None else jnp.maximum(top, m)
    total, out = 0.0, 0.0
    for t in range(4096 // TILE):
        at = pl.ds(t * TILE, TILE)
        p = jnp.exp(score[:, at] - top)
        total = total + jnp.sum(p, axis=-1, keepdims=True)
        out = out + nn(p.astype(bf16), v_ref[at, :])
    attn_ref[...] = unstacked(out * (1.0 / total))
    lse = top + jnp.log(total)
    lse_ref[0] = jnp.broadcast_to(lse, (512, 128))
    rows_ref[0] = as_rows(lse)


def attend(q, k, v, bias):
    wide = pl.BlockSpec((4096, 256), lambda g: (0, g))
    own = pl.BlockSpec((128, 256), lambda g: (0, g))
    return pl.pallas_call(
        forward_kernel,
        grid=(3,),
        out_shape=[
            jax.ShapeDtypeStruct((128, D), f32),
            jax.ShapeDtypeStruct((3, 512, 128), f32),
            jax.ShapeDtypeStruct((3, 8, 128), f32),
        ],
        in_specs=[own, wide, wide, pl.BlockSpec((1, 4096), lambda g: (0, 0))],
        out_specs=[
            own,
            pl.BlockSpec((1, 512, 128), lambda g: (g, 0, 0)),
            pl.BlockSpec((1, 8, 128), lambda g: (g, 0, 0)),
        ],
        scratch_shapes=[pltpu.VMEM((512, 4096), f32)],
        compiler_params=pltpu.CompilerParams(vmem_limit_bytes=60 * MIB),
    )(q, k, v, bias)


FC = 768


def norm_parts(resid):
    centre = resid - jnp.mean(resid, axis=-1, keepdims=True)
    spread = jnp.mean(centre * centre, axis=-1, keepdims=True)
    scale = lax.rsqrt(spread + 1e-12)
    return centre * scale, scale


def norm_back(grad, norm, scale):
    return scale * (
        grad
        - jnp.mean(grad, axis=-1, keepdims=True)
        - norm * jnp.mean(grad * norm, axis=-1, keepdims=True)
    )


def middle_kernel(
    attn_ref, x_ref, cot_ref, vec_ref, wo_hbm, wup_hbm, wdown_hbm,
    result_ref, resid_ref, mixed_grad_ref, mixed_ref, first_ref, act_ref, pre_grad_ref,
    down_grad_ref, branch_ref, small_ref,
    wo, wup, wdown, slope, arrive,
):
    copies = []
    for n, (src, dst) in enumerate(((wo_hbm, wo), (wup_hbm, wup), (wdown_hbm, wdown))):
        copy = pltpu.make_async_copy(src, dst, arrive.at[n])
        copy.start()
        copies.append(copy)

    def row(i):
        return jnp.concatenate([vec_ref[c, i : i + 1] for c in range(2)], axis=1).astype(f32)

    def put(i, value):
        for c in range(2):
            small_ref[c, i : i + 1, :] = value[:, c * 384 : (c + 1) * 384]

    def down(value):
        return jnp.sum(value, axis=0, keepdims=True)

    mixed = attn_ref[...].astype(bf16)
    mixed_ref[...] = mixed
    copies[0].wait()
    resid = x_ref[...].astype(f32) + nn(mixed, wo[...].reshape(D, D)) + row(2)
    norm_one, scale_one = norm_parts(resid)
    gain_one = row(3)
    first = norm_one * gain_one + row(4)
    first_low = first.astype(bf16)
    first_ref[...] = first_low
    copies[1].wait()
    copies[2].wait()
    total = first + row(5)
    for j in range(4):
        cols = slice(j * FC, (j + 1) * FC)
        bias = jnp.concatenate(
            [vec_ref[j // 2, 8 + 2 * (j % 2) + k : 9 + 2 * (j % 2) + k] for k in range(2)], axis=1
        ).astype(f32)
        pre = nn(first_low, wup[:, :, cols].reshape(D, FC)) + bias
        phi = 0.5 * (1.0 + lax.erf(pre * (0.5**0.5)))
        slope[:, cols] = phi + pre * jnp.exp(-0.5 * pre * pre) * (1.0 / math.sqrt(2.0 * math.pi))
        act = (pre * phi).astype(bf16)
        act_ref[:, cols] = act
        total = total + nn(act, wdown[j // 2, (j % 2) * FC : (j % 2 + 1) * FC, :])
    norm_two, scale_two = norm_parts(total)
    gain_two = row(6)
    result_ref[...] = (norm_two * gain_two + row(7)).astype(bf16)
    cot = cot_ref[...].astype(f32)
    put(6, down(cot * norm_two))
    put(7, down(cot))
    grad_two = norm_back(cot * gain_two, norm_two, scale_two)
    put(5, down(grad_two))
    grad_down = grad_two.astype(bf16)
    down_grad_ref[...] = grad_down
    grad_first = grad_two
    for j in range(4):
        cols = slice(j * FC, (j + 1) * FC)
        grad_act = nt(grad_down, wdown[j // 2, (j % 2) * FC : (j % 2 + 1) * FC, :])
        grad_pre = (grad_act * slope[:, cols]).astype(bf16)
        pre_grad_ref[:, cols] = grad_pre
        sums = down(grad_pre.astype(f32))
        for k in range(2):
            i = 8 + 2 * (j % 2) + k
            small_ref[j // 2, i : i + 1, :] = sums[:, k * 384 : (k + 1) * 384]
        grad_first = grad_first + nt(grad_pre, wup[:, :, cols].reshape(D, FC))
    put(3, down(grad_first * norm_one))
    put(4, down(grad_first))
    grad_one = norm_back(grad_first * gain_one, norm_one, scale_one)
    resid_ref[...] = grad_one
    put(2, down(grad_one))
    branch = grad_one.astype(bf16)
    branch_ref[...] = branch
    mixed_grad_ref[...] = nt(branch, wo[...].reshape(D, D)).astype(bf16)
    zero = jnp.zeros((1, D), f32)
    put(0, zero)
    put(1, zero)
    for c in range(2):
        small_ref[c, 12:16, :] = jnp.zeros((4, 384), f32)


def middle(attn, x, cot, vecs, wo, wup, wdown):
    vm = pl.BlockSpec(memory_space=pltpu.VMEM)
    hbm = pl.BlockSpec(memory_space=pltpu.HBM)
    thin, wide = jax.ShapeDtypeStruct((128, D), bf16), jax.ShapeDtypeStruct((128, 3072), bf16)
    return pl.pallas_call(
        middle_kernel,
        out_shape=[
            thin, jax.ShapeDtypeStruct((128, D), f32), thin, thin, thin, wide, wide, thin, thin,
            jax.ShapeDtypeStruct((2, 16, 384), f32),
        ],
        in_specs=[vm] * 4 + [hbm] * 3,
        out_specs=[vm] * 10,
        scratch_shapes=[
            pltpu.VMEM(wo.shape, bf16),
            pltpu.VMEM(wup.shape, bf16),
            pltpu.VMEM(wdown.shape, bf16),
            pltpu.VMEM((128, 3072), f32),
            pltpu.SemaphoreType.DMA((3,)),
        ],
        compiler_params=pltpu.CompilerParams(vmem_limit_bytes=60 * MIB),
    )(attn, x, cot, vecs, wo, wup, wdown)


def back_kernel(
    q_hbm, k_hbm, v_hbm, g_in, attn_ref, lse_ref, rows_ref, bias_ref,
    dq_ref, dk_ref, dv_ref,
    qv, kv, vv, gv, stats, stat_own, q_own, k_own, v_own, g_own, delta, dq_acc, dk_acc, dv_acc,
    send, recv, local,
):
    sends = Sends(send, recv)
    y, z, x = (lax.axis_index(a) for a in CTX)
    meet([away("x", 1), away("x", -1), away("z", 1), away("z", -1), far()])
    loads = []
    for n, (src, dst) in enumerate(
        ((k_hbm, kv), (v_hbm, vv), (q_hbm, qv))
    ):
        copy = pltpu.make_async_copy(src, dst, local.at[n])
        copy.start()
        loads.append(copy)
    eighth = jnp.asarray(0.125, bf16)
    low = lax.broadcasted_iota(jnp.int32, (4, 128), 1) < 64
    stat_own[...] = jnp.zeros_like(stat_own)
    for n in range(3):
        cols = pl.ds(n * 256, 256)
        g = stacked(g_in[:, cols])
        g_own[n] = g
        tall = jnp.concatenate([attn_ref[:, cols]] * 4, axis=0)
        d = jnp.sum(g.astype(f32) * tall, axis=-1, keepdims=True)
        delta[n] = jnp.broadcast_to(d, (512, 128))
        d = as_rows(d)[:4]
        lse = rows_ref[n][:4]
        stat_own[pl.ds(4 * n, 4), :] = jnp.where(low, lse, pltpu.roll(d, 64, 1))
        stat_own[pl.ds(16 + 4 * n, 4), :] = jnp.where(low, pltpu.roll(lse, 64, 1), d)
        dq_acc[n] = jnp.zeros((512, 256), f32)
        dk_acc[n] = jnp.zeros((512, 256), f32)
        dv_acc[n] = jnp.zeros((512, 256), f32)
    ins, outs = [g_in, stat_own], [gv, stats]
    crossing = [sends.start(i, o.at[y, z, x], far()) for i, o in zip(ins, outs)]
    mine = Flow(sends, ins, outs, y, True)
    theirs = Flow(sends, ins, outs, 1 - y, False)
    mine.first()
    own = []
    for n, (i, o) in enumerate(zip(ins, outs)):
        copy = pltpu.make_async_copy(i, o.at[y, z, x], local.at[3 + n])
        copy.start()
        own.append(copy)
    for copy in loads:
        copy.wait()
    for n in range(3):
        cols = pl.ds(n * 256, 256)
        q_own[n] = stacked(qv[y, z, x, :, cols] * eighth)
        k_own[n] = stacked(kv[y, z, x, :, cols] * eighth)
        v_own[n] = stacked(vv[y, z, x, :, cols])

    def queries(lo, hi):
        @pl.loop(lo, hi)
        def _(c):
            n, t = c // 4, c % 4
            cols = pl.ds(pl.multiple_of(n * 256, 256), 256)
            k = kv[t // 2, pl.ds(2 * (t % 2), 2), :, :, cols].reshape(TILE, 256)
            v = vv[t // 2, pl.ds(2 * (t % 2), 2), :, :, cols].reshape(TILE, 256)
            bias = bias_ref[:, pl.ds(pl.multiple_of(t * TILE, TILE), TILE)]
            p = jnp.exp(nt(q_own[n], k) + bias - lse_ref[n][:, :1])
            dp = nt(g_own[n], v)
            ds = (p * (dp - delta[n][:, :1])).astype(bf16)
            dq_acc[n] = dq_acc[n] + nn(ds, k)

    low16 = lax.broadcasted_iota(jnp.int32, (16, 128), 1) < 64

    def keys(unit):
        half, layer, i = unit
        r = 0 if half == "A" else 64
        if half == "A":
            st = stats[layer, i, :, pl.ds(0, 16)]
        else:
            st = stats[layer, :, i, pl.ds(16, 16)]
        turned = [pltpu.roll(st[b], 64, 1) for b in range(4)]
        lse = jnp.concatenate(
            [jnp.where(low16, st[b], turned[b + 1]) for b in (0, 2)], axis=1
        )
        dlt = jnp.concatenate(
            [jnp.where(low16, turned[b], st[b + 1]) for b in (0, 2)], axis=1
        )
        for n in range(3):
            cols = pl.ds(n * 256, 256)
            if half == "A":
                at = (layer, i, slice(None), pl.ds(0, 64), cols)
            else:
                at = (layer, slice(None), i, pl.ds(64, 64), cols)
            q, g = qv[at].reshape(256, 256), gv[at].reshape(256, 256)

            def spread(rows):
                return jnp.concatenate(
                    [jnp.broadcast_to(rows[4 * n + h : 4 * n + h + 1], (128, 256)) for h in range(4)],
                    axis=0,
                )

            p = jnp.exp(nt(k_own[n], q) - spread(lse))
            ds = (p * (nt(v_own[n], g) - spread(dlt))).astype(bf16)
            dv_acc[n] = dv_acc[n] + nn(p.astype(bf16), g)
            dk_acc[n] = dk_acc[n] + nn(ds, q)

    queries(0, 2)
    mine.first_on()
    for copy in crossing:
        copy.wait_recv()
    theirs.first()
    queries(2, 4)
    for copy in own:
        copy.wait()
    mine.second()
    theirs.first_on()
    queries(4, 8)
    for unit in units(y, (0,)):
        keys(unit)
    mine.second_on()
    theirs.second()
    for unit in units(y, (1, -1)):
        keys(unit)
    queries(8, 12)
    mine.wait()
    for unit in units(y, (2,)):
        keys(unit)
    for unit in units(1 - y, (0,)):
        keys(unit)
    theirs.second_on()
    for n in range(3):
        dq_ref[:, pl.ds(n * 256, 256)] = (unstacked(dq_acc[n]) * 0.125).astype(bf16)
    for unit in units(1 - y, (1, -1)):
        keys(unit)
    theirs.wait()
    for unit in units(1 - y, (2,)):
        keys(unit)
    at = pl.multiple_of(((y * 4 + z) * 4 + x) * 128, 128)
    keep = jnp.broadcast_to(bias_ref[:, pl.ds(at, 128)], (128, 128)).T[:, :1] > -1.0
    for n in range(3):
        cols = pl.ds(n * 256, 256)
        dk_ref[:, cols] = jnp.where(keep, unstacked(dk_acc[n]) * 0.125, 0.0).astype(bf16)
        dv_ref[:, cols] = jnp.where(keep, unstacked(dv_acc[n]), 0.0).astype(bf16)
    sends.finish()


def attend_back(q, k, v, g, attn, lse, lse_rows, bias, cid):
    n_send = 33 * 2
    vm = pl.BlockSpec(memory_space=pltpu.VMEM)
    wide = pltpu.VMEM((2, 4, 4, 128, D), bf16)
    tall = pltpu.VMEM((3, 512, 256), bf16)
    sums = pltpu.VMEM((3, 512, 256), f32)
    return pl.pallas_call(
        back_kernel,
        out_shape=[jax.ShapeDtypeStruct((128, D), bf16)] * 3,
        in_specs=[pl.BlockSpec(memory_space=pltpu.HBM)] * 3 + [vm] * 5,
        out_specs=[vm] * 3,
        scratch_shapes=[wide] * 4
        + [pltpu.VMEM((2, 4, 4, 32, 128), f32), pltpu.VMEM((32, 128), f32)]
        + [tall] * 4
        + [pltpu.VMEM((3, 512, 128), f32)]
        + [sums] * 3
        + [
            pltpu.SemaphoreType.DMA((n_send,)),
            pltpu.SemaphoreType.DMA((n_send,)),
            pltpu.SemaphoreType.DMA((5,)),
        ],
        compiler_params=pltpu.CompilerParams(
            collective_id=cid, has_side_effects=True, vmem_limit_bytes=60 * MIB
        ),
    )(q, k, v, g, attn, lse, lse_rows, bias)


def local(
    tokens, lengths, w_query, b_query, w_key, w_value, b_value, w_out, b_out, gain_one, shift_one,
    w_up, b_up, w_down, b_down, gain_two, shift_two, cotangent,
):
    inputs = tokens[0]
    all_q, all_k, all_v, wq, wk, wv, wo, wup, wdown, vecs, q = start(
        inputs,
        [w_query, w_key, w_value, w_out, w_up, w_down],
        [b_query, b_value, b_out, gain_one, shift_one, b_down, gain_two, shift_two, b_up],
        0,
    )
    bias = jnp.where(jnp.arange(4096) < lengths[0], 0.0, -1e30).astype(f32)[None]
    attn, lse, lse_rows = attend(q, all_k.reshape(4096, D), all_v.reshape(4096, D), bias)
    (
        result, grad_resid, grad_mixed, mixed, first, act, grad_pre, grad_down, branch, small
    ) = middle(attn, inputs, cotangent[0], vecs, wo, wup, wdown)
    dq, dk, dv = attend_back(all_q, all_k, all_v, grad_mixed, attn, lse, lse_rows, bias, 1)
    big, small, grad_inputs = reduce_params(
        [
            inputs, mixed, dq, dk, dv, branch, grad_resid, wq, wk, wv,
            first, grad_pre, act, grad_down, small,
        ],
        2,
    )
    tot_wq, tot_wk, tot_wv, tot_wo, tot_wup, tot_wdown, *rest = finish(big, small)
    (
        tot_bq, tot_bv, tot_bo, tot_gone, tot_sone, tot_bdown, tot_gtwo, tot_stwo, tot_bup
    ) = rest
    return (
        result[None],
        grad_inputs[None],
        tot_wq,
        tot_bq,
        tot_wk,
        tot_wv,
        tot_bv,
        tot_wo,
        tot_bo,
        tot_gone,
        tot_sone,
        tot_wup,
        tot_bup,
        tot_wdown.reshape(1536, 768),
        tot_bdown,
        tot_gtwo,
        tot_stwo,
    )


def solution(mesh):
    split = Mesh(
        mesh.devices.reshape(mesh.shape["seq"], 2, 4, 4, mesh.shape["wsh"]),
        ("seq", "ctx_0", "ctx_1", "ctx_2", "wsh"),
    )
    rows = P(("seq", "wsh"), CTX, None)
    mat, vec = P("wsh", None), P("wsh")
    params = (mat, vec, mat, mat, vec, mat, vec, vec, vec, mat, vec, mat, vec, vec, vec)
    return jax.shard_map(
        local,
        mesh=split,
        in_specs=(rows, P(("seq", "wsh")), *params, rows),
        out_specs=(rows, rows, *params),
        check_vma=False,
    )
```
